512 devices in a mesh: cell: 128 (over y, z, core), view: 4 (over x).
Axes of the slice: x: 4, y: 8, z: 8, core: 2. Of those that a mesh axis runs over, the one named last changes fastest.
Arguments:
- params: float32 [59, 262144], P(None, 'cell'), may hold values from -8 to 8, as said below
- cameras: float32 [4, 3], P('view'), may hold values from -0.005 to 0.005
- targets: float32 [4, 256, 3, 256], P('view', 'cell'), may hold values from 0 to 1
- tile_ids: int32 [4, 256], P('view', 'cell'), may hold values from 0 to 255, as said below
- send_slots: int32 [4, 128, 2048], P('view', 'cell'), may hold values from 0 to 2047, as said below
- tile_lists: int32 [4, 256, 512], P('view', 'cell'), may hold values from 0 to 2047, as said below
- tile_len: int32 [4, 256], P('view', 'cell'), may hold values from 0 to 512
Outputs:
- rendered: float32 [4, 256, 3, 256], P('view', 'cell')
- gradient: float32 [59, 262144], P(None, 'cell')
The draws below stay inside these ranges and needn't reach their ends.
Inputs may be any that keep to these rules, and one draw needn't show every extreme that they name: `params`: row 2 (depth) lies in [2, 8]; row 6 in [0.5, 1]; rows 3 to 5 in [-4.5, -2.8]; row 10 in [-8, 3]; rows 0 and 1 place each Gaussian in front of the camera. `tile_ids`: each view's entries name every window tile once. `send_slots`: for one view, source cell and destination, the live slots come first and name distinct Gaussians of that cell; slots past them hold 0 and no tile list refers to them. `tile_lists`: live entries of one list are distinct live slots of the device owning the tile, nearest first; entries past tile_len are 0.
All inputs are finite; a program needn't handle non-finite values.
Results may differ from the reference program's by a relative error of at most 0.0003.
Values sent between devices are 32-bit elements; how exact they have to be, the bound alone decides.
A program may use at most 64 MiB of HBM per device.

```python
import jax
import jax.numpy as jnp
from jax import lax

TILE_SIDE = 16
PIX = 256
TILE_COLS = 32
BLOCK = 256
BLOCKS = 2
G_DEV = 2048
TILES_DEV = 2
TILES = 256
VIEWS = 4
N_CELL = 128
N_VIEW = 4


focal_length = 800.0


def layout(key):
    slot_cap = G_DEV // N_CELL
    depth_len = BLOCKS * BLOCK
    keys = jax.random.split(key, 7)
    dest_weight = jax.random.randint(keys[0], (N_CELL,), 1, 5)
    raw_count = jax.random.randint(keys[1], (N_CELL, N_CELL), 0, slot_cap + 1)
    counts = jnp.minimum(slot_cap, raw_count * dest_weight[None, :] // 2)
    heavy = jax.random.randint(keys[2], (), 0, N_CELL)
    counts = jnp.where(jnp.arange(N_CELL)[None, :] == heavy, slot_cap, counts).astype(jnp.int32)
    orders = jax.vmap(lambda sub_key: jax.random.permutation(sub_key, G_DEV))(jax.random.split(keys[3], N_CELL)).astype(jnp.int32)
    within = jnp.arange(G_DEV) % slot_cap
    block_of = jnp.arange(G_DEV) // slot_cap
    send_live = within[None, :] < counts[:, block_of]
    base_send = jnp.where(send_live, orders, 0).astype(jnp.int32)
    tile_pick = jax.random.randint(keys[4], (N_CELL, G_DEV), 0, TILES_DEV)
    depth_rank = jax.vmap(lambda sub_key: jax.random.permutation(sub_key, G_DEV))(jax.random.split(keys[5], N_CELL)).astype(jnp.int32)
    recv_live = within[None, :] < jnp.transpose(counts)[:, block_of]

    def lists_of(pick_row, live_row, rank_row):

        def one_tile(tile_number):
            member = live_row & (pick_row == tile_number)
            score = jnp.where(member, rank_row, rank_row + G_DEV)
            order = jnp.argsort(score)[:depth_len].astype(jnp.int32)
            filled = jnp.minimum(jnp.sum(member.astype(jnp.int32)), depth_len).astype(jnp.int32)
            return (jnp.where(jnp.arange(depth_len) < filled, order, 0).astype(jnp.int32), filled)
        return jax.vmap(one_tile)(jnp.arange(TILES_DEV))
    lists, lengths = jax.vmap(lists_of)(tile_pick, recv_live, depth_rank)
    base_of = jax.vmap(lambda sub_key: jax.random.permutation(sub_key, N_CELL))(jax.random.split(keys[6], N_VIEW)).astype(jnp.int32)
    return (orders, base_send, tile_pick, depth_rank, lists, lengths, base_of)


def draw_send_slots(key, part):
    orders, base_send, tile_pick, depth_rank, lists, lengths, base_of = layout(key)
    key = jax.random.fold_in(key, 3)
    slot_cap = G_DEV // N_CELL
    columns = (base_of[:, :, None] * slot_cap + jnp.arange(slot_cap)[None, None, :]).reshape(N_VIEW, -1)
    return jax.vmap(lambda column_row: base_send[:, column_row])(columns).astype(jnp.int32)


def draw_tile_lists(key, part):
    orders, base_send, tile_pick, depth_rank, lists, lengths, base_of = layout(key)
    key = jax.random.fold_in(key, 5)
    return lists[base_of].reshape(N_VIEW, N_CELL * TILES_DEV, BLOCKS * BLOCK).astype(jnp.int32)


def draw_tile_len(key, part):
    orders, base_send, tile_pick, depth_rank, lists, lengths, base_of = layout(key)
    key = jax.random.fold_in(key, 7)
    return lengths[base_of].reshape(N_VIEW, N_CELL * TILES_DEV).astype(jnp.int32)


def draw_tile_ids(key, part):
    orders, base_send, tile_pick, depth_rank, lists, lengths, base_of = layout(key)
    key = jax.random.fold_in(key, 9)
    return (base_of[:, :, None] * TILES_DEV + jnp.arange(TILES_DEV)[None, None, :]).reshape(N_VIEW, -1).astype(jnp.int32)


def draw_params(key, part):
    orders, base_send, tile_pick, depth_rank, lists, lengths, base_of = layout(key)
    key = jax.random.fold_in(key, 11)
    slot_cap = G_DEV // N_CELL
    position = jnp.argsort(orders, axis=1)
    home_block = position // slot_cap
    recv_index = jnp.arange(N_CELL)[:, None] * slot_cap + position % slot_cap
    tile_number = (home_block * TILES_DEV + tile_pick[home_block, recv_index]).reshape(-1)
    rank = depth_rank[home_block, recv_index].reshape(-1).astype(jnp.float32)
    total = N_CELL * G_DEV
    keys = jax.random.split(key, 9)
    screen_x = TILE_SIDE * (tile_number % TILE_COLS).astype(jnp.float32) + TILE_SIDE * jax.random.uniform(keys[0], (total,))
    screen_y = TILE_SIDE * (tile_number // TILE_COLS).astype(jnp.float32) + TILE_SIDE * jax.random.uniform(keys[1], (total,))
    depth_cam = 2.0 + 6.0 * (rank + 0.5) / G_DEV
    pos_x = screen_x * depth_cam / focal_length
    pos_y = screen_y * depth_cam / focal_length
    real_part = jax.random.uniform(keys[3], (1, total), minval=0.5, maxval=1.0)
    imag_part = jax.random.uniform(keys[4], (3, total), minval=-1.0, maxval=1.0)
    strong = jax.random.uniform(keys[7], (1, total)) < 1.0 / 64.0
    log_scale = jax.random.uniform(keys[2], (3, total), minval=-4.5, maxval=-2.8)
    faint_logit = jax.random.uniform(keys[5], (1, total), minval=-8.0, maxval=-5.0)
    strong_logit = jax.random.uniform(keys[8], (1, total), minval=-1.0, maxval=2.5)
    harmonics = jnp.clip(0.3 * jax.random.normal(keys[6], (48, total)), -1.2, 1.2)
    opacity_logit = jnp.where(strong, strong_logit, faint_logit)
    rows = jnp.concatenate([pos_x[None], pos_y[None], depth_cam[None], log_scale, real_part, imag_part, opacity_logit, harmonics], axis=0)
    return rows.astype(jnp.float32)


def level_of(rng, extent, cuts, smallest, high):
    level, own = 1.0, jax.random.fold_in(rng, 6)
    for dim, parts in cuts:
        steps = jnp.exp(jax.random.uniform(jax.random.fold_in(own, dim), (parts,), jnp.float32, smallest / len(cuts), high / len(cuts)))
        level = level * jnp.repeat(steps, extent[dim] // parts).reshape([-1 if axis == dim else 1 for axis in range(len(extent))])
    return level


def setup_inputs(seed: int = 0) -> dict:
    arg_keys = jax.random.split(jax.random.key(seed), 8)
    params = draw_params(jax.random.fold_in(arg_keys[7], 71), 0)
    cameras = jnp.clip(jax.random.uniform(arg_keys[1], (VIEWS, 3), jnp.float32, -0.005, 0.005) * level_of(arg_keys[1], (VIEWS, 3), ((0, 4),), -0.4, 0.0), -0.005, 0.005)
    targets = jnp.clip(1.0 * jax.random.uniform(arg_keys[2], (VIEWS, TILES, 3, PIX), jnp.float32) ** level_of(arg_keys[2], (VIEWS, TILES, 3, PIX), ((0, 4), (1, 128)), -0.2, 0.2), 0.0, 1.0)
    tile_ids = draw_tile_ids(jax.random.fold_in(arg_keys[7], 71), 0)
    send_slots = draw_send_slots(jax.random.fold_in(arg_keys[7], 71), 0)
    tile_lists = draw_tile_lists(jax.random.fold_in(arg_keys[7], 71), 0)
    tile_len = draw_tile_len(jax.random.fold_in(arg_keys[7], 71), 0)
    return {"params": params, "cameras": cameras, "targets": targets, "tile_ids": tile_ids, "send_slots": send_slots, "tile_lists": tile_lists, "tile_len": tile_len}


focal_length = 800.0
dilation = 0.3
sh_first = 0.28209479177387814
sh_second = 0.4886025119029199
sh_third = (1.0925484305920792, -1.0925484305920792, 0.31539156525252005, -1.0925484305920792, 0.5462742152960396)
sh_fourth = (-0.5900435899266435, 2.890611442640554, -0.4570457994644658, 0.3731763325901154, -0.4570457994644658, 1.445305721320277, -0.5900435899266435)

def project(raw_rows, camera):
    pos_x = raw_rows[0] - camera[0]
    pos_y = raw_rows[1] - camera[1]
    depth_cam = raw_rows[2] - camera[2]
    inv_depth = 1.0 / depth_cam
    screen_x = focal_length * pos_x * inv_depth
    screen_y = focal_length * pos_y * inv_depth
    scales = jnp.exp(raw_rows[3:6])
    quaternion = raw_rows[6:10]
    quaternion = quaternion / jnp.sqrt(lax.optimization_barrier(jnp.sum(quaternion * quaternion, axis=0)))
    q_w, q_x, q_y, q_z = (quaternion[0], quaternion[1], quaternion[2], quaternion[3])
    rotation = [[1.0 - 2.0 * (q_y * q_y + q_z * q_z), 2.0 * (q_x * q_y - q_w * q_z), 2.0 * (q_x * q_z + q_w * q_y)], [2.0 * (q_x * q_y + q_w * q_z), 1.0 - 2.0 * (q_x * q_x + q_z * q_z), 2.0 * (q_y * q_z - q_w * q_x)], [2.0 * (q_x * q_z - q_w * q_y), 2.0 * (q_y * q_z + q_w * q_x), 1.0 - 2.0 * (q_x * q_x + q_y * q_y)]]
    jac_diag = focal_length * inv_depth
    jac_x = -screen_x * inv_depth
    jac_y = -screen_y * inv_depth
    row_u = [(jac_diag * rotation[0][j] + jac_x * rotation[2][j]) * scales[j] for j in range(3)]
    row_v = [(jac_diag * rotation[1][j] + jac_y * rotation[2][j]) * scales[j] for j in range(3)]
    cov_xx = row_u[0] * row_u[0] + row_u[1] * row_u[1] + row_u[2] * row_u[2] + dilation
    cov_yy = row_v[0] * row_v[0] + row_v[1] * row_v[1] + row_v[2] * row_v[2] + dilation
    cov_xy = row_u[0] * row_v[0] + row_u[1] * row_v[1] + row_u[2] * row_v[2]
    determinant = cov_xx * cov_yy - cov_xy * cov_xy
    conic_a = cov_yy / determinant
    conic_b = -cov_xy / determinant
    conic_c = cov_xx / determinant
    opacity = jax.nn.sigmoid(raw_rows[10])
    distance = jnp.sqrt(pos_x * pos_x + pos_y * pos_y + depth_cam * depth_cam)
    dir_x = pos_x / distance
    dir_y = pos_y / distance
    dir_z = depth_cam / distance
    dir_xx = dir_x * dir_x
    dir_yy = dir_y * dir_y
    dir_zz = dir_z * dir_z
    sh_basis = jnp.stack([sh_first * jnp.ones_like(dir_x), -sh_second * dir_y, sh_second * dir_z, -sh_second * dir_x, sh_third[0] * dir_x * dir_y, sh_third[1] * dir_y * dir_z, sh_third[2] * (2.0 * dir_zz - dir_xx - dir_yy), sh_third[3] * dir_x * dir_z, sh_third[4] * (dir_xx - dir_yy), sh_fourth[0] * dir_y * (3.0 * dir_xx - dir_yy), sh_fourth[1] * dir_x * dir_y * dir_z, sh_fourth[2] * dir_y * (4.0 * dir_zz - dir_xx - dir_yy), sh_fourth[3] * dir_z * (2.0 * dir_zz - 3.0 * dir_xx - 3.0 * dir_yy), sh_fourth[4] * dir_x * (4.0 * dir_zz - dir_xx - dir_yy), sh_fourth[5] * dir_z * (dir_xx - dir_yy), sh_fourth[6] * dir_x * (dir_xx - 3.0 * dir_yy)])
    coeffs = raw_rows[11:59].reshape(3, 16, -1)
    colors = jnp.maximum(lax.optimization_barrier(jnp.sum(coeffs * sh_basis[None], axis=1)) + 0.5, 0.0)
    geometry = jnp.stack([screen_x, screen_y, conic_a, conic_b, conic_c, opacity])
    return jnp.concatenate([geometry, colors], axis=0)

def shade_tile(feature_block, live_mask, pixel_x, pixel_y):
    delta_x = feature_block[0][None, :] - pixel_x[:, None]
    delta_y = feature_block[1][None, :] - pixel_y[:, None]
    exponent = -0.5 * (feature_block[2][None, :] * delta_x * delta_x + feature_block[4][None, :] * delta_y * delta_y) - feature_block[3][None, :] * delta_x * delta_y
    alphas = (feature_block[5] * live_mask)[None, :] * jnp.exp(exponent)
    keep_log = jnp.log1p(-alphas)
    before = jnp.cumsum(keep_log, axis=1) - keep_log
    weights = jnp.exp(before) * alphas
    return jnp.einsum('cl,pl->cp', feature_block[6:9], weights, precision=lax.Precision.HIGHEST)

def pixel_grid(tile_number):
    offsets = jnp.arange(TILE_SIDE * TILE_SIDE, dtype=jnp.int32)
    column = tile_number % TILE_COLS
    row_index = tile_number // TILE_COLS
    pixel_x = (TILE_SIDE * column + offsets % TILE_SIDE).astype(jnp.float32) + 0.5
    pixel_y = (TILE_SIDE * row_index + offsets // TILE_SIDE).astype(jnp.float32) + 0.5
    return (pixel_x, pixel_y)

def reference(params, cameras, targets, tile_ids, send_slots, tile_lists, tile_len):
    slot_cap = G_DEV // N_CELL
    depth_len = BLOCKS * BLOCK
    dest_of = jnp.arange(TILES_DEV * N_CELL, dtype=jnp.int32) // TILES_DEV

    def render_all(raw_rows):
        pictures = []
        for view_index in range(N_VIEW):
            projected = project(raw_rows, cameras[view_index])
            entries = tile_lists[view_index]
            source = entries // slot_cap
            within = entries % slot_cap
            local_index = send_slots[view_index][source, dest_of[:, None] * slot_cap + within]
            global_index = (source * G_DEV + local_index).astype(jnp.int32)

            def one_tile(tile_items):
                tile_number, index_row, length = tile_items
                gathered = jnp.take(projected, index_row, axis=1)
                pixel_x, pixel_y = pixel_grid(tile_number)
                live_mask = (jnp.arange(depth_len, dtype=jnp.int32) < length).astype(jnp.float32)
                return shade_tile(gathered, live_mask, pixel_x, pixel_y)
            pictures.append(lax.map(jax.checkpoint(one_tile), (tile_ids[view_index], global_index, tile_len[view_index])))
        return jnp.stack(pictures)
    rendered, pull_back = jax.vjp(render_all, params)
    gradient = pull_back(rendered - targets)[0]
    return (rendered, gradient)
```

```python
import functools

import jax
import jax.numpy as jnp
from jax import lax
from jax.experimental import pallas as pl
from jax.experimental.pallas import tpu as pltpu
from jax.sharding import PartitionSpec as P

TILE_SIDE = 16
TILE_COLS = 32
LANES = 128
Y_DEVS = 8
ZC_DEVS = 16
VIEW_DEVS = 4
FEATS = 9
F32 = jnp.float32
BF16 = jnp.bfloat16

focal_length = 800.0
dilation = 0.3
sh_first = 0.28209479177387814
sh_second = 0.4886025119029199
sh_third = (
    1.0925484305920792,
    -1.0925484305920792,
    0.31539156525252005,
    -1.0925484305920792,
    0.5462742152960396,
)
sh_fourth = (
    -0.5900435899266435,
    2.890611442640554,
    -0.4570457994644658,
    0.3731763325901154,
    -0.4570457994644658,
    1.445305721320277,
    -0.5900435899266435,
)


def split2(value):
    high = value.astype(BF16)
    return high, (value - high.astype(F32)).astype(BF16)


def split3(value):
    high = value.astype(BF16).astype(F32)
    rest = value - high
    mid = rest.astype(BF16).astype(F32)
    return high, mid, rest - mid


def dot_nt(lhs, rhs):
    return lax.dot_general(lhs, rhs, (((1,), (1,)), ((), ())), preferred_element_type=F32)


def dot_nn(lhs, rhs):
    return lax.dot_general(lhs, rhs, (((1,), (0,)), ((), ())), preferred_element_type=F32)


def rotation_of(q_w, q_x, q_y, q_z):
    return [
        1.0 - 2.0 * (q_y * q_y + q_z * q_z),
        2.0 * (q_x * q_y - q_w * q_z),
        2.0 * (q_x * q_z + q_w * q_y),
        2.0 * (q_x * q_y + q_w * q_z),
        1.0 - 2.0 * (q_x * q_x + q_z * q_z),
        2.0 * (q_y * q_z - q_w * q_x),
        2.0 * (q_x * q_z - q_w * q_y),
        2.0 * (q_y * q_z + q_w * q_x),
        1.0 - 2.0 * (q_x * q_x + q_y * q_y),
    ]


def unit_quaternion(quaternion):
    total = sum(part * part for part in quaternion[1:]) + quaternion[0] * quaternion[0]
    inverse = lax.rsqrt(total)
    return [part * inverse for part in quaternion], inverse


def shape_matrix(log_scales, quaternion):
    scales = [jnp.exp(part) for part in log_scales]
    unit, inverse = unit_quaternion(quaternion)
    rotation = rotation_of(*unit)
    matrix = [rotation[3 * i + j] * scales[j] for i in range(3) for j in range(3)]
    return matrix, scales, unit, inverse


def harmonics(x, y, z):
    xx, yy, zz = x * x, y * y, z * z
    rim = 4.0 * zz - xx - yy
    gap = xx - yy
    return [
        -sh_second * y,
        sh_second * z,
        -sh_second * x,
        sh_third[0] * (x * y),
        sh_third[1] * (y * z),
        sh_third[2] * (2.0 * zz - xx - yy),
        sh_third[3] * (x * z),
        sh_third[4] * gap,
        sh_fourth[0] * (y * (3.0 * xx - yy)),
        sh_fourth[1] * (x * y * z),
        sh_fourth[2] * (y * rim),
        sh_fourth[3] * (z * (2.0 * zz - 3.0 * xx - 3.0 * yy)),
        sh_fourth[4] * (x * rim),
        sh_fourth[5] * (z * gap),
        sh_fourth[6] * (x * (xx - 3.0 * yy)),
    ]


def geometry(pos, matrix):
    x, y, z = pos
    inv_z = 1.0 / z
    jac = focal_length * inv_z
    screen_x = x * jac
    screen_y = y * jac
    jac_x = -screen_x * inv_z
    jac_y = -screen_y * inv_z
    row_u = [jac * matrix[j] + jac_x * matrix[6 + j] for j in range(3)]
    row_v = [jac * matrix[3 + j] + jac_y * matrix[6 + j] for j in range(3)]
    cov_a = row_u[0] * row_u[0] + row_u[1] * row_u[1] + row_u[2] * row_u[2] + dilation
    cov_c = row_v[0] * row_v[0] + row_v[1] * row_v[1] + row_v[2] * row_v[2] + dilation
    cov_b = row_u[0] * row_v[0] + row_u[1] * row_v[1] + row_u[2] * row_v[2]
    inv_det = 1.0 / (cov_a * cov_c - cov_b * cov_b)
    return inv_z, jac, screen_x, screen_y, jac_x, jac_y, row_u, row_v, cov_a, cov_b, cov_c, inv_det


def direction(pos):
    x, y, z = pos
    inverse = lax.rsqrt(x * x + y * y + z * z)
    return [x * inverse, y * inverse, z * inverse], inverse


def raw_colour(load, channel, basis):
    total = load(11 + 16 * channel) * sh_first
    for j in range(15):
        total = total + load(12 + 16 * channel + j) * basis[j]
    return total + 0.5


def lane_gather(source, index):
    return jnp.take_along_axis(source, index, axis=1, mode="promise_in_bounds")


def gather_chunk(table, high, low):
    shape = (8, LANES)
    low = jnp.broadcast_to(low, shape)
    high = jnp.broadcast_to(high, shape)
    top = bottom = jnp.zeros(shape, F32)
    for chunk in range(16):
        here = high == chunk
        top = jnp.where(here, lane_gather(table[pl.ds(16 * chunk, 8), :], low), top)
        bottom = jnp.where(here, lane_gather(table[pl.ds(16 * chunk + 8, 8), :], low), bottom)
    return top, bottom


def project_kernel(camera, params, slots, dense, outgoing, packed, table):
    rows = params.shape[0]
    for group in range(0, rows, 8):
        size = min(8, rows - group)
        for chunk in range(16):
            packed[pl.ds(group * 16 + chunk * 8, size), :] = params[
                pl.ds(group, size), pl.ds(chunk * LANES, LANES)
            ]
    for row in range(rows):
        dense[row] = packed[pl.ds((row // 8) * 128 + row % 8, 16, stride=8), :]
    table[...] = jnp.zeros_like(table)

    load = lambda row: dense[row]
    pos = [load(i) - camera[0, i] for i in range(3)]
    matrix, _, _, _ = shape_matrix([load(3 + i) for i in range(3)], [load(6 + i) for i in range(4)])
    _, _, screen_x, screen_y, _, _, _, _, cov_a, cov_b, cov_c, inv_det = geometry(pos, matrix)
    unit, _ = direction(pos)
    basis = harmonics(*unit)
    features = [
        screen_x,
        screen_y,
        cov_c * inv_det,
        -cov_b * inv_det,
        cov_a * inv_det,
        1.0 / (1.0 + jnp.exp(-load(10))),
    ]
    features += [jnp.maximum(raw_colour(load, channel, basis), 0.0) for channel in range(3)]
    for i, feature in enumerate(features):
        table[pl.ds(i, 16, stride=16), :] = feature

    def one_chunk(chunk, carry):
        index = slots[0, :, pl.ds(pl.multiple_of(chunk * LANES, LANES), LANES)]
        top, bottom = gather_chunk(table, index >> 7, index & 127)
        outgoing[chunk, pl.ds(0, 8), :] = top
        outgoing[chunk, pl.ds(8, 1), :] = bottom[0:1]
        return carry

    lax.fori_loop(0, 16, one_chunk, 0, unroll=2)


def project_call(camera, params, slots):
    rows = params.shape[0]
    return pl.pallas_call(
        project_kernel,
        out_shape=(
            jax.ShapeDtypeStruct((rows, 16, LANES), F32),
            jax.ShapeDtypeStruct((16, FEATS, LANES), F32),
        ),
        in_specs=[
            pl.BlockSpec(memory_space=pltpu.SMEM),
            pl.BlockSpec(memory_space=pltpu.VMEM),
            pl.BlockSpec(memory_space=pltpu.VMEM),
        ],
        out_specs=(pl.BlockSpec(memory_space=pltpu.VMEM),) * 2,
        scratch_shapes=[pltpu.VMEM((64 * 16, LANES), F32), pltpu.VMEM((256, LANES), F32)],
        compiler_params=pltpu.CompilerParams(vmem_limit_bytes=24 * 2**20),
        name="project",
    )(camera, params, slots)


def block_transpose(rows):
    group = lax.broadcasted_iota(jnp.int32, rows[0].shape, 1) // 16
    for step in (1, 2, 4):
        odd = (group & step) != 0
        fresh = list(rows)
        for i in range(8):
            if i & step:
                continue
            first, second = rows[i], rows[i + step]
            fresh[i] = jnp.where(odd, pltpu.roll(second, 16 * step, 1), first)
            fresh[i + step] = jnp.where(odd, second, pltpu.roll(first, LANES - 16 * step, 1))
        rows = fresh
    return rows


def greet(my_y, my_zc):
    barrier = pltpu.get_barrier_semaphore()
    for k in range(1, Y_DEVS):
        pl.semaphore_signal(
            barrier,
            inc=1,
            device_id={"cell": lax.rem(my_y + k, Y_DEVS) * ZC_DEVS + my_zc},
            device_id_type=pl.DeviceIdType.MESH,
        )
    for k in range(1, ZC_DEVS):
        pl.semaphore_signal(
            barrier,
            inc=1,
            device_id={"cell": my_y * ZC_DEVS + lax.rem(my_zc + k, ZC_DEVS)},
            device_id_type=pl.DeviceIdType.MESH,
        )
    return barrier


def forward_kernel(outgoing, received, landed, staged, send_y, recv_y, send_zc, recv_zc):
    cell = lax.axis_index("cell")
    my_y, my_zc = cell // ZC_DEVS, lax.rem(cell, ZC_DEVS)
    barrier = greet(my_y, my_zc)
    pl.semaphore_wait(barrier, Y_DEVS + ZC_DEVS - 2)
    copies = []
    for k in range(1, Y_DEVS):
        peer = lax.rem(my_y + k, Y_DEVS)
        copy = pltpu.make_async_remote_copy(
            src_ref=outgoing.at[pl.ds(2 * peer, 2)],
            dst_ref=landed.at[my_y],
            send_sem=send_y.at[k - 1],
            recv_sem=recv_y.at[k - 1],
            device_id={"cell": peer * ZC_DEVS + my_zc},
            device_id_type=pl.DeviceIdType.MESH,
        )
        copy.start()
        copies.append(copy)
    landed[my_y] = outgoing[pl.ds(2 * my_y, 2)]
    for copy in copies:
        copy.wait()
    for half in range(2):
        rows = block_transpose([landed[y, half] for y in range(Y_DEVS)])
        for i in range(8):
            staged[8 * half + i] = rows[i]
    copies = []
    for k in range(1, ZC_DEVS):
        peer = lax.rem(my_zc + k, ZC_DEVS)
        copy = pltpu.make_async_remote_copy(
            src_ref=staged.at[peer],
            dst_ref=received.at[my_zc],
            send_sem=send_zc.at[k - 1],
            recv_sem=recv_zc.at[k - 1],
            device_id={"cell": my_y * ZC_DEVS + peer},
            device_id_type=pl.DeviceIdType.MESH,
        )
        copy.start()
        copies.append(copy)
    received[my_zc] = staged[my_zc]
    for copy in copies:
        copy.wait()


def backward_kernel(slot_grads, returned, landed, staged, send_y, recv_y, send_zc, recv_zc):
    cell = lax.axis_index("cell")
    my_y, my_zc = cell // ZC_DEVS, lax.rem(cell, ZC_DEVS)
    barrier = greet(my_y, my_zc)
    pl.semaphore_wait(barrier, Y_DEVS + ZC_DEVS - 2)
    copies = []
    for k in range(1, ZC_DEVS):
        peer = lax.rem(my_zc + k, ZC_DEVS)
        copy = pltpu.make_async_remote_copy(
            src_ref=slot_grads.at[peer],
            dst_ref=landed.at[my_zc],
            send_sem=send_zc.at[k - 1],
            recv_sem=recv_zc.at[k - 1],
            device_id={"cell": my_y * ZC_DEVS + peer},
            device_id_type=pl.DeviceIdType.MESH,
        )
        copy.start()
        copies.append(copy)
    landed[my_zc] = slot_grads[my_zc]
    for copy in copies:
        copy.wait()
    for half in range(2):
        rows = block_transpose([landed[8 * half + i] for i in range(8)])
        for y in range(Y_DEVS):
            staged[y, half] = rows[y]
    copies = []
    for k in range(1, Y_DEVS):
        peer = lax.rem(my_y + k, Y_DEVS)
        copy = pltpu.make_async_remote_copy(
            src_ref=staged.at[peer],
            dst_ref=returned.at[pl.ds(2 * my_y, 2)],
            send_sem=send_y.at[k - 1],
            recv_sem=recv_y.at[k - 1],
            device_id={"cell": peer * ZC_DEVS + my_zc},
            device_id_type=pl.DeviceIdType.MESH,
        )
        copy.start()
        copies.append(copy)
    returned[pl.ds(2 * my_y, 2)] = staged[my_y]
    for copy in copies:
        copy.wait()


def exchange_call(kernel, collective_id, operand, name):
    by_y = pltpu.VMEM((Y_DEVS, 2, FEATS, LANES), F32)
    by_zc = pltpu.VMEM((ZC_DEVS, FEATS, LANES), F32)
    buffers = [by_y, by_zc] if kernel is forward_kernel else [by_zc, by_y]
    return pl.pallas_call(
        kernel,
        out_shape=jax.ShapeDtypeStruct((16, FEATS, LANES), F32),
        in_specs=[pl.BlockSpec(memory_space=pltpu.VMEM)],
        out_specs=pl.BlockSpec(memory_space=pltpu.VMEM),
        scratch_shapes=buffers
        + [
            pltpu.SemaphoreType.DMA((Y_DEVS - 1,)),
            pltpu.SemaphoreType.DMA((Y_DEVS - 1,)),
            pltpu.SemaphoreType.DMA((ZC_DEVS - 1,)),
            pltpu.SemaphoreType.DMA((ZC_DEVS - 1,)),
        ],
        compiler_params=pltpu.CompilerParams(
            collective_id=collective_id, has_side_effects=True, vmem_limit_bytes=16 * 2**20
        ),
        name=name,
    )(operand)


def scatter_operands(values, high, low, left, right, column):
    columns = pl.ds(pl.multiple_of(column, LANES), LANES)
    shape = (16, LANES)
    here = jnp.broadcast_to(high, shape) == lax.broadcasted_iota(jnp.int32, shape, 0)
    for piece, rows in enumerate(split3(values)):
        for f in range(FEATS):
            spread = jnp.where(here, jnp.broadcast_to(rows[f : f + 1], shape), 0.0)
            left[pl.ds((piece * FEATS + f) * 16, 16), columns] = spread.astype(BF16)
    shape = (LANES, LANES)
    hot = jnp.broadcast_to(low, shape) == lax.broadcasted_iota(jnp.int32, shape, 0)
    right[:, columns] = jnp.where(hot, 1.0, 0.0).astype(BF16)


def scatter_product(left, right):
    size = FEATS * 16
    total = dot_nt(left[...], right[...])
    return total[0:size] + total[size : 2 * size] + total[2 * size : 3 * size]


def tile_kernel(
    tile_ids, tile_len, received, lists, targets, pictures, slot_grads,
    table, feats, alpha, before, weight, weight_hi, weight_lo, part_hi, part_lo, upper, grads, left, right, spread,
):
    tiles, entries = lists.shape[1], lists.shape[2]
    chunks = entries // LANES
    pixels = TILE_SIDE * TILE_SIDE
    half = entries // 2
    table[...] = jnp.zeros_like(table)
    for chunk in range(16):
        table[pl.ds(16 * chunk, FEATS), :] = received[chunk]
    row = lax.broadcasted_iota(jnp.int32, (entries, entries), 0)
    col = lax.broadcasted_iota(jnp.int32, (entries, entries), 1)
    upper[...] = jnp.where(row < col, 1.0, 0.0).astype(BF16)
    grads[...] = jnp.zeros_like(grads)

    def slot_of(tile, chunk):
        index = lists[0, pl.ds(tile, 1), pl.ds(chunk * LANES, LANES)]
        return (index >> 4) & 15, ((index >> 8) << 4) | (index & 15)

    for tile in range(tiles):
        for chunk in range(chunks):
            high, low = slot_of(tile, chunk)
            top, bottom = gather_chunk(table, high, low)
            feats[pl.ds(0, 8), pl.ds(chunk * LANES, LANES)] = top
            feats[pl.ds(8, 8), pl.ds(chunk * LANES, LANES)] = bottom
        number = tile_ids[0, tile]
        length = tile_len[0, tile]
        left_x = (TILE_SIDE * lax.rem(number, TILE_COLS)).astype(F32) + 0.5
        top_y = (TILE_SIDE * (number // TILE_COLS)).astype(F32) + 0.5
        shape = (TILE_SIDE, LANES)
        pixel_x = lax.broadcasted_iota(jnp.int32, shape, 0).astype(F32) + left_x

        def feature(f, chunk):
            return jnp.broadcast_to(feats[pl.ds(f, 1), pl.ds(chunk * LANES, LANES)], (8, LANES))

        def twice(rows):
            return jnp.concatenate([rows, rows], axis=0)

        for chunk in range(chunks):
            lanes = pl.ds(chunk * LANES, LANES)
            lane = lax.broadcasted_iota(jnp.int32, (8, LANES), 1) + chunk * LANES
            opacity = twice(jnp.where(lane < length, feature(5, chunk), 0.0))
            delta_x = twice(feature(0, chunk)) - pixel_x
            part_x = twice(-0.5 * feature(2, chunk)) * delta_x * delta_x
            cross = twice(-feature(3, chunk)) * delta_x
            screen_y = feature(1, chunk)
            conic_c = -0.5 * feature(4, chunk)

            def one_row(y, carry):
                rows = pl.ds(pl.multiple_of(y * TILE_SIDE, TILE_SIDE), TILE_SIDE)
                delta_y = screen_y - (top_y + y.astype(F32))
                part_y = conic_c * delta_y * delta_y
                value = opacity * jnp.exp(part_x + cross * twice(delta_y) + twice(part_y))
                alpha[rows, lanes] = value
                part_hi[rows, lanes], part_lo[rows, lanes] = split2(jnp.log(1.0 - value))
                return carry

            lax.fori_loop(0, TILE_SIDE, one_row, 0, unroll=4)

        def prefix(part):
            first = dot_nn(part[:, pl.ds(0, half)], upper[pl.ds(0, half), :])
            second = dot_nn(part[:, pl.ds(half, half)], upper[pl.ds(half, half), pl.ds(half, half)])
            return first[:, :half], first[:, half:] + second

        high_left, high_right = prefix(part_hi)
        low_left, low_right = prefix(part_lo)
        before[:, pl.ds(0, half)] = high_left + low_left
        before[:, pl.ds(half, half)] = high_right + low_right

        def one_weight(y, carry):
            rows = pl.ds(pl.multiple_of(y * TILE_SIDE, TILE_SIDE), TILE_SIDE)
            value = jnp.exp(before[rows, :]) * alpha[rows, :]
            weight[rows, :] = value
            weight_hi[rows, :], weight_lo[rows, :] = split2(value)
            return carry

        lax.fori_loop(0, TILE_SIDE, one_weight, 0, unroll=2)

        colours = jnp.concatenate([feats[pl.ds(6, 3), :], jnp.zeros((5, entries), F32)], axis=0)
        colour_hi = colours.astype(BF16).astype(F32)
        colour_lo = (colours - colour_hi).astype(BF16).astype(F32)
        both = jnp.concatenate([colour_hi, colour_lo], axis=0).astype(BF16)
        product = dot_nt(both, weight_hi[...])
        picture = product[0:8] + product[8:16] + dot_nt(both, weight_lo[...])[0:8]
        pictures[0, tile] = picture[0:3]
        residual = picture - jnp.concatenate([targets[0, tile], jnp.zeros((5, pixels), F32)], axis=0)
        residual_hi = residual.astype(BF16).astype(F32)
        residual_lo = (residual - residual_hi).astype(BF16).astype(F32)

        pair = jnp.concatenate([residual_hi, residual_lo], axis=0).astype(BF16)
        product = dot_nn(pair, weight_hi[...])
        colour_grad = product[0:8] + product[8:16] + dot_nn(pair, weight_lo[...])[0:8]

        stack = jnp.concatenate(
            [residual_hi, residual_lo, residual_hi, jnp.zeros((104, pixels), F32)], axis=0
        )
        columns = jnp.transpose(stack).astype(BF16)
        rows24 = jnp.concatenate(
            [colour_hi, colour_hi, colour_lo, jnp.zeros((104, entries), F32)], axis=0
        ).astype(BF16)
        before[...] = dot_nn(columns, rows24)

        def one_share(y, carry):
            rows = pl.ds(pl.multiple_of(y * TILE_SIDE, TILE_SIDE), TILE_SIDE)
            value = before[rows, :] * weight[rows, :]
            weight[rows, :] = value
            part_hi[rows, :], part_lo[rows, :] = split2(value)
            return carry

        lax.fori_loop(0, TILE_SIDE, one_share, 0, unroll=2)

        def suffix(part):
            first = dot_nt(part[:, pl.ds(0, half)], upper[pl.ds(0, half), pl.ds(0, half)])
            second = dot_nt(part[:, pl.ds(half, half)], upper[:, pl.ds(half, half)])
            return first + second[:, :half], second[:, half:]

        high_left, high_right = suffix(part_hi)
        low_left, low_right = suffix(part_lo)
        before[:, pl.ds(0, half)] = high_left + low_left
        before[:, pl.ds(half, half)] = high_right + low_right

        for chunk in range(chunks):
            lanes = pl.ds(chunk * LANES, LANES)
            screen_y = feature(1, chunk)

            def one_row(y, carry):
                rows = pl.ds(pl.multiple_of(y * TILE_SIDE, TILE_SIDE), TILE_SIDE)
                sum_0, sum_1, sum_2 = carry
                delta_y = twice(screen_y - (top_y + y.astype(F32)))
                value = alpha[rows, lanes]
                grad = weight[rows, lanes] - before[rows, lanes] * (value / (1.0 - value))
                slope = grad * delta_y
                return sum_0 + grad, sum_1 + slope, sum_2 + slope * delta_y

            zero = jnp.zeros(shape, F32)
            sum_0, sum_1, sum_2 = lax.fori_loop(0, TILE_SIDE, one_row, (zero, zero, zero), unroll=4)
            delta_x = twice(feature(0, chunk)) - pixel_x
            over = lambda rows: jnp.sum(rows, axis=0, keepdims=True)
            first_x = over(delta_x * sum_0)
            first_y = over(sum_1)
            row_of = lambda f: feats[pl.ds(f, 1), lanes]
            out = pl.ds(tile * entries + chunk * LANES, LANES)
            grads[pl.ds(0, 1), out] = -row_of(2) * first_x - row_of(3) * first_y
            grads[pl.ds(1, 1), out] = -row_of(4) * first_y - row_of(3) * first_x
            grads[pl.ds(2, 1), out] = -0.5 * over(delta_x * delta_x * sum_0)
            grads[pl.ds(3, 1), out] = -over(delta_x * sum_1)
            grads[pl.ds(4, 1), out] = -0.5 * over(sum_2)
            grads[pl.ds(5, 1), out] = over(sum_0)
        grads[pl.ds(6, 3), pl.ds(tile * entries, entries)] = colour_grad[0:3]

        for chunk in range(chunks):
            high, low = slot_of(tile, chunk)
            column = tile * entries + chunk * LANES
            scatter_operands(grads[:, pl.ds(column, LANES)], high, low, left, right, column)

    total = scatter_product(left, right)
    for f in range(FEATS):
        spread[pl.ds(f, 16, stride=16), :] = total[16 * f : 16 * f + 16]
    for chunk in range(16):
        slot_grads[chunk] = spread[pl.ds(16 * chunk, FEATS), :]


def tile_call(tile_ids, tile_len, received, lists, targets):
    tiles, entries = lists.shape[1], lists.shape[2]
    pixels = TILE_SIDE * TILE_SIDE
    smem = pl.BlockSpec(memory_space=pltpu.SMEM)
    vmem = pl.BlockSpec(memory_space=pltpu.VMEM)
    plane = pltpu.VMEM((pixels, entries), F32)
    thin = pltpu.VMEM((pixels, entries), BF16)
    return pl.pallas_call(
        tile_kernel,
        out_shape=(
            jax.ShapeDtypeStruct(targets.shape, F32),
            jax.ShapeDtypeStruct((16, FEATS, LANES), F32),
        ),
        in_specs=[smem, smem, vmem, vmem, vmem],
        out_specs=(vmem, vmem),
        scratch_shapes=[
            pltpu.VMEM((256, LANES), F32),
            pltpu.VMEM((16, entries), F32),
            plane,
            plane,
            plane,
            thin,
            thin,
            thin,
            thin,
            pltpu.VMEM((entries, entries), BF16),
            pltpu.VMEM((16, tiles * entries), F32),
            pltpu.VMEM((3 * FEATS * 16, tiles * entries), BF16),
            pltpu.VMEM((LANES, tiles * entries), BF16),
            pltpu.VMEM((256, LANES), F32),
        ],
        compiler_params=pltpu.CompilerParams(vmem_limit_bytes=32 * 2**20),
        name="tiles",
    )(tile_ids, tile_len, received, lists, targets)


VIEW_ROWS = FEATS * 16 + 8


def gauss_kernel(camera, returned, slots, out, left, right):
    def one_chunk(chunk, carry):
        column = pl.multiple_of(chunk * LANES, LANES)
        index = slots[0, :, pl.ds(column, LANES)]
        scatter_operands(returned[chunk], index >> 7, index & 127, left, right, column)
        return carry

    lax.fori_loop(0, 16, one_chunk, 0)
    out[pl.ds(0, FEATS * 16), :] = scatter_product(left, right)
    row = lax.broadcasted_iota(jnp.int32, (8, LANES), 0)
    shift = jnp.where(row == 0, camera[0, 0], jnp.where(row == 1, camera[0, 1], camera[0, 2]))
    out[pl.ds(FEATS * 16, 8), :] = shift


def gauss_call(camera, returned, slots):
    vmem = pl.BlockSpec(memory_space=pltpu.VMEM)
    return pl.pallas_call(
        gauss_kernel,
        out_shape=jax.ShapeDtypeStruct((VIEW_ROWS, LANES), F32),
        in_specs=[pl.BlockSpec(memory_space=pltpu.SMEM), vmem, vmem],
        out_specs=vmem,
        scratch_shapes=[
            pltpu.VMEM((3 * FEATS * 16, 2048), BF16),
            pltpu.VMEM((LANES, 2048), BF16),
        ],
        compiler_params=pltpu.CompilerParams(vmem_limit_bytes=24 * 2**20),
        name="gauss",
    )(camera, returned, slots)


def views_kernel(mine, every, send_sem, recv_sem):
    view = lax.axis_index("view")
    barrier = pltpu.get_barrier_semaphore()
    for k in range(1, VIEW_DEVS):
        pl.semaphore_signal(
            barrier,
            inc=1,
            device_id={"view": lax.rem(view + k, VIEW_DEVS)},
            device_id_type=pl.DeviceIdType.MESH,
        )
    pl.semaphore_wait(barrier, VIEW_DEVS - 1)
    copies = []
    for k in range(1, VIEW_DEVS):
        copy = pltpu.make_async_remote_copy(
            src_ref=mine,
            dst_ref=every.at[view],
            send_sem=send_sem.at[k - 1],
            recv_sem=recv_sem.at[k - 1],
            device_id={"view": lax.rem(view + k, VIEW_DEVS)},
            device_id_type=pl.DeviceIdType.MESH,
        )
        copy.start()
        copies.append(copy)
    every[view] = mine[...]
    for copy in copies:
        copy.wait()


def views_call(mine):
    vmem = pl.BlockSpec(memory_space=pltpu.VMEM)
    return pl.pallas_call(
        views_kernel,
        out_shape=jax.ShapeDtypeStruct((VIEW_DEVS, VIEW_ROWS, LANES), F32),
        in_specs=[vmem],
        out_specs=vmem,
        scratch_shapes=[
            pltpu.SemaphoreType.DMA((VIEW_DEVS - 1,)),
            pltpu.SemaphoreType.DMA((VIEW_DEVS - 1,)),
        ],
        compiler_params=pltpu.CompilerParams(
            collective_id=2, has_side_effects=True, vmem_limit_bytes=16 * 2**20
        ),
        name="views",
    )(mine)


def param_kernel(dense, every, gradient, packed):
    rows = gradient.shape[0]

    def one_half(half, carry):
        part = pl.ds(pl.multiple_of(half * 8, 8), 8)
        load = lambda row: dense[row, part, :]

        def store(row, value):
            packed[pl.ds((row // 8) * 128 + row % 8 + half * 64, 8, stride=8), :] = value

        def add(row, value, view):
            if view:
                where = pl.ds((row // 8) * 128 + row % 8 + half * 64, 8, stride=8)
                packed[where, :] = packed[where, :] + value
            else:
                store(row, value)

        quaternion = [load(6 + i) for i in range(4)]
        matrix, scales, unit_q, inv_norm = shape_matrix([load(3 + i) for i in range(3)], quaternion)
        grad_matrix = [0.0] * 9
        grad_pos = [0.0] * 3
        grad_log = 0.0
        for view in range(VIEW_DEVS):
            slot = lambda f: every[view, pl.ds(pl.multiple_of(f * 16 + half * 8, 8), 8), :]
            shift = lambda i: jnp.broadcast_to(every[view, pl.ds(FEATS * 16 + i, 1), :], (8, LANES))
            pos = [load(i) - shift(i) for i in range(3)]
            inv_z, jac, screen_x, screen_y, jac_x, jac_y, row_u, row_v, cov_a, cov_b, cov_c, inv_det = geometry(
                pos, matrix
            )
            g_a, g_b, g_c = slot(2), slot(3), slot(4)
            g_det = -(g_a * cov_c - g_b * cov_b + g_c * cov_a) * inv_det * inv_det
            d_a = g_c * inv_det + g_det * cov_c
            d_c = g_a * inv_det + g_det * cov_a
            d_b = -g_b * inv_det - 2.0 * g_det * cov_b
            d_a, d_c = 2.0 * d_a, 2.0 * d_c
            g_u = [d_a * row_u[j] + d_b * row_v[j] for j in range(3)]
            g_v = [d_c * row_v[j] + d_b * row_u[j] for j in range(3)]
            for j in range(3):
                grad_matrix[j] = grad_matrix[j] + jac * g_u[j]
                grad_matrix[3 + j] = grad_matrix[3 + j] + jac * g_v[j]
                grad_matrix[6 + j] = grad_matrix[6 + j] + jac_x * g_u[j] + jac_y * g_v[j]
            g_jac = sum(g_u[j] * matrix[j] + g_v[j] * matrix[3 + j] for j in range(3))
            g_jac_x = sum(g_u[j] * matrix[6 + j] for j in range(3))
            g_jac_y = sum(g_v[j] * matrix[6 + j] for j in range(3))
            g_sx = slot(0) - inv_z * g_jac_x
            g_sy = slot(1) - inv_z * g_jac_y
            g_inv = (
                focal_length * (g_jac + pos[0] * g_sx + pos[1] * g_sy) - screen_x * g_jac_x - screen_y * g_jac_y
            )
            g_pos = [jac * g_sx, jac * g_sy, -inv_z * inv_z * g_inv]

            unit, inv_len = direction(pos)
            basis, pull = jax.vjp(harmonics, *unit)
            g_basis = [0.0] * 15
            for channel in range(3):
                colour = raw_colour(load, channel, basis)
                g_colour = slot(6 + channel)
                g_colour = jnp.where(colour > 0.0, g_colour, jnp.where(colour < 0.0, 0.0, 0.5 * g_colour))
                add(11 + 16 * channel, sh_first * g_colour, view)
                for j in range(15):
                    add(12 + 16 * channel + j, basis[j] * g_colour, view)
                    g_basis[j] = g_basis[j] + load(12 + 16 * channel + j) * g_colour
            g_unit = pull(g_basis)
            along = unit[0] * g_unit[0] + unit[1] * g_unit[1] + unit[2] * g_unit[2]
            for i in range(3):
                grad_pos[i] = grad_pos[i] + g_pos[i] + inv_len * (g_unit[i] - unit[i] * along)
            grad_log = grad_log + slot(5)

        for i in range(3):
            store(i, grad_pos[i])
            store(3 + i, sum(grad_matrix[3 * k + i] * matrix[3 * k + i] for k in range(3)))
        rotation, pull = jax.vjp(rotation_of, *unit_q)
        g_unit = pull([grad_matrix[3 * i + j] * scales[j] for i in range(3) for j in range(3)])
        along = sum(unit_q[i] * g_unit[i] for i in range(4))
        for i in range(4):
            store(6 + i, inv_norm * (g_unit[i] - unit_q[i] * along))
        store(10, grad_log * (1.0 / (1.0 + jnp.exp(load(10)))))
        return carry

    lax.fori_loop(0, 2, one_half, 0)
    for group in range(0, rows, 8):
        size = min(8, rows - group)
        for chunk in range(16):
            gradient[pl.ds(group, size), pl.ds(chunk * LANES, LANES)] = packed[
                pl.ds(group * 16 + chunk * 8, size), :
            ]


def param_call(dense, every):
    vmem = pl.BlockSpec(memory_space=pltpu.VMEM)
    return pl.pallas_call(
        param_kernel,
        out_shape=jax.ShapeDtypeStruct((dense.shape[0], 2048), F32),
        in_specs=[vmem, vmem],
        out_specs=vmem,
        scratch_shapes=[pltpu.VMEM((64 * 16, LANES), F32)],
        compiler_params=pltpu.CompilerParams(vmem_limit_bytes=24 * 2**20),
        name="params",
    )(dense, every)


def local(params, cameras, targets, tile_ids, send_slots, tile_lists, tile_len):
    dense, outgoing = project_call(cameras, params, send_slots)
    received = exchange_call(forward_kernel, 0, outgoing, "forward")
    pictures, slot_grads = tile_call(tile_ids, tile_len, received, tile_lists, targets)
    returned = exchange_call(backward_kernel, 1, slot_grads, "backward")
    mine = gauss_call(cameras, returned, send_slots)
    every = views_call(mine)
    return pictures, param_call(dense, every)


def solution(mesh):
    return jax.shard_map(
        local,
        mesh=mesh,
        in_specs=(
            P(None, "cell"),
            P("view", None),
            P("view", "cell", None, None),
            P("view", "cell"),
            P("view", "cell", None),
            P("view", "cell", None),
            P("view", "cell"),
        ),
        out_specs=(P("view", "cell", None, None), P(None, "cell")),
        check_vma=False,
    )
```

```python
import functools

import jax
import jax.numpy as jnp
from jax import lax
from jax.experimental import pallas as pl
from jax.experimental.pallas import tpu as pltpu
from jax.sharding import PartitionSpec as P

TILE_SIDE = 16
TILE_COLS = 32
LANES = 128
Y_DEVS = 8
ZC_DEVS = 16
VIEW_DEVS = 4
FEATS = 9
Y_ORDER = (4, 3, 5, 2, 6, 1, 7)
ZC_ORDER = (8, 9, 7, 6, 10, 5, 11, 4, 12, 3, 13, 2, 14, 1, 15)
VIEW_ORDER = (2, 1, 3)
F32 = jnp.float32
BF16 = jnp.bfloat16

focal_length = 800.0
dilation = 0.3
sh_first = 0.28209479177387814
sh_second = 0.4886025119029199
sh_third = (
    1.0925484305920792,
    -1.0925484305920792,
    0.31539156525252005,
    -1.0925484305920792,
    0.5462742152960396,
)
sh_fourth = (
    -0.5900435899266435,
    2.890611442640554,
    -0.4570457994644658,
    0.3731763325901154,
    -0.4570457994644658,
    1.445305721320277,
    -0.5900435899266435,
)


def split2(value):
    high = value.astype(BF16)
    return high, (value - high.astype(F32)).astype(BF16)


def split3(value):
    high = value.astype(BF16).astype(F32)
    rest = value - high
    mid = rest.astype(BF16).astype(F32)
    return high, mid, rest - mid


def dot_nt(lhs, rhs):
    return lax.dot_general(lhs, rhs, (((1,), (1,)), ((), ())), preferred_element_type=F32)


def dot_nn(lhs, rhs):
    return lax.dot_general(lhs, rhs, (((1,), (0,)), ((), ())), preferred_element_type=F32)


def rotation_of(q_w, q_x, q_y, q_z):
    return [
        1.0 - 2.0 * (q_y * q_y + q_z * q_z),
        2.0 * (q_x * q_y - q_w * q_z),
        2.0 * (q_x * q_z + q_w * q_y),
        2.0 * (q_x * q_y + q_w * q_z),
        1.0 - 2.0 * (q_x * q_x + q_z * q_z),
        2.0 * (q_y * q_z - q_w * q_x),
        2.0 * (q_x * q_z - q_w * q_y),
        2.0 * (q_y * q_z + q_w * q_x),
        1.0 - 2.0 * (q_x * q_x + q_y * q_y),
    ]


def unit_quaternion(quaternion):
    total = sum(part * part for part in quaternion[1:]) + quaternion[0] * quaternion[0]
    inverse = lax.rsqrt(total)
    return [part * inverse for part in quaternion], inverse


def shape_matrix(log_scales, quaternion):
    scales = [jnp.exp(part) for part in log_scales]
    unit, inverse = unit_quaternion(quaternion)
    rotation = rotation_of(*unit)
    matrix = [rotation[3 * i + j] * scales[j] for i in range(3) for j in range(3)]
    return matrix, scales, unit, inverse


def harmonics(x, y, z):
    xx, yy, zz = x * x, y * y, z * z
    rim = 4.0 * zz - xx - yy
    gap = xx - yy
    return [
        -sh_second * y,
        sh_second * z,
        -sh_second * x,
        sh_third[0] * (x * y),
        sh_third[1] * (y * z),
        sh_third[2] * (2.0 * zz - xx - yy),
        sh_third[3] * (x * z),
        sh_third[4] * gap,
        sh_fourth[0] * (y * (3.0 * xx - yy)),
        sh_fourth[1] * (x * y * z),
        sh_fourth[2] * (y * rim),
        sh_fourth[3] * (z * (2.0 * zz - 3.0 * xx - 3.0 * yy)),
        sh_fourth[4] * (x * rim),
        sh_fourth[5] * (z * gap),
        sh_fourth[6] * (x * (xx - 3.0 * yy)),
    ]


def geometry(pos, matrix):
    x, y, z = pos
    inv_z = 1.0 / z
    jac = focal_length * inv_z
    screen_x = x * jac
    screen_y = y * jac
    jac_x = -screen_x * inv_z
    jac_y = -screen_y * inv_z
    row_u = [jac * matrix[j] + jac_x * matrix[6 + j] for j in range(3)]
    row_v = [jac * matrix[3 + j] + jac_y * matrix[6 + j] for j in range(3)]
    cov_a = row_u[0] * row_u[0] + row_u[1] * row_u[1] + row_u[2] * row_u[2] + dilation
    cov_c = row_v[0] * row_v[0] + row_v[1] * row_v[1] + row_v[2] * row_v[2] + dilation
    cov_b = row_u[0] * row_v[0] + row_u[1] * row_v[1] + row_u[2] * row_v[2]
    inv_det = 1.0 / (cov_a * cov_c - cov_b * cov_b)
    return inv_z, jac, screen_x, screen_y, jac_x, jac_y, row_u, row_v, cov_a, cov_b, cov_c, inv_det


def direction(pos):
    x, y, z = pos
    inverse = lax.rsqrt(x * x + y * y + z * z)
    return [x * inverse, y * inverse, z * inverse], inverse


def raw_colour(load, channel, basis):
    total = load(11 + 16 * channel) * sh_first
    for j in range(15):
        total = total + load(12 + 16 * channel + j) * basis[j]
    return total + 0.5


def lane_gather(source, index):
    return jnp.take_along_axis(source, index, axis=1, mode="promise_in_bounds")


def gather_chunk(table, high, low):
    shape = (8, LANES)
    low = jnp.broadcast_to(low, shape)
    high = jnp.broadcast_to(high, shape)
    top = bottom = jnp.zeros(shape, F32)
    for chunk in range(16):
        here = high == chunk
        top = jnp.where(here, lane_gather(table[pl.ds(16 * chunk, 8), :], low), top)
        bottom = jnp.where(here, lane_gather(table[pl.ds(16 * chunk + 8, 8), :], low), bottom)
    return top, bottom


def project_body(camera, params, slots, dense, outgoing, packed, table):
    rows = params.shape[0]
    for group in range(0, rows, 8):
        size = min(8, rows - group)
        for chunk in range(16):
            packed[pl.ds(group * 16 + chunk * 8, size), :] = params[
                pl.ds(group, size), pl.ds(chunk * LANES, LANES)
            ]
    for row in range(rows):
        dense[row] = packed[pl.ds((row // 8) * 128 + row % 8, 16, stride=8), :]
    table[...] = jnp.zeros_like(table)

    load = lambda row: dense[row]
    pos = [load(i) - camera[0, i] for i in range(3)]
    matrix, _, _, _ = shape_matrix([load(3 + i) for i in range(3)], [load(6 + i) for i in range(4)])
    _, _, screen_x, screen_y, _, _, _, _, cov_a, cov_b, cov_c, inv_det = geometry(pos, matrix)
    unit, _ = direction(pos)
    basis = harmonics(*unit)
    features = [
        screen_x,
        screen_y,
        cov_c * inv_det,
        -cov_b * inv_det,
        cov_a * inv_det,
        1.0 / (1.0 + jnp.exp(-load(10))),
    ]
    features += [jnp.maximum(raw_colour(load, channel, basis), 0.0) for channel in range(3)]
    for i, feature in enumerate(features):
        table[pl.ds(i, 16, stride=16), :] = feature

    def one_chunk(chunk, carry):
        index = slots[0, :, pl.ds(pl.multiple_of(chunk * LANES, LANES), LANES)]
        top, bottom = gather_chunk(table, index >> 7, index & 127)
        outgoing[chunk, pl.ds(0, 8), :] = top
        outgoing[chunk, pl.ds(8, 1), :] = bottom[0:1]
        return carry

    lax.fori_loop(0, 16, one_chunk, 0, unroll=2)


def block_transpose(rows):
    group = lax.broadcasted_iota(jnp.int32, rows[0].shape, 1) // 16
    for step in (1, 2, 4):
        odd = (group & step) != 0
        fresh = list(rows)
        for i in range(8):
            if i & step:
                continue
            first, second = rows[i], rows[i + step]
            fresh[i] = jnp.where(odd, pltpu.roll(second, 16 * step, 1), first)
            fresh[i + step] = jnp.where(odd, second, pltpu.roll(first, LANES - 16 * step, 1))
        rows = fresh
    return rows


def remote(src_ref, dst_ref, send_sem, recv_sem, k, device_id):
    copy = pltpu.make_async_remote_copy(
        src_ref=src_ref,
        dst_ref=dst_ref,
        send_sem=send_sem.at[k - 1],
        recv_sem=recv_sem.at[k - 1],
        device_id=device_id,
        device_id_type=pl.DeviceIdType.MESH,
    )
    copy.start()
    return copy


def y_peer(my_y, my_zc, k):
    peer = lax.rem(my_y + k, Y_DEVS)
    return peer, {"cell": peer * ZC_DEVS + my_zc}


def zc_peer(my_y, my_zc, k):
    peer = lax.rem(my_zc + k, ZC_DEVS)
    return peer, {"cell": my_y * ZC_DEVS + peer}


def view_peer(view, k):
    return {"view": lax.rem(view + k, VIEW_DEVS)}


def greet(my_y, my_zc, view):
    barrier = pltpu.get_barrier_semaphore()
    peers = [y_peer(my_y, my_zc, k)[1] for k in Y_ORDER]
    peers += [zc_peer(my_y, my_zc, k)[1] for k in ZC_ORDER]
    peers += [view_peer(view, k) for k in VIEW_ORDER]
    for peer in peers:
        pl.semaphore_signal(barrier, inc=1, device_id=peer, device_id_type=pl.DeviceIdType.MESH)
    return barrier, len(peers)


def over_y(source, target, my_y, my_zc, sems):
    copies = []
    for k in Y_ORDER:
        peer, device_id = y_peer(my_y, my_zc, k)
        copies.append(
            remote(source.at[pl.ds(2 * peer, 2)], target.at[pl.ds(2 * my_y, 2)], *sems, k, device_id)
        )
    target[pl.ds(2 * my_y, 2)] = source[pl.ds(2 * my_y, 2)]
    return copies


def over_zc(source, target, my_y, my_zc, sems):
    copies = []
    for k in ZC_ORDER:
        peer, device_id = zc_peer(my_y, my_zc, k)
        copies.append(remote(source.at[peer], target.at[my_zc], *sems, k, device_id))
    target[my_zc] = source[my_zc]
    return copies


def wait_all(copies):
    for copy in copies:
        copy.wait()


def regroup_by_zc(source, target):
    for half in range(2):
        rows = block_transpose([source[2 * y + half] for y in range(Y_DEVS)])
        for i in range(8):
            target[8 * half + i] = rows[i]


def regroup_by_y(source, target):
    for half in range(2):
        rows = block_transpose([source[8 * half + i] for i in range(8)])
        for y in range(Y_DEVS):
            target[2 * y + half] = rows[y]


def scatter_operands(values, high, low, left, right, column):
    columns = pl.ds(pl.multiple_of(column, LANES), LANES)
    shape = (16, LANES)
    here = jnp.broadcast_to(high, shape) == lax.broadcasted_iota(jnp.int32, shape, 0)
    for piece, rows in enumerate(split3(values)):
        for f in range(FEATS):
            spread = jnp.where(here, jnp.broadcast_to(rows[f : f + 1], shape), 0.0)
            left[pl.ds((piece * FEATS + f) * 16, 16), columns] = spread.astype(BF16)
    shape = (LANES, LANES)
    hot = jnp.broadcast_to(low, shape) == lax.broadcasted_iota(jnp.int32, shape, 0)
    right[:, columns] = jnp.where(hot, 1.0, 0.0).astype(BF16)


def scatter_product(left, right):
    size = FEATS * 16
    total = dot_nt(left[...], right[...])
    return total[0:size] + total[size : 2 * size] + total[2 * size : 3 * size]


def tile_body(
    tile_ids, tile_len, received, lists, targets, pictures, slot_grads,
    table, feats, alpha, before, weight, weight_hi, weight_lo, part_hi, part_lo, upper, grads, left, right, spread,
):
    tiles, entries = lists.shape[1], lists.shape[2]
    chunks = entries // LANES
    pixels = TILE_SIDE * TILE_SIDE
    half = entries // 2
    table[...] = jnp.zeros_like(table)
    for chunk in range(16):
        table[pl.ds(16 * chunk, FEATS), :] = received[chunk]
    row = lax.broadcasted_iota(jnp.int32, (entries, entries), 0)
    col = lax.broadcasted_iota(jnp.int32, (entries, entries), 1)
    upper[...] = jnp.where(row < col, 1.0, 0.0).astype(BF16)
    grads[...] = jnp.zeros_like(grads)

    def slot_of(tile, chunk):
        index = lists[0, pl.ds(tile, 1), pl.ds(chunk * LANES, LANES)]
        return (index >> 4) & 15, ((index >> 8) << 4) | (index & 15)

    for tile in range(tiles):
        for chunk in range(chunks):
            high, low = slot_of(tile, chunk)
            top, bottom = gather_chunk(table, high, low)
            feats[pl.ds(0, 8), pl.ds(chunk * LANES, LANES)] = top
            feats[pl.ds(8, 8), pl.ds(chunk * LANES, LANES)] = bottom
        number = tile_ids[0, tile]
        length = tile_len[0, tile]
        left_x = (TILE_SIDE * lax.rem(number, TILE_COLS)).astype(F32) + 0.5
        top_y = (TILE_SIDE * (number // TILE_COLS)).astype(F32) + 0.5
        shape = (TILE_SIDE, LANES)
        pixel_x = lax.broadcasted_iota(jnp.int32, shape, 0).astype(F32) + left_x

        def feature(f, chunk):
            return jnp.broadcast_to(feats[pl.ds(f, 1), pl.ds(chunk * LANES, LANES)], (8, LANES))

        def twice(rows):
            return jnp.concatenate([rows, rows], axis=0)

        for chunk in range(chunks):
            lanes = pl.ds(chunk * LANES, LANES)
            lane = lax.broadcasted_iota(jnp.int32, (8, LANES), 1) + chunk * LANES
            opacity = twice(jnp.where(lane < length, feature(5, chunk), 0.0))
            delta_x = twice(feature(0, chunk)) - pixel_x
            part_x = twice(-0.5 * feature(2, chunk)) * delta_x * delta_x
            cross = twice(-feature(3, chunk)) * delta_x
            screen_y = feature(1, chunk)
            conic_c = -0.5 * feature(4, chunk)

            def one_row(y, carry):
                rows = pl.ds(pl.multiple_of(y * TILE_SIDE, TILE_SIDE), TILE_SIDE)
                delta_y = screen_y - (top_y + y.astype(F32))
                part_y = conic_c * delta_y * delta_y
                value = opacity * jnp.exp(part_x + cross * twice(delta_y) + twice(part_y))
                alpha[rows, lanes] = value
                part_hi[rows, lanes], part_lo[rows, lanes] = split2(jnp.log(1.0 - value))
                return carry

            lax.fori_loop(0, TILE_SIDE, one_row, 0, unroll=4)

        def prefix(part):
            first = dot_nn(part[:, pl.ds(0, half)], upper[pl.ds(0, half), :])
            second = dot_nn(part[:, pl.ds(half, half)], upper[pl.ds(half, half), pl.ds(half, half)])
            return first[:, :half], first[:, half:] + second

        high_left, high_right = prefix(part_hi)
        low_left, low_right = prefix(part_lo)
        before[:, pl.ds(0, half)] = high_left + low_left
        before[:, pl.ds(half, half)] = high_right + low_right

        def one_weight(y, carry):
            rows = pl.ds(pl.multiple_of(y * TILE_SIDE, TILE_SIDE), TILE_SIDE)
            value = jnp.exp(before[rows, :]) * alpha[rows, :]
            weight[rows, :] = value
            weight_hi[rows, :], weight_lo[rows, :] = split2(value)
            return carry

        lax.fori_loop(0, TILE_SIDE, one_weight, 0, unroll=2)

        colours = jnp.concatenate([feats[pl.ds(6, 3), :], jnp.zeros((5, entries), F32)], axis=0)
        colour_hi = colours.astype(BF16).astype(F32)
        colour_lo = (colours - colour_hi).astype(BF16).astype(F32)
        both = jnp.concatenate([colour_hi, colour_lo], axis=0).astype(BF16)
        product = dot_nt(both, weight_hi[...])
        picture = product[0:8] + product[8:16] + dot_nt(both, weight_lo[...])[0:8]
        pictures[0, :, tile, :] = picture[0:3]
        residual = picture - jnp.concatenate([targets[0, :, tile, :], jnp.zeros((5, pixels), F32)], axis=0)
        residual_hi = residual.astype(BF16).astype(F32)
        residual_lo = (residual - residual_hi).astype(BF16).astype(F32)

        pair = jnp.concatenate([residual_hi, residual_lo], axis=0).astype(BF16)
        product = dot_nn(pair, weight_hi[...])
        colour_grad = product[0:8] + product[8:16] + dot_nn(pair, weight_lo[...])[0:8]

        stack = jnp.concatenate(
            [residual_hi, residual_lo, residual_hi, jnp.zeros((104, pixels), F32)], axis=0
        )
        columns = jnp.transpose(stack).astype(BF16)
        rows24 = jnp.concatenate(
            [colour_hi, colour_hi, colour_lo, jnp.zeros((104, entries), F32)], axis=0
        ).astype(BF16)
        before[...] = dot_nn(columns, rows24)

        def one_share(y, carry):
            rows = pl.ds(pl.multiple_of(y * TILE_SIDE, TILE_SIDE), TILE_SIDE)
            value = before[rows, :] * weight[rows, :]
            weight[rows, :] = value
            part_hi[rows, :], part_lo[rows, :] = split2(value)
            return carry

        lax.fori_loop(0, TILE_SIDE, one_share, 0, unroll=2)

        def suffix(part):
            first = dot_nt(part[:, pl.ds(0, half)], upper[pl.ds(0, half), pl.ds(0, half)])
            second = dot_nt(part[:, pl.ds(half, half)], upper[:, pl.ds(half, half)])
            return first + second[:, :half], second[:, half:]

        high_left, high_right = suffix(part_hi)
        low_left, low_right = suffix(part_lo)
        before[:, pl.ds(0, half)] = high_left + low_left
        before[:, pl.ds(half, half)] = high_right + low_right

        for chunk in range(chunks):
            lanes = pl.ds(chunk * LANES, LANES)
            screen_y = feature(1, chunk)

            def one_row(y, carry):
                rows = pl.ds(pl.multiple_of(y * TILE_SIDE, TILE_SIDE), TILE_SIDE)
                sum_0, sum_1, sum_2 = carry
                delta_y = twice(screen_y - (top_y + y.astype(F32)))
                value = alpha[rows, lanes]
                grad = weight[rows, lanes] - before[rows, lanes] * (value / (1.0 - value))
                slope = grad * delta_y
                return sum_0 + grad, sum_1 + slope, sum_2 + slope * delta_y

            zero = jnp.zeros(shape, F32)
            sum_0, sum_1, sum_2 = lax.fori_loop(0, TILE_SIDE, one_row, (zero, zero, zero), unroll=4)
            delta_x = twice(feature(0, chunk)) - pixel_x
            over = lambda rows: jnp.sum(rows, axis=0, keepdims=True)
            first_x = over(delta_x * sum_0)
            first_y = over(sum_1)
            row_of = lambda f: feats[pl.ds(f, 1), lanes]
            out = pl.ds(tile * entries + chunk * LANES, LANES)
            grads[pl.ds(0, 1), out] = -row_of(2) * first_x - row_of(3) * first_y
            grads[pl.ds(1, 1), out] = -row_of(4) * first_y - row_of(3) * first_x
            grads[pl.ds(2, 1), out] = -0.5 * over(delta_x * delta_x * sum_0)
            grads[pl.ds(3, 1), out] = -over(delta_x * sum_1)
            grads[pl.ds(4, 1), out] = -0.5 * over(sum_2)
            grads[pl.ds(5, 1), out] = over(sum_0)
        grads[pl.ds(6, 3), pl.ds(tile * entries, entries)] = colour_grad[0:3]

        for chunk in range(chunks):
            high, low = slot_of(tile, chunk)
            column = tile * entries + chunk * LANES
            scatter_operands(grads[:, pl.ds(column, LANES)], high, low, left, right, column)

    total = scatter_product(left, right)
    for f in range(FEATS):
        spread[pl.ds(f, 16, stride=16), :] = total[16 * f : 16 * f + 16]
    for chunk in range(16):
        slot_grads[chunk] = spread[pl.ds(16 * chunk, FEATS), :]


VIEW_ROWS = FEATS * 16 + 8


def gauss_body(camera, returned, slots, out, left, right):
    def one_chunk(chunk, carry):
        column = pl.multiple_of(chunk * LANES, LANES)
        index = slots[0, :, pl.ds(column, LANES)]
        scatter_operands(returned[chunk], index >> 7, index & 127, left, right, column)
        return carry

    lax.fori_loop(0, 16, one_chunk, 0)
    out[pl.ds(0, FEATS * 16), :] = scatter_product(left, right)
    row = lax.broadcasted_iota(jnp.int32, (8, LANES), 0)
    shift = jnp.where(row == 0, camera[0, 0], jnp.where(row == 1, camera[0, 1], camera[0, 2]))
    out[pl.ds(FEATS * 16, 8), :] = shift


def render_kernel(
    camera, tile_ids, tile_len, params, slots, lists, targets,
    pictures, dense, every,
    packed, table, outgoing, landed, staged, received, slot_grads, landed_back, staged_back, returned, mine,
    feats, alpha, before, weight, weight_hi, weight_lo, part_hi, part_lo, upper, grads, tile_left, tile_right, spread,
    left, right, *sems,
):
    cell, view = lax.axis_index("cell"), lax.axis_index("view")
    my_y, my_zc = cell // ZC_DEVS, lax.rem(cell, ZC_DEVS)
    barrier, greetings = greet(my_y, my_zc, view)
    project_body(camera, params, slots, dense, outgoing, packed, table)
    pl.semaphore_wait(barrier, greetings)

    wait_all(over_y(outgoing, landed, my_y, my_zc, sems[0:2]))
    regroup_by_zc(landed, staged)
    wait_all(over_zc(staged, received, my_y, my_zc, sems[2:4]))
    tile_body(
        tile_ids, tile_len, received, lists, targets, pictures, slot_grads,
        table, feats, alpha, before, weight, weight_hi, weight_lo, part_hi, part_lo, upper, grads,
        tile_left, tile_right, spread,
    )
    wait_all(over_zc(slot_grads, landed_back, my_y, my_zc, sems[4:6]))
    regroup_by_y(landed_back, staged_back)
    wait_all(over_y(staged_back, returned, my_y, my_zc, sems[6:8]))
    gauss_body(camera, returned, slots, mine, left, right)
    copies = [remote(mine, every.at[view], sems[8], sems[9], k, view_peer(view, k)) for k in VIEW_ORDER]
    every[view] = mine[...]
    wait_all(copies)


def render_call(camera, tile_ids, tile_len, params, slots, lists, targets):
    rows = params.shape[0]
    tiles, entries = lists.shape[1], lists.shape[2]
    pixels = TILE_SIDE * TILE_SIDE
    smem = pl.BlockSpec(memory_space=pltpu.SMEM)
    vmem = pl.BlockSpec(memory_space=pltpu.VMEM)
    plane = pltpu.VMEM((pixels, entries), F32)
    thin = pltpu.VMEM((pixels, entries), BF16)
    blocks = pltpu.VMEM((16, FEATS, LANES), F32)
    pair = [pltpu.SemaphoreType.DMA((Y_DEVS - 1,))] * 2
    many = [pltpu.SemaphoreType.DMA((ZC_DEVS - 1,))] * 2
    few = [pltpu.SemaphoreType.DMA((VIEW_DEVS - 1,))] * 2
    return pl.pallas_call(
        render_kernel,
        out_shape=(
            jax.ShapeDtypeStruct(targets.shape, F32),
            jax.ShapeDtypeStruct((rows, 16, LANES), F32),
            jax.ShapeDtypeStruct((VIEW_DEVS, VIEW_ROWS, LANES), F32),
        ),
        in_specs=[smem, smem, smem, vmem, vmem, vmem, vmem],
        out_specs=(vmem, vmem, vmem),
        scratch_shapes=[
            pltpu.VMEM((64 * 16, LANES), F32),
            pltpu.VMEM((256, LANES), F32),
        ]
        + [blocks] * 8
        + [
            pltpu.VMEM((VIEW_ROWS, LANES), F32),
            pltpu.VMEM((16, entries), F32),
            plane,
            plane,
            plane,
            thin,
            thin,
            thin,
            thin,
            pltpu.VMEM((entries, entries), BF16),
            pltpu.VMEM((16, tiles * entries), F32),
            pltpu.VMEM((3 * FEATS * 16, tiles * entries), BF16),
            pltpu.VMEM((LANES, tiles * entries), BF16),
            pltpu.VMEM((256, LANES), F32),
            pltpu.VMEM((3 * FEATS * 16, 2048), BF16),
            pltpu.VMEM((LANES, 2048), BF16),
        ]
        + pair + many + many + pair + few,
        compiler_params=pltpu.CompilerParams(
            collective_id=0, has_side_effects=True, vmem_limit_bytes=40 * 2**20
        ),
        name="render",
    )(camera, tile_ids, tile_len, params, slots, lists, targets)


def param_kernel(pictures_in, dense, every, pictures, gradient, packed):
    pictures[...] = pictures_in[...]
    rows = gradient.shape[0]

    def one_half(half, carry):
        part = pl.ds(pl.multiple_of(half * 8, 8), 8)
        load = lambda row: dense[row, part, :]

        def store(row, value):
            packed[pl.ds((row // 8) * 128 + row % 8 + half * 64, 8, stride=8), :] = value

        def add(row, value, view):
            if view:
                where = pl.ds((row // 8) * 128 + row % 8 + half * 64, 8, stride=8)
                packed[where, :] = packed[where, :] + value
            else:
                store(row, value)

        quaternion = [load(6 + i) for i in range(4)]
        matrix, scales, unit_q, inv_norm = shape_matrix([load(3 + i) for i in range(3)], quaternion)
        grad_matrix = [0.0] * 9
        grad_pos = [0.0] * 3
        grad_log = 0.0
        for view in range(VIEW_DEVS):
            slot = lambda f: every[view, pl.ds(pl.multiple_of(f * 16 + half * 8, 8), 8), :]
            shift = lambda i: jnp.broadcast_to(every[view, pl.ds(FEATS * 16 + i, 1), :], (8, LANES))
            pos = [load(i) - shift(i) for i in range(3)]
            inv_z, jac, screen_x, screen_y, jac_x, jac_y, row_u, row_v, cov_a, cov_b, cov_c, inv_det = geometry(
                pos, matrix
            )
            g_a, g_b, g_c = slot(2), slot(3), slot(4)
            g_det = -(g_a * cov_c - g_b * cov_b + g_c * cov_a) * inv_det * inv_det
            d_a = g_c * inv_det + g_det * cov_c
            d_c = g_a * inv_det + g_det * cov_a
            d_b = -g_b * inv_det - 2.0 * g_det * cov_b
            d_a, d_c = 2.0 * d_a, 2.0 * d_c
            g_u = [d_a * row_u[j] + d_b * row_v[j] for j in range(3)]
            g_v = [d_c * row_v[j] + d_b * row_u[j] for j in range(3)]
            for j in range(3):
                grad_matrix[j] = grad_matrix[j] + jac * g_u[j]
                grad_matrix[3 + j] = grad_matrix[3 + j] + jac * g_v[j]
                grad_matrix[6 + j] = grad_matrix[6 + j] + jac_x * g_u[j] + jac_y * g_v[j]
            g_jac = sum(g_u[j] * matrix[j] + g_v[j] * matrix[3 + j] for j in range(3))
            g_jac_x = sum(g_u[j] * matrix[6 + j] for j in range(3))
            g_jac_y = sum(g_v[j] * matrix[6 + j] for j in range(3))
            g_sx = slot(0) - inv_z * g_jac_x
            g_sy = slot(1) - inv_z * g_jac_y
            g_inv = (
                focal_length * (g_jac + pos[0] * g_sx + pos[1] * g_sy) - screen_x * g_jac_x - screen_y * g_jac_y
            )
            g_pos = [jac * g_sx, jac * g_sy, -inv_z * inv_z * g_inv]

            unit, inv_len = direction(pos)
            basis, pull = jax.vjp(harmonics, *unit)
            g_basis = [0.0] * 15
            for channel in range(3):
                colour = raw_colour(load, channel, basis)
                g_colour = slot(6 + channel)
                g_colour = jnp.where(colour > 0.0, g_colour, jnp.where(colour < 0.0, 0.0, 0.5 * g_colour))
                add(11 + 16 * channel, sh_first * g_colour, view)
                for j in range(15):
                    add(12 + 16 * channel + j, basis[j] * g_colour, view)
                    g_basis[j] = g_basis[j] + load(12 + 16 * channel + j) * g_colour
            g_unit = pull(g_basis)
            along = unit[0] * g_unit[0] + unit[1] * g_unit[1] + unit[2] * g_unit[2]
            for i in range(3):
                grad_pos[i] = grad_pos[i] + g_pos[i] + inv_len * (g_unit[i] - unit[i] * along)
            grad_log = grad_log + slot(5)

        for i in range(3):
            store(i, grad_pos[i])
            store(3 + i, sum(grad_matrix[3 * k + i] * matrix[3 * k + i] for k in range(3)))
        rotation, pull = jax.vjp(rotation_of, *unit_q)
        g_unit = pull([grad_matrix[3 * i + j] * scales[j] for i in range(3) for j in range(3)])
        along = sum(unit_q[i] * g_unit[i] for i in range(4))
        for i in range(4):
            store(6 + i, inv_norm * (g_unit[i] - unit_q[i] * along))
        store(10, grad_log * (1.0 / (1.0 + jnp.exp(load(10)))))
        return carry

    lax.fori_loop(0, 2, one_half, 0)
    for group in range(0, rows, 8):
        size = min(8, rows - group)
        for chunk in range(16):
            gradient[pl.ds(group, size), pl.ds(chunk * LANES, LANES)] = packed[
                pl.ds(group * 16 + chunk * 8, size), :
            ]


def param_call(pictures, dense, every):
    vmem = pl.BlockSpec(memory_space=pltpu.VMEM)
    return pl.pallas_call(
        param_kernel,
        out_shape=(
            jax.ShapeDtypeStruct(pictures.shape, F32),
            jax.ShapeDtypeStruct((dense.shape[0], 2048), F32),
        ),
        in_specs=[vmem, vmem, vmem],
        out_specs=(vmem, vmem),
        scratch_shapes=[pltpu.VMEM((64 * 16, LANES), F32)],
        compiler_params=pltpu.CompilerParams(vmem_limit_bytes=24 * 2**20),
        name="params",
    )(pictures, dense, every)


def local(params, cameras, targets, tile_ids, send_slots, tile_lists, tile_len):
    pictures, dense, every = render_call(
        cameras, tile_ids, tile_len, params, send_slots, tile_lists, jnp.transpose(targets, (0, 2, 1, 3))
    )
    pictures, gradient = param_call(pictures, dense, every)
    return jnp.transpose(pictures, (0, 2, 1, 3)), gradient


def solution(mesh):
    return jax.shard_map(
        local,
        mesh=mesh,
        in_specs=(
            P(None, "cell"),
            P("view", None),
            P("view", "cell", None, None),
            P("view", "cell"),
            P("view", "cell", None),
            P("view", "cell", None),
            P("view", "cell"),
        ),
        out_specs=(P("view", "cell", None, None), P(None, "cell")),
        check_vma=False,
    )
```

```python
import jax
import jax.numpy as jnp
from jax import lax
from jax.experimental import pallas as pl
from jax.experimental.pallas import tpu as pltpu
from jax.sharding import PartitionSpec as P

TILE_SIDE = 16
TILE_COLS = 32
LANES = 128
Y_DEVS = 8
ZC_DEVS = 16
VIEW_DEVS = 4
FEATS = 9
Y_ORDER = (4, 3, 5, 2, 6, 1, 7)
ZC_ORDER = (8, 9, 7, 6, 10, 5, 11, 4, 12, 3, 13, 2, 14, 1, 15)
VIEW_ORDER = (2, 1, 3)
ENTRIES = 512
TILES_DEV = 2
PIXELS = 256
ROWS = 59
G_DEV = 2048
LOG2_E = 1.4426950408889634
F32 = jnp.float32
BF16 = jnp.bfloat16

focal_length = 800.0
dilation = 0.3
sh_first = 0.28209479177387814
sh_second = 0.4886025119029199
sh_third = (
    1.0925484305920792,
    -1.0925484305920792,
    0.31539156525252005,
    -1.0925484305920792,
    0.5462742152960396,
)
sh_fourth = (
    -0.5900435899266435,
    2.890611442640554,
    -0.4570457994644658,
    0.3731763325901154,
    -0.4570457994644658,
    1.445305721320277,
    -0.5900435899266435,
)


def split2(value):
    high = value.astype(BF16)
    return high, (value - high.astype(F32)).astype(BF16)


def dot_nt(lhs, rhs):
    return lax.dot_general(lhs, rhs, (((1,), (1,)), ((), ())), preferred_element_type=F32)


def dot_nn(lhs, rhs):
    return lax.dot_general(lhs, rhs, (((1,), (0,)), ((), ())), preferred_element_type=F32)


def rotation_of(q_w, q_x, q_y, q_z):
    return [
        1.0 - 2.0 * (q_y * q_y + q_z * q_z),
        2.0 * (q_x * q_y - q_w * q_z),
        2.0 * (q_x * q_z + q_w * q_y),
        2.0 * (q_x * q_y + q_w * q_z),
        1.0 - 2.0 * (q_x * q_x + q_z * q_z),
        2.0 * (q_y * q_z - q_w * q_x),
        2.0 * (q_x * q_z - q_w * q_y),
        2.0 * (q_y * q_z + q_w * q_x),
        1.0 - 2.0 * (q_x * q_x + q_y * q_y),
    ]


def unit_quaternion(quaternion):
    total = sum(part * part for part in quaternion[1:]) + quaternion[0] * quaternion[0]
    inverse = lax.rsqrt(total)
    return [part * inverse for part in quaternion], inverse


def shape_matrix(log_scales, quaternion):
    scales = [jnp.exp(part) for part in log_scales]
    unit, inverse = unit_quaternion(quaternion)
    rotation = rotation_of(*unit)
    matrix = [rotation[3 * i + j] * scales[j] for i in range(3) for j in range(3)]
    return matrix, scales, unit, inverse


def harmonics(x, y, z):
    xx, yy, zz = x * x, y * y, z * z
    rim = 4.0 * zz - xx - yy
    gap = xx - yy
    return [
        -sh_second * y,
        sh_second * z,
        -sh_second * x,
        sh_third[0] * (x * y),
        sh_third[1] * (y * z),
        sh_third[2] * (2.0 * zz - xx - yy),
        sh_third[3] * (x * z),
        sh_third[4] * gap,
        sh_fourth[0] * (y * (3.0 * xx - yy)),
        sh_fourth[1] * (x * y * z),
        sh_fourth[2] * (y * rim),
        sh_fourth[3] * (z * (2.0 * zz - 3.0 * xx - 3.0 * yy)),
        sh_fourth[4] * (x * rim),
        sh_fourth[5] * (z * gap),
        sh_fourth[6] * (x * (xx - 3.0 * yy)),
    ]


def geometry(pos, matrix):
    x, y, z = pos
    inv_z = 1.0 / z
    jac = focal_length * inv_z
    screen_x = x * jac
    screen_y = y * jac
    jac_x = -screen_x * inv_z
    jac_y = -screen_y * inv_z
    row_u = [jac * matrix[j] + jac_x * matrix[6 + j] for j in range(3)]
    row_v = [jac * matrix[3 + j] + jac_y * matrix[6 + j] for j in range(3)]
    cov_a = row_u[0] * row_u[0] + row_u[1] * row_u[1] + row_u[2] * row_u[2] + dilation
    cov_c = row_v[0] * row_v[0] + row_v[1] * row_v[1] + row_v[2] * row_v[2] + dilation
    cov_b = row_u[0] * row_v[0] + row_u[1] * row_v[1] + row_u[2] * row_v[2]
    inv_det = 1.0 / (cov_a * cov_c - cov_b * cov_b)
    return inv_z, jac, screen_x, screen_y, jac_x, jac_y, row_u, row_v, cov_a, cov_b, cov_c, inv_det


def direction(pos):
    x, y, z = pos
    inverse = lax.rsqrt(x * x + y * y + z * z)
    return [x * inverse, y * inverse, z * inverse], inverse


def raw_colour(load, channel, basis):
    total = load(11 + 16 * channel) * sh_first
    for j in range(15):
        total = total + load(12 + 16 * channel + j) * basis[j]
    return total + 0.5


KEPT = 40
SHAPE_ROWS = 17


def keep_view(load, shift, matrix, saved, base):
    pos = [load(i) - shift[i] for i in range(3)]
    inv_z, jac, screen_x, screen_y, jac_x, jac_y, row_u, row_v, cov_a, cov_b, cov_c, inv_det = geometry(pos, matrix)
    unit, inv_len = direction(pos)
    basis = harmonics(*unit)
    raw = [raw_colour(load, channel, basis) for channel in range(3)]
    gates = [jnp.where(value > 0.0, 1.0, jnp.where(value < 0.0, 0.0, 0.5)) for value in raw]
    values = [pos[0], pos[1], inv_z, jac, screen_x, screen_y, jac_x, jac_y]
    values += row_u + row_v + [cov_a, cov_b, cov_c, inv_det] + unit + [inv_len] + basis + gates
    for i, value in enumerate(values):
        saved[base + i] = value
    features = [screen_x, screen_y, cov_c * inv_det, -cov_b * inv_det, cov_a * inv_det]
    features.append(1.0 / (1.0 + jnp.exp(-load(10))))
    return features + [jnp.maximum(value, 0.0) for value in raw]


def pull_view(load, slot, matrix, saved, base, totals, total_base, first, colour, colour_base):
    kept = lambda i: saved[base + i]
    inv_z, jac, screen_x, screen_y, jac_x, jac_y = [kept(2 + i) for i in range(6)]
    row_u, row_v = [kept(8 + i) for i in range(3)], [kept(11 + i) for i in range(3)]
    cov_a, cov_b, cov_c, inv_det = [kept(14 + i) for i in range(4)]
    g_a, g_b, g_c = slot(2), slot(3), slot(4)
    g_det = -(g_a * cov_c - g_b * cov_b + g_c * cov_a) * inv_det * inv_det
    d_a = 2.0 * (g_c * inv_det + g_det * cov_c)
    d_c = 2.0 * (g_a * inv_det + g_det * cov_a)
    d_b = -g_b * inv_det - 2.0 * g_det * cov_b
    g_u = [d_a * row_u[j] + d_b * row_v[j] for j in range(3)]
    g_v = [d_c * row_v[j] + d_b * row_u[j] for j in range(3)]
    g_matrix = [jac * g_u[j] for j in range(3)] + [jac * g_v[j] for j in range(3)]
    g_matrix += [jac_x * g_u[j] + jac_y * g_v[j] for j in range(3)]
    g_jac = sum(g_u[j] * matrix[j] + g_v[j] * matrix[3 + j] for j in range(1, 3)) + (
        g_u[0] * matrix[0] + g_v[0] * matrix[3]
    )
    g_jac_x = g_u[0] * matrix[6] + g_u[1] * matrix[7] + g_u[2] * matrix[8]
    g_jac_y = g_v[0] * matrix[6] + g_v[1] * matrix[7] + g_v[2] * matrix[8]
    g_sx = slot(0) - inv_z * g_jac_x
    g_sy = slot(1) - inv_z * g_jac_y
    g_inv = focal_length * (g_jac + kept(0) * g_sx + kept(1) * g_sy) - screen_x * g_jac_x - screen_y * g_jac_y
    g_pos = [jac * g_sx, jac * g_sy, -inv_z * inv_z * g_inv]

    g_basis = None
    for channel in range(3):
        g_colour = slot(6 + channel) * kept(37 + channel)
        colour[colour_base + channel] = g_colour
        terms = [load(12 + 16 * channel + j) * g_colour for j in range(15)]
        g_basis = terms if g_basis is None else [a + b for a, b in zip(g_basis, terms)]
    unit, inv_len = [kept(18 + i) for i in range(3)], kept(21)
    _, pull = jax.vjp(harmonics, *unit)
    g_unit = pull(g_basis)
    along = unit[0] * g_unit[0] + unit[1] * g_unit[1] + unit[2] * g_unit[2]
    for i in range(3):
        g_pos[i] = g_pos[i] + inv_len * (g_unit[i] - unit[i] * along)
    for i, value in enumerate(g_pos + g_matrix + [slot(5)]):
        totals[total_base + i] = value if first else totals[total_base + i] + value


def lane_gather(source, index):
    return jnp.take_along_axis(source, index, axis=1, mode="promise_in_bounds")


def gather_chunk(table, index):
    shape = (8, LANES)
    low = jnp.broadcast_to(index & 127, shape)
    high = jnp.broadcast_to(index >> 7, shape)
    top = bottom = jnp.zeros(shape, F32)
    for chunk in range(16):
        here = high == chunk
        top = jnp.where(here, lane_gather(table[pl.ds(16 * chunk, 8), :], low), top)
        bottom = jnp.where(here, lane_gather(table[pl.ds(16 * chunk + 8, 8), :], low), bottom)
    return top, bottom


def block_transpose(rows):
    group = lax.broadcasted_iota(jnp.int32, rows[0].shape, 1) // 16
    for step in (1, 2, 4):
        odd = (group & step) != 0
        fresh = list(rows)
        for i in range(8):
            if i & step:
                continue
            first, second = rows[i], rows[i + step]
            fresh[i] = jnp.where(odd, pltpu.roll(second, 16 * step, 1), first)
            fresh[i + step] = jnp.where(odd, second, pltpu.roll(first, LANES - 16 * step, 1))
        rows = fresh
    return rows


def remote(src_ref, dst_ref, send_sem, recv_sem, device_id):
    copy = pltpu.make_async_remote_copy(
        src_ref=src_ref,
        dst_ref=dst_ref,
        send_sem=send_sem,
        recv_sem=recv_sem,
        device_id=device_id,
        device_id_type=pl.DeviceIdType.MESH,
    )
    copy.start()
    return copy


def y_peer(my_y, my_zc, k):
    peer = lax.rem(my_y + k, Y_DEVS)
    return peer, {"cell": peer * ZC_DEVS + my_zc}


def zc_peer(my_y, my_zc, k):
    peer = lax.rem(my_zc + k, ZC_DEVS)
    return peer, {"cell": my_y * ZC_DEVS + peer}


def view_peer(view, k):
    return {"view": lax.rem(view + k, VIEW_DEVS)}


def greet(my_y, my_zc, view):
    barrier = pltpu.get_barrier_semaphore()
    peers = [y_peer(my_y, my_zc, k)[1] for k in Y_ORDER]
    peers += [zc_peer(my_y, my_zc, k)[1] for k in ZC_ORDER]
    peers += [view_peer(view, k) for k in VIEW_ORDER]
    for peer in peers:
        pl.semaphore_signal(barrier, inc=1, device_id=peer, device_id_type=pl.DeviceIdType.MESH)
    return barrier, len(peers)


def regroup(load, store):
    for half in range(2):
        for j, rows in enumerate(block_transpose([load(i, half) for i in range(8)])):
            store(j, half, rows)


def part_lanes(chunk):
    base = (chunk // 2) * 512 + (chunk % 2) * LANES
    return pl.ds(base, LANES), pl.ds(base + 256, LANES)


def fill_triangles(upper, lower):
    row = lax.broadcasted_iota(jnp.int32, (256, 256), 0)
    col = lax.broadcasted_iota(jnp.int32, (256, 256), 1)
    above = jnp.where(row < col, 1.0, 0.0).astype(BF16)
    below = jnp.where(row > col, 1.0, 0.0).astype(BF16)
    ones = jnp.ones((256, 256), BF16)
    for i in range(4):
        upper[pl.ds(256 * i, 256), :] = ones if i < 2 else above
        lower[pl.ds(256 * i, 256), :] = below if i < 2 else ones


def entry_slot(lists, tile, chunk):
    index = lists[0, pl.ds(tile, 1), pl.ds(chunk * LANES, LANES)]
    return (index >> 4) & 15, ((index >> 8) << 4) | (index & 15)


def hot_rows(index, count):
    shape = (count, LANES)
    return jnp.where(
        jnp.broadcast_to(index, shape) == lax.broadcasted_iota(jnp.int32, shape, 0), 1.0, 0.0
    ).astype(BF16)


def fill_masks(high, count, masks, base):
    high = jnp.broadcast_to(high, (16, LANES))
    for value in range(count):
        masks[pl.ds(base + 16 * value, 16), :] = jnp.where(high == value, 1.0, 0.0).astype(BF16)


def spread(values, count, masks, base, left, column):
    for i, piece in enumerate(split2(values)):
        for value in range(count):
            left[pl.ds((i * count + value) * 16, 16), pl.ds(column, LANES)] = (
                masks[pl.ds(base + 16 * value, 16), :] * piece
            )


def tile_body(
    tile_ids, tile_len, targets, pictures, slot_grads,
    feats, alpha, ratio, plane, weight, part, upper, lower, grads, masks, left, right,
):
    chunks = ENTRIES // LANES
    half = ENTRIES // 2
    for tile in range(TILES_DEV):
        number = tile_ids[0, tile]
        length = tile_len[0, tile]
        left_x = (TILE_SIDE * lax.rem(number, TILE_COLS)).astype(F32) + 0.5
        top_y = (TILE_SIDE * (number // TILE_COLS)).astype(F32) + 0.5
        shape = (TILE_SIDE, LANES)
        pixel_x = lax.broadcasted_iota(jnp.int32, shape, 0).astype(F32) + left_x
        whole = pl.ds(tile * ENTRIES, ENTRIES)

        def row_of(f, chunk):
            return feats[pl.ds(f, 1), pl.ds(tile * ENTRIES + chunk * LANES, LANES)]

        def feature(f, chunk):
            return jnp.broadcast_to(row_of(f, chunk), (8, LANES))

        def twice(rows):
            return jnp.concatenate([rows, rows], axis=0)

        def pixels_of(y):
            return pl.ds(pl.multiple_of(y * TILE_SIDE, TILE_SIDE), TILE_SIDE)

        for chunk in range(chunks):
            lanes = pl.ds(chunk * LANES, LANES)
            high, low = part_lanes(chunk)
            lane = lax.broadcasted_iota(jnp.int32, (8, LANES), 1) + chunk * LANES
            log_opacity = jnp.where(lane < length, jnp.log2(feature(5, chunk)), -1e30)
            delta_x = twice(feature(0, chunk)) - pixel_x
            part_x = twice((-0.5 * LOG2_E) * feature(2, chunk)) * delta_x * delta_x + twice(log_opacity)
            cross = twice(-LOG2_E * feature(3, chunk)) * delta_x
            screen_y = feature(1, chunk) - top_y
            conic_c = (-0.5 * LOG2_E) * feature(4, chunk)

            def one_row(y, carry):
                rows = pixels_of(y)
                delta_y = screen_y - y.astype(F32)
                part_y = conic_c * delta_y * delta_y
                value = jnp.exp2(part_x + cross * twice(delta_y) + twice(part_y))
                keep = jnp.log2(1.0 - value)
                alpha[rows, lanes] = value
                ratio[rows, lanes] = value * jnp.exp2(-keep)
                part[rows, high], part[rows, low] = split2(keep)
                return carry

            lax.fori_loop(0, TILE_SIDE, one_row, 0, unroll=TILE_SIDE)

        plane[:, pl.ds(0, half)] = dot_nn(part[:, pl.ds(0, 512)], upper[pl.ds(512, 512), :])
        plane[:, pl.ds(half, half)] = dot_nn(part[...], upper[...])

        for chunk in range(chunks):
            lanes = pl.ds(chunk * LANES, LANES)
            high, low = part_lanes(chunk)

            def one_weight(y, carry):
                rows = pixels_of(y)
                value = jnp.exp2(plane[rows, lanes]) * alpha[rows, lanes]
                weight[rows, lanes] = value
                part[rows, high], part[rows, low] = split2(value)
                return carry

            lax.fori_loop(0, TILE_SIDE, one_weight, 0, unroll=TILE_SIDE)

        colours = jnp.concatenate([feats[pl.ds(6, 3), whole], jnp.zeros((5, ENTRIES), F32)], axis=0)
        colour_hi = colours.astype(BF16).astype(F32)
        colour_lo = (colours - colour_hi).astype(BF16).astype(F32)
        both = jnp.concatenate([colour_hi, colour_lo], axis=0)
        both = jnp.concatenate([both[:, :half], both[:, :half], both[:, half:], both[:, half:]], axis=1)
        product = dot_nt(both.astype(BF16), part[...])
        picture = product[0:8] + product[8:16]
        pictures[0, :, tile, :] = picture[0:3]
        residual = picture - jnp.concatenate([targets[0, :, tile, :], jnp.zeros((5, PIXELS), F32)], axis=0)
        residual_hi = residual.astype(BF16).astype(F32)
        residual_lo = (residual - residual_hi).astype(BF16).astype(F32)
        pair = jnp.concatenate([residual_hi, residual_lo], axis=0).astype(BF16)
        product = dot_nn(pair, part[...])
        product = product[0:8] + product[8:16]
        grads[pl.ds(6, 3), whole] = jnp.concatenate(
            [product[0:3, 0:256] + product[0:3, 256:512], product[0:3, 512:768] + product[0:3, 768:1024]], axis=1
        )
        stack = jnp.concatenate([residual_hi, residual_lo, residual_hi, jnp.zeros((104, PIXELS), F32)], axis=0)
        rows24 = jnp.concatenate([colour_hi, colour_hi, colour_lo, jnp.zeros((104, ENTRIES), F32)], axis=0)
        plane[...] = dot_nn(jnp.transpose(stack).astype(BF16), rows24.astype(BF16))

        for chunk in range(chunks):
            lanes = pl.ds(chunk * LANES, LANES)
            high, low = part_lanes(chunk)

            def one_share(y, carry):
                rows = pixels_of(y)
                value = plane[rows, lanes] * weight[rows, lanes]
                weight[rows, lanes] = value
                part[rows, high], part[rows, low] = split2(value)
                return carry

            lax.fori_loop(0, TILE_SIDE, one_share, 0, unroll=TILE_SIDE)

        plane[:, pl.ds(0, half)] = dot_nn(part[...], lower[...])
        plane[:, pl.ds(half, half)] = dot_nn(part[:, pl.ds(512, 512)], lower[pl.ds(0, 512), :])

        for chunk in range(chunks):
            lanes = pl.ds(chunk * LANES, LANES)
            screen_y = feature(1, chunk) - top_y

            def one_sum(y, carry):
                rows = pixels_of(y)
                sum_0, sum_1, sum_2 = carry
                delta_y = twice(screen_y - y.astype(F32))
                grad = weight[rows, lanes] - plane[rows, lanes] * ratio[rows, lanes]
                slope = grad * delta_y
                return sum_0 + grad, sum_1 + slope, sum_2 + slope * delta_y

            zero = jnp.zeros(shape, F32)
            sum_0, sum_1, sum_2 = lax.fori_loop(0, TILE_SIDE, one_sum, (zero, zero, zero), unroll=TILE_SIDE)
            delta_x = twice(feature(0, chunk)) - pixel_x
            over = lambda rows: jnp.sum(rows, axis=0, keepdims=True)
            first_x = over(delta_x * sum_0)
            first_y = over(sum_1)
            out = pl.ds(tile * ENTRIES + chunk * LANES, LANES)
            grads[pl.ds(0, 1), out] = -row_of(2, chunk) * first_x - row_of(3, chunk) * first_y
            grads[pl.ds(1, 1), out] = -row_of(4, chunk) * first_y - row_of(3, chunk) * first_x
            grads[pl.ds(2, 1), out] = -0.5 * over(delta_x * delta_x * sum_0)
            grads[pl.ds(3, 1), out] = -over(delta_x * sum_1)
            grads[pl.ds(4, 1), out] = -0.5 * over(sum_2)
            grads[pl.ds(5, 1), out] = over(sum_0)

    for n in range(TILES_DEV * chunks):
        spread(grads[:, pl.ds(n * LANES, LANES)], 16, masks, n * 256, left, n * LANES)
    total = dot_nt(left[...], right[...])
    for zc in range(16):
        slot_grads[zc] = total[16 * zc : 16 * zc + FEATS] + total[256 + 16 * zc : 256 + 16 * zc + FEATS]


Y_ARRIVAL = (0, 1, 7, 2, 6, 3, 5, 4)
ZC_ARRIVAL = (0, 1, 15, 2, 14, 3, 13, 4, 12, 5, 11, 6, 10, 7, 9, 8)
LAST = 7 * 256


def render_kernel(
    camera, tile_ids, tile_len, params_hbm, slots_hbm, lists_hbm, targets_hbm,
    pictures_hbm, gradient_hbm,
    params, packed, dense, lists, targets, pictures, slots, cams,
    table, outgoing, landed, staged, received, slot_grads, landed_back, staged_back, returned, every,
    feats, alpha, ratio, plane, weight, part, upper, lower, grads, masks, left, right,
    view_masks, view_left, view_right, view_grads, saved, shape_rows, totals, colour,
    load_sem, store_sem, send_y, recv_y, send_zc, recv_zc, send_zc2, recv_zc2, send_y2, recv_y2,
    send_slots, recv_slots, send_cams, recv_cams, send_view, recv_view,
):
    cell, view = lax.axis_index("cell"), lax.axis_index("view")
    my_y, my_zc = cell // ZC_DEVS, lax.rem(cell, ZC_DEVS)
    barrier, greetings = greet(my_y, my_zc, view)

    loads = [
        pltpu.make_async_copy(source, target, load_sem.at[i])
        for i, (source, target) in enumerate(
            (
                (params_hbm.at[pl.ds(0, 16)], params.at[pl.ds(0, 16)]),
                (params_hbm.at[pl.ds(16, ROWS - 16)], params.at[pl.ds(16, ROWS - 16)]),
                (slots_hbm, slots.at[0]),
                (lists_hbm, lists),
                (targets_hbm, targets),
            )
        )
    ]
    for load in loads:
        load.start()
    table[...] = jnp.zeros_like(table)
    feats[...] = jnp.zeros_like(feats)
    grads[...] = jnp.zeros_like(grads)
    shift_row = lax.broadcasted_iota(jnp.int32, (8, LANES), 0)
    cams[0] = jnp.where(shift_row == 0, camera[0, 0], jnp.where(shift_row == 1, camera[0, 1], camera[0, 2]))

    def unpack(first, last):
        for group in range(first, last, 8):
            size = min(8, last - group)
            for chunk in range(16):
                packed[pl.ds(group * 16 + chunk * 8, size), :] = params[
                    pl.ds(group, size), pl.ds(chunk * LANES, LANES)
                ]
        for row in range(first, last):
            for half in range(2):
                dense[2 * row + half] = packed[pl.ds((row // 8) * 128 + half * 8 + row % 8, 8, stride=16), :]

    def loader(half):
        return lambda row: dense[2 * row + half]

    loads[0].wait()
    unpack(0, 16)
    loads[1].wait()
    unpack(16, ROWS)

    for half in range(2):
        load = loader(half)
        matrix, scales, unit_q, inv_norm = shape_matrix([load(3 + i) for i in range(3)], [load(6 + i) for i in range(4)])
        for i, value in enumerate(matrix + scales + unit_q + [inv_norm]):
            shape_rows[half * SHAPE_ROWS + i] = value
        features = keep_view(load, [camera[0, i] for i in range(3)], matrix, saved, half * KEPT)
        for f, feature in enumerate(features):
            table[pl.ds(half * 16 + f, 8, stride=32), :] = feature

    loads[2].wait()
    pl.semaphore_wait(barrier, greetings)
    y_sends = {}
    for k in Y_ORDER + (0,):
        peer, device_id = y_peer(my_y, my_zc, k)
        for half in range(2):
            chunk = 2 * peer + half
            top, bottom = gather_chunk(table, slots[0, pl.ds(chunk, 1), :])
            outgoing[chunk, pl.ds(0, 8), :] = top
            outgoing[chunk, pl.ds(8, 1), :] = bottom[0:1]
        if k:
            y_sends[k] = remote(
                outgoing.at[pl.ds(2 * peer, 2)], landed.at[pl.ds(2 * my_y, 2)],
                send_y.at[k - 1], recv_y.at[k - 1], device_id,
            )
    landed[pl.ds(2 * my_y, 2)] = outgoing[pl.ds(2 * my_y, 2)]
    side_sends = []
    for k in VIEW_ORDER:
        peer = view_peer(view, k)
        side_sends.append(remote(slots.at[0], slots.at[k], send_slots.at[k - 1], recv_slots.at[k - 1], peer))
        side_sends.append(remote(cams.at[0], cams.at[k], send_cams.at[k - 1], recv_cams.at[k - 1], peer))

    fill_triangles(upper, lower)
    loads[3].wait()
    loads[4].wait()
    for tile in range(TILES_DEV):
        for chunk in range(ENTRIES // LANES):
            n = tile * (ENTRIES // LANES) + chunk
            high, low = entry_slot(lists, tile, chunk)
            fill_masks(high, 16, masks, n * 256)
            right[:, pl.ds(n * LANES, LANES)] = hot_rows(low, LANES)

    def view_factors(k):
        for p, step in enumerate(Y_ARRIVAL):
            for half in range(2):
                n = 2 * p + half
                index = slots[k, pl.ds(2 * lax.rem(my_y + Y_DEVS - step, Y_DEVS) + half, 1), :]
                fill_masks(index >> 8, 8, view_masks, (k * 16 + n) * 128)
                view_right[k, :, pl.ds(n * LANES, LANES)] = hot_rows(index & 255, 256)

    view_factors(0)
    for k in Y_ORDER:
        y_sends[k].wait()

    def to_zc(j, half, rows):
        staged[8 * half + j] = rows

    regroup(lambda i, half: landed[2 * i + half], to_zc)
    zc_sends = {}
    for k in ZC_ORDER:
        peer, device_id = zc_peer(my_y, my_zc, k)
        zc_sends[k] = remote(
            staged.at[peer], received.at[my_zc], send_zc.at[k - 1], recv_zc.at[k - 1], device_id
        )
    received[my_zc] = staged[my_zc]

    for copy in side_sends:
        copy.wait()
    for k in range(1, VIEW_DEVS):
        for half in range(2):
            shift = [jnp.broadcast_to(cams[k, pl.ds(i, 1), :], (8, LANES)) for i in range(3)]
            matrix = [shape_rows[half * SHAPE_ROWS + i] for i in range(9)]
            keep_view(loader(half), shift, matrix, saved, (2 * k + half) * KEPT)
        view_factors(k)

    places = [entry_slot(lists, n // 4, n % 4) for n in range(8)]
    places = [(jnp.broadcast_to(high, (8, LANES)), jnp.broadcast_to(low, (8, LANES))) for high, low in places]
    tops = [jnp.zeros((8, LANES), F32)] * 8
    bottoms = [jnp.zeros((8, LANES), F32)] * 8
    for k in ZC_ARRIVAL:
        if k:
            zc_sends[k].wait()
        source = lax.rem(my_zc + ZC_DEVS - k, ZC_DEVS)
        top = received[source, pl.ds(0, 8), :]
        bottom = jnp.broadcast_to(received[source, pl.ds(8, 1), :], (8, LANES))
        for n, (high, low) in enumerate(places):
            here = high == source
            tops[n] = jnp.where(here, lane_gather(top, low), tops[n])
            bottoms[n] = jnp.where(here, lane_gather(bottom, low), bottoms[n])
    for n in range(8):
        feats[pl.ds(0, 8), pl.ds(n * LANES, LANES)] = tops[n]
        feats[pl.ds(8, 8), pl.ds(n * LANES, LANES)] = bottoms[n]

    tile_body(
        tile_ids, tile_len, targets, pictures, slot_grads,
        feats, alpha, ratio, plane, weight, part, upper, lower, grads, masks, left, right,
    )
    store_pictures = pltpu.make_async_copy(pictures, pictures_hbm, store_sem.at[0])
    store_pictures.start()

    for k in ZC_ORDER:
        peer, device_id = zc_peer(my_y, my_zc, k)
        zc_sends[k] = remote(
            slot_grads.at[peer], landed_back.at[my_zc], send_zc2.at[k - 1], recv_zc2.at[k - 1], device_id
        )
    landed_back[my_zc] = slot_grads[my_zc]
    for k in ZC_ORDER[::-1]:
        zc_sends[k].wait()

    def to_y(j, half, rows):
        staged_back[2 * j + half] = rows

    regroup(lambda i, half: landed_back[8 * half + i], to_y)
    for k in Y_ORDER:
        peer, device_id = y_peer(my_y, my_zc, k)
        y_sends[k] = remote(
            staged_back.at[pl.ds(2 * peer, 2)], returned.at[pl.ds(2 * my_y, 2)],
            send_y2.at[k - 1], recv_y2.at[k - 1], device_id,
        )
    returned[pl.ds(2 * my_y, 2)] = staged_back[pl.ds(2 * my_y, 2)]

    def add_left(k, p, block):
        for half in range(2):
            n = 2 * p + half
            values = jnp.concatenate(
                [block(half, 0, 8), jnp.broadcast_to(block(half, 8, 1), (8, LANES))], axis=0
            )
            spread(values, 8, view_masks, (k * 16 + n) * 128, view_left.at[k], n * LANES)

    def scatter(k, columns, first):
        product = dot_nt(view_left[k, :, columns], view_right[k, :, columns])
        for half in range(2):
            lanes = slice(half * LANES, (half + 1) * LANES)
            rows = pl.ds((2 * k + half) * 128, 128)
            value = product[0:128, lanes] + product[128:256, lanes]
            view_grads[rows, :] = value if first else view_grads[rows, :] + value

    def pull(k):
        for half in range(2):
            matrix = [shape_rows[half * SHAPE_ROWS + i] for i in range(9)]
            slot = lambda f: view_grads[pl.ds((2 * k + half) * 128 + f, 8, stride=16), :]
            pull_view(
                loader(half), slot, matrix, saved, (2 * k + half) * KEPT, totals, half * 13, k == 0,
                colour, (2 * k + half) * 3,
            )

    view_sends = {}
    for p, step in enumerate(Y_ARRIVAL):
        if step:
            y_sends[step].wait()
        y = lax.rem(my_y + Y_DEVS - step, Y_DEVS)
        for k in VIEW_ORDER:
            view_sends[k, p] = remote(
                returned.at[pl.ds(2 * y, 2)], every.at[k, pl.ds(2 * p, 2)],
                send_view.at[k - 1, p], recv_view.at[k - 1, p], view_peer(view, k),
            )
        add_left(0, p, lambda half, row, size, y=y: returned[2 * y + half, pl.ds(row, size), :])
    scatter(0, pl.ds(0, G_DEV), True)
    pull(0)
    for p in range(8):
        for k in (1, 3, 2):
            view_sends[k, p].wait()
            add_left(k, p, lambda half, row, size: every[k, 2 * p + half, pl.ds(row, size), :])
            if p == 6:
                scatter(k, pl.ds(0, LAST), True)
            if p == 7:
                scatter(k, pl.ds(LAST, 256), False)
                pull(k)

    def put(row, half, value):
        packed[pl.ds((row // 8) * 128 + half * 8 + row % 8, 8, stride=16), :] = value

    def pack(first, last):
        for group in range(first, last, 8):
            size = min(8, last - group)
            for chunk in range(16):
                params[pl.ds(group, size), pl.ds(chunk * LANES, LANES)] = packed[
                    pl.ds(group * 16 + chunk * 8, size), :
                ]

    for half in range(2):
        kept = lambda k, i: saved[(2 * k + half) * KEPT + i]
        for channel in range(3):
            parts = [colour[(2 * k + half) * 3 + channel] for k in range(VIEW_DEVS)]
            put(11 + 16 * channel, half, sh_first * (parts[0] + parts[1] + parts[2] + parts[3]))
            for j in range(15):
                terms = [kept(k, 22 + j) * parts[k] for k in range(VIEW_DEVS)]
                put(12 + 16 * channel + j, half, terms[0] + terms[1] + terms[2] + terms[3])
    pack(16, ROWS)
    store_tail = pltpu.make_async_copy(
        params.at[pl.ds(16, ROWS - 16)], gradient_hbm.at[pl.ds(16, ROWS - 16)], store_sem.at[1]
    )
    store_tail.start()
    for half in range(2):
        total = [totals[half * 13 + i] for i in range(13)]
        shape = [shape_rows[half * SHAPE_ROWS + i] for i in range(SHAPE_ROWS)]
        matrix, scales, unit_q, inv_norm = shape[0:9], shape[9:12], shape[12:16], shape[16]
        for i in range(3):
            put(i, half, total[i])
            put(3 + i, half, sum(total[3 + 3 * r + i] * matrix[3 * r + i] for r in range(1, 3)) + total[3 + i] * matrix[i])
        _, pull_back = jax.vjp(rotation_of, *unit_q)
        g_unit = pull_back([total[3 + 3 * i + j] * scales[j] for i in range(3) for j in range(3)])
        along = unit_q[0] * g_unit[0] + unit_q[1] * g_unit[1] + unit_q[2] * g_unit[2] + unit_q[3] * g_unit[3]
        for i in range(4):
            put(6 + i, half, inv_norm * (g_unit[i] - unit_q[i] * along))
        put(10, half, total[12] * (1.0 / (1.0 + jnp.exp(dense[20 + half]))))
    pack(0, 16)
    store_head = pltpu.make_async_copy(params.at[pl.ds(0, 16)], gradient_hbm.at[pl.ds(0, 16)], store_sem.at[2])
    store_head.start()
    store_pictures.wait()
    store_tail.wait()
    store_head.wait()


def render_call(camera, tile_ids, tile_len, params, slots, lists, targets):
    smem = pl.BlockSpec(memory_space=pltpu.SMEM)
    anywhere = pl.BlockSpec(memory_space=pl.ANY)
    plane = pltpu.VMEM((PIXELS, ENTRIES), F32)
    blocks = pltpu.VMEM((16, FEATS, LANES), F32)
    tile = (8, LANES)
    y_sems = [pltpu.SemaphoreType.DMA((Y_DEVS - 1,))] * 2
    zc_sems = [pltpu.SemaphoreType.DMA((ZC_DEVS - 1,))] * 2
    view_sems = [pltpu.SemaphoreType.DMA((VIEW_DEVS - 1,))] * 2
    return pl.pallas_call(
        render_kernel,
        out_shape=(
            jax.ShapeDtypeStruct(targets.shape, F32),
            jax.ShapeDtypeStruct(params.shape, F32),
        ),
        in_specs=[smem, smem, smem, anywhere, anywhere, anywhere, anywhere],
        out_specs=(anywhere, anywhere),
        scratch_shapes=[
            pltpu.VMEM((ROWS, G_DEV), F32),
            pltpu.VMEM((64 * 16, LANES), F32),
            pltpu.VMEM((2 * ROWS,) + tile, F32),
            pltpu.VMEM(lists.shape, jnp.int32),
            pltpu.VMEM(targets.shape, F32),
            pltpu.VMEM(targets.shape, F32),
            pltpu.VMEM((VIEW_DEVS, 16, LANES), jnp.int32),
            pltpu.VMEM((VIEW_DEVS,) + tile, F32),
            pltpu.VMEM((256, LANES), F32),
        ]
        + [blocks] * 8
        + [
            pltpu.VMEM((VIEW_DEVS, 16, FEATS, LANES), F32),
            pltpu.VMEM((16, TILES_DEV * ENTRIES), F32),
            plane,
            plane,
            plane,
            plane,
            pltpu.VMEM((PIXELS, 2 * ENTRIES), BF16),
            pltpu.VMEM((1024, 256), BF16),
            pltpu.VMEM((1024, 256), BF16),
            pltpu.VMEM((16, TILES_DEV * ENTRIES), F32),
            pltpu.VMEM((8 * 256, LANES), BF16),
            pltpu.VMEM((512, TILES_DEV * ENTRIES), BF16),
            pltpu.VMEM((LANES, TILES_DEV * ENTRIES), BF16),
            pltpu.VMEM((VIEW_DEVS * 16 * 128, LANES), BF16),
            pltpu.VMEM((VIEW_DEVS, 256, G_DEV), BF16),
            pltpu.VMEM((VIEW_DEVS, 256, G_DEV), BF16),
            pltpu.VMEM((VIEW_DEVS * 256, LANES), F32),
            pltpu.VMEM((VIEW_DEVS * 2 * KEPT,) + tile, F32),
            pltpu.VMEM((2 * SHAPE_ROWS,) + tile, F32),
            pltpu.VMEM((2 * 13,) + tile, F32),
            pltpu.VMEM((VIEW_DEVS * 2 * 3,) + tile, F32),
            pltpu.SemaphoreType.DMA((5,)),
            pltpu.SemaphoreType.DMA((3,)),
        ]
        + y_sems + zc_sems + zc_sems + y_sems + view_sems + view_sems
        + [pltpu.SemaphoreType.DMA((VIEW_DEVS - 1, 8))] * 2,
        compiler_params=pltpu.CompilerParams(
            collective_id=0, has_side_effects=True, vmem_limit_bytes=58 * 2**20
        ),
        name="render",
    )(camera, tile_ids, tile_len, params, slots, lists, targets)


def local(params, cameras, targets, tile_ids, send_slots, tile_lists, tile_len):
    pictures, gradient = render_call(
        cameras, tile_ids, tile_len, params, send_slots.reshape(16, LANES), tile_lists,
        jnp.transpose(targets, (0, 2, 1, 3)),
    )
    return jnp.transpose(pictures, (0, 2, 1, 3)), gradient


def solution(mesh):
    return jax.shard_map(
        local,
        mesh=mesh,
        in_specs=(
            P(None, "cell"),
            P("view", None),
            P("view", "cell", None, None),
            P("view", "cell"),
            P("view", "cell", None),
            P("view", "cell", None),
            P("view", "cell"),
        ),
        out_specs=(P("view", "cell", None, None), P(None, "cell")),
        check_vma=False,
    )
```

```python
import jax
import jax.numpy as jnp
from jax import lax
from jax.experimental import pallas as pl
from jax.experimental.pallas import tpu as pltpu
from jax.sharding import PartitionSpec as P

TILE_SIDE = 16
TILE_COLS = 32
LANES = 128
Y_DEVS = 8
ZC_DEVS = 16
VIEW_DEVS = 4
FEATS = 9
Y_ORDER = (4, 3, 5, 2, 6, 1, 7)
ZC_ORDER = (8, 9, 7, 6, 10, 5, 11, 4, 12, 3, 13, 2, 14, 1, 15)
VIEW_ORDER = (2, 1, 3)
ENTRIES = 512
CHUNKS = ENTRIES // LANES
HALF = ENTRIES // 2
TILES_DEV = 2
PIXELS = 256
ROWS = 59
G_DEV = 2048
LOG2_E = 1.4426950408889634
F32 = jnp.float32
BF16 = jnp.bfloat16

focal_length = 800.0
dilation = 0.3
sh_first = 0.28209479177387814
sh_second = 0.4886025119029199
sh_third = (
    1.0925484305920792,
    -1.0925484305920792,
    0.31539156525252005,
    -1.0925484305920792,
    0.5462742152960396,
)
sh_fourth = (
    -0.5900435899266435,
    2.890611442640554,
    -0.4570457994644658,
    0.3731763325901154,
    -0.4570457994644658,
    1.445305721320277,
    -0.5900435899266435,
)


def split2(value):
    high = value.astype(BF16)
    return high, (value - high.astype(F32)).astype(BF16)


def dot_nt(lhs, rhs):
    return lax.dot_general(lhs, rhs, (((1,), (1,)), ((), ())), preferred_element_type=F32)


def dot_nn(lhs, rhs):
    return lax.dot_general(lhs, rhs, (((1,), (0,)), ((), ())), preferred_element_type=F32)


def rotation_of(q_w, q_x, q_y, q_z):
    return [
        1.0 - 2.0 * (q_y * q_y + q_z * q_z),
        2.0 * (q_x * q_y - q_w * q_z),
        2.0 * (q_x * q_z + q_w * q_y),
        2.0 * (q_x * q_y + q_w * q_z),
        1.0 - 2.0 * (q_x * q_x + q_z * q_z),
        2.0 * (q_y * q_z - q_w * q_x),
        2.0 * (q_x * q_z - q_w * q_y),
        2.0 * (q_y * q_z + q_w * q_x),
        1.0 - 2.0 * (q_x * q_x + q_y * q_y),
    ]


def unit_quaternion(quaternion):
    total = sum(part * part for part in quaternion[1:]) + quaternion[0] * quaternion[0]
    inverse = lax.rsqrt(total)
    return [part * inverse for part in quaternion], inverse


def shape_matrix(log_scales, quaternion):
    scales = [jnp.exp(part) for part in log_scales]
    unit, inverse = unit_quaternion(quaternion)
    rotation = rotation_of(*unit)
    matrix = [rotation[3 * i + j] * scales[j] for i in range(3) for j in range(3)]
    return matrix, scales, unit, inverse


def harmonics(x, y, z):
    xx, yy, zz = x * x, y * y, z * z
    rim = 4.0 * zz - xx - yy
    gap = xx - yy
    return [
        -sh_second * y,
        sh_second * z,
        -sh_second * x,
        sh_third[0] * (x * y),
        sh_third[1] * (y * z),
        sh_third[2] * (2.0 * zz - xx - yy),
        sh_third[3] * (x * z),
        sh_third[4] * gap,
        sh_fourth[0] * (y * (3.0 * xx - yy)),
        sh_fourth[1] * (x * y * z),
        sh_fourth[2] * (y * rim),
        sh_fourth[3] * (z * (2.0 * zz - 3.0 * xx - 3.0 * yy)),
        sh_fourth[4] * (x * rim),
        sh_fourth[5] * (z * gap),
        sh_fourth[6] * (x * (xx - 3.0 * yy)),
    ]


def geometry(pos, matrix):
    x, y, z = pos
    inv_z = 1.0 / z
    jac = focal_length * inv_z
    screen_x = x * jac
    screen_y = y * jac
    jac_x = -screen_x * inv_z
    jac_y = -screen_y * inv_z
    row_u = [jac * matrix[j] + jac_x * matrix[6 + j] for j in range(3)]
    row_v = [jac * matrix[3 + j] + jac_y * matrix[6 + j] for j in range(3)]
    cov_a = row_u[0] * row_u[0] + row_u[1] * row_u[1] + row_u[2] * row_u[2] + dilation
    cov_c = row_v[0] * row_v[0] + row_v[1] * row_v[1] + row_v[2] * row_v[2] + dilation
    cov_b = row_u[0] * row_v[0] + row_u[1] * row_v[1] + row_u[2] * row_v[2]
    inv_det = 1.0 / (cov_a * cov_c - cov_b * cov_b)
    return inv_z, jac, screen_x, screen_y, jac_x, jac_y, row_u, row_v, cov_a, cov_b, cov_c, inv_det


def direction(pos):
    x, y, z = pos
    inverse = lax.rsqrt(x * x + y * y + z * z)
    return [x * inverse, y * inverse, z * inverse], inverse


def raw_colour(load, channel, basis):
    total = load(11 + 16 * channel) * sh_first
    for j in range(15):
        total = total + load(12 + 16 * channel + j) * basis[j]
    return total + 0.5


KEPT = 40
SHAPE_ROWS = 17


def keep_view(load, shift, matrix, saved, base):
    pos = [load(i) - shift[i] for i in range(3)]
    inv_z, jac, screen_x, screen_y, jac_x, jac_y, row_u, row_v, cov_a, cov_b, cov_c, inv_det = geometry(pos, matrix)
    unit, inv_len = direction(pos)
    basis = harmonics(*unit)
    raw = [raw_colour(load, channel, basis) for channel in range(3)]
    gates = [jnp.where(value > 0.0, 1.0, jnp.where(value < 0.0, 0.0, 0.5)) for value in raw]
    values = [pos[0], pos[1], inv_z, jac, screen_x, screen_y, jac_x, jac_y]
    values += row_u + row_v + [cov_a, cov_b, cov_c, inv_det] + unit + [inv_len] + basis + gates
    for i, value in enumerate(values):
        saved[base + i] = value
    features = [screen_x, screen_y, cov_c * inv_det, -cov_b * inv_det, cov_a * inv_det]
    features.append(1.0 / (1.0 + jnp.exp(-load(10))))
    return features + [jnp.maximum(value, 0.0) for value in raw]


def pull_view(load, slot, matrix, saved, base, totals, total_base, first, colour, colour_base):
    kept = lambda i: saved[base + i]
    inv_z, jac, screen_x, screen_y, jac_x, jac_y = [kept(2 + i) for i in range(6)]
    row_u, row_v = [kept(8 + i) for i in range(3)], [kept(11 + i) for i in range(3)]
    cov_a, cov_b, cov_c, inv_det = [kept(14 + i) for i in range(4)]
    g_a, g_b, g_c = slot(2), slot(3), slot(4)
    g_det = -(g_a * cov_c - g_b * cov_b + g_c * cov_a) * inv_det * inv_det
    d_a = 2.0 * (g_c * inv_det + g_det * cov_c)
    d_c = 2.0 * (g_a * inv_det + g_det * cov_a)
    d_b = -g_b * inv_det - 2.0 * g_det * cov_b
    g_u = [d_a * row_u[j] + d_b * row_v[j] for j in range(3)]
    g_v = [d_c * row_v[j] + d_b * row_u[j] for j in range(3)]
    g_matrix = [jac * g_u[j] for j in range(3)] + [jac * g_v[j] for j in range(3)]
    g_matrix += [jac_x * g_u[j] + jac_y * g_v[j] for j in range(3)]
    g_jac = sum(g_u[j] * matrix[j] + g_v[j] * matrix[3 + j] for j in range(1, 3)) + (
        g_u[0] * matrix[0] + g_v[0] * matrix[3]
    )
    g_jac_x = g_u[0] * matrix[6] + g_u[1] * matrix[7] + g_u[2] * matrix[8]
    g_jac_y = g_v[0] * matrix[6] + g_v[1] * matrix[7] + g_v[2] * matrix[8]
    g_sx = slot(0) - inv_z * g_jac_x
    g_sy = slot(1) - inv_z * g_jac_y
    g_inv = focal_length * (g_jac + kept(0) * g_sx + kept(1) * g_sy) - screen_x * g_jac_x - screen_y * g_jac_y
    g_pos = [jac * g_sx, jac * g_sy, -inv_z * inv_z * g_inv]

    g_basis = None
    for channel in range(3):
        g_colour = slot(6 + channel) * kept(37 + channel)
        colour[colour_base + channel] = g_colour
        terms = [load(12 + 16 * channel + j) * g_colour for j in range(15)]
        g_basis = terms if g_basis is None else [a + b for a, b in zip(g_basis, terms)]
    unit, inv_len = [kept(18 + i) for i in range(3)], kept(21)
    _, pull = jax.vjp(harmonics, *unit)
    g_unit = pull(g_basis)
    along = unit[0] * g_unit[0] + unit[1] * g_unit[1] + unit[2] * g_unit[2]
    for i in range(3):
        g_pos[i] = g_pos[i] + inv_len * (g_unit[i] - unit[i] * along)
    for i, value in enumerate(g_pos + g_matrix + [slot(5)]):
        totals[total_base + i] = value if first else totals[total_base + i] + value


def lane_gather(source, index):
    return jnp.take_along_axis(source, index, axis=1, mode="promise_in_bounds")


def gather_chunk(table, index):
    shape = (8, LANES)
    low = jnp.broadcast_to(index & 127, shape)
    high = jnp.broadcast_to(index >> 7, shape)
    top = bottom = jnp.zeros(shape, F32)
    for chunk in range(16):
        here = high == chunk
        top = jnp.where(here, lane_gather(table[pl.ds(16 * chunk, 8), :], low), top)
        bottom = jnp.where(here, lane_gather(table[pl.ds(16 * chunk + 8, 8), :], low), bottom)
    return top, bottom


def block_transpose(rows):
    group = lax.broadcasted_iota(jnp.int32, rows[0].shape, 1) // 16
    for step in (1, 2, 4):
        odd = (group & step) != 0
        fresh = list(rows)
        for i in range(8):
            if i & step:
                continue
            first, second = rows[i], rows[i + step]
            fresh[i] = jnp.where(odd, pltpu.roll(second, 16 * step, 1), first)
            fresh[i + step] = jnp.where(odd, second, pltpu.roll(first, LANES - 16 * step, 1))
        rows = fresh
    return rows


def remote(src_ref, dst_ref, send_sem, recv_sem, device_id):
    copy = pltpu.make_async_remote_copy(
        src_ref=src_ref,
        dst_ref=dst_ref,
        send_sem=send_sem,
        recv_sem=recv_sem,
        device_id=device_id,
        device_id_type=pl.DeviceIdType.MESH,
    )
    copy.start()
    return copy


def y_peer(my_y, my_zc, k):
    peer = lax.rem(my_y + k, Y_DEVS)
    return peer, {"cell": peer * ZC_DEVS + my_zc}


def zc_peer(my_y, my_zc, k):
    peer = lax.rem(my_zc + k, ZC_DEVS)
    return peer, {"cell": my_y * ZC_DEVS + peer}


def view_peer(view, k):
    return {"view": lax.rem(view + k, VIEW_DEVS)}


def greet(my_y, my_zc, view):
    barrier = pltpu.get_barrier_semaphore()
    peers = [y_peer(my_y, my_zc, k)[1] for k in Y_ORDER]
    peers += [zc_peer(my_y, my_zc, k)[1] for k in ZC_ORDER]
    peers += [view_peer(view, k) for k in VIEW_ORDER]
    for peer in peers:
        pl.semaphore_signal(barrier, inc=1, device_id=peer, device_id_type=pl.DeviceIdType.MESH)
    return barrier, len(peers)


def regroup(load, store):
    for half in range(2):
        for j, rows in enumerate(block_transpose([load(i, half) for i in range(8)])):
            store(j, half, rows)


def part_lanes(chunk):
    base = (chunk // 2) * 512 + (chunk % 2) * LANES
    return pl.ds(base, LANES), pl.ds(base + 256, LANES)


def fill_triangles(upper, lower):
    row = lax.broadcasted_iota(jnp.int32, (256, 256), 0)
    col = lax.broadcasted_iota(jnp.int32, (256, 256), 1)
    above = jnp.where(row < col, 1.0, 0.0).astype(BF16)
    below = jnp.where(row > col, 1.0, 0.0).astype(BF16)
    ones = jnp.ones((256, 256), BF16)
    for i in range(4):
        upper[pl.ds(256 * i, 256), :] = ones if i < 2 else above
        lower[pl.ds(256 * i, 256), :] = below if i < 2 else ones


def entry_slot(lists, tile, chunk):
    index = lists[0, pl.ds(tile, 1), pl.ds(chunk * LANES, LANES)]
    return (index >> 4) & 15, ((index >> 8) << 4) | (index & 15)


def hot_rows(index, count):
    shape = (count, LANES)
    return jnp.where(
        jnp.broadcast_to(index, shape) == lax.broadcasted_iota(jnp.int32, shape, 0), 1.0, 0.0
    ).astype(BF16)


def fill_masks(high, count, masks, base):
    high = jnp.broadcast_to(high, (16, LANES))
    for value in range(count):
        masks[pl.ds(base + 16 * value, 16), :] = jnp.where(high == value, 1.0, 0.0).astype(BF16)


def spread(values, count, masks, base, left, column):
    for i, piece in enumerate(split2(values)):
        for value in range(count):
            left[pl.ds((i * count + value) * 16, 16), pl.ds(column, LANES)] = (
                masks[pl.ds(base + 16 * value, 16), :] * piece
            )


class Tile:
    def __init__(self, tile, number, length, feats, grads, alpha, ratio, plane, weight, part):
        self.tile, self.length, self.feats, self.grads = tile, length, feats, grads
        self.alpha, self.ratio, self.plane, self.weight, self.part = alpha, ratio, plane, weight, part
        self.whole = pl.ds(tile * ENTRIES, ENTRIES)
        left_x = (TILE_SIDE * lax.rem(number, TILE_COLS)).astype(F32) + 0.5
        self.top_y = (TILE_SIDE * (number // TILE_COLS)).astype(F32) + 0.5
        self.pixel_x = lax.broadcasted_iota(jnp.int32, (TILE_SIDE, LANES), 0).astype(F32) + left_x

    def row_of(self, f, chunk):
        return self.feats[pl.ds(f, 1), pl.ds(self.tile * ENTRIES + chunk * LANES, LANES)]

    def feature(self, f, chunk):
        return jnp.broadcast_to(self.row_of(f, chunk), (8, LANES))

    def each_row(self, body, carry):
        def one_row(y, carry):
            rows = pl.ds(pl.multiple_of(y * TILE_SIDE, TILE_SIDE), TILE_SIDE)
            return body(y.astype(F32), rows, carry)

        return lax.fori_loop(0, TILE_SIDE, one_row, carry, unroll=TILE_SIDE)

    def opacities(self):
        for chunk in range(CHUNKS):
            lanes = pl.ds(chunk * LANES, LANES)
            high, low = part_lanes(chunk)
            lane = lax.broadcasted_iota(jnp.int32, (8, LANES), 1) + chunk * LANES
            log_opacity = jnp.where(lane < self.length, jnp.log2(self.feature(5, chunk)), -1e30)
            delta_x = twice(self.feature(0, chunk)) - self.pixel_x
            part_x = twice((-0.5 * LOG2_E) * self.feature(2, chunk)) * delta_x * delta_x + twice(log_opacity)
            cross = twice(-LOG2_E * self.feature(3, chunk)) * delta_x
            screen_y = self.feature(1, chunk) - self.top_y
            conic_c = (-0.5 * LOG2_E) * self.feature(4, chunk)

            def body(y, rows, carry):
                delta_y = screen_y - y
                part_y = conic_c * delta_y * delta_y
                value = jnp.exp2(part_x + cross * twice(delta_y) + twice(part_y))
                keep = jnp.log2(1.0 - value)
                self.alpha[rows, lanes] = value
                self.ratio[rows, lanes] = value * jnp.exp2(-keep)
                self.part[rows, high], self.part[rows, low] = split2(keep)
                return carry

            self.each_row(body, 0)

    def log_transmittance(self, upper):
        self.plane[:, pl.ds(0, HALF)] = dot_nn(self.part[:, pl.ds(0, 512)], upper[pl.ds(512, 512), :])
        self.plane[:, pl.ds(HALF, HALF)] = dot_nn(self.part[...], upper[...])

    def weights(self):
        for chunk in range(CHUNKS):
            lanes = pl.ds(chunk * LANES, LANES)
            high, low = part_lanes(chunk)

            def body(y, rows, carry):
                value = jnp.exp2(self.plane[rows, lanes]) * self.alpha[rows, lanes]
                self.weight[rows, lanes] = value
                self.part[rows, high], self.part[rows, low] = split2(value)
                return carry

            self.each_row(body, 0)

    def picture(self, targets, pictures):
        colours = jnp.concatenate([self.feats[pl.ds(6, 3), self.whole], jnp.zeros((5, ENTRIES), F32)], axis=0)
        colour_hi = colours.astype(BF16).astype(F32)
        colour_lo = (colours - colour_hi).astype(BF16).astype(F32)
        both = jnp.concatenate([colour_hi, colour_lo], axis=0)
        both = jnp.concatenate([both[:, :HALF], both[:, :HALF], both[:, HALF:], both[:, HALF:]], axis=1)
        product = dot_nt(both.astype(BF16), self.part[...])
        picture = product[0:8] + product[8:16]
        pictures[0, :, self.tile, :] = picture[0:3]
        residual = picture - jnp.concatenate([targets[0, :, self.tile, :], jnp.zeros((5, PIXELS), F32)], axis=0)
        residual_hi = residual.astype(BF16).astype(F32)
        residual_lo = (residual - residual_hi).astype(BF16).astype(F32)
        pair = jnp.concatenate([residual_hi, residual_lo], axis=0).astype(BF16)
        product = dot_nn(pair, self.part[...])
        product = product[0:8] + product[8:16]
        self.grads[pl.ds(6, 3), self.whole] = jnp.concatenate(
            [product[0:3, 0:256] + product[0:3, 256:512], product[0:3, 512:768] + product[0:3, 768:1024]], axis=1
        )
        stack = jnp.concatenate([residual_hi, residual_lo, residual_hi, jnp.zeros((104, PIXELS), F32)], axis=0)
        rows24 = jnp.concatenate([colour_hi, colour_hi, colour_lo, jnp.zeros((104, ENTRIES), F32)], axis=0)
        self.plane[...] = dot_nn(jnp.transpose(stack).astype(BF16), rows24.astype(BF16))

    def shares(self):
        for chunk in range(CHUNKS):
            lanes = pl.ds(chunk * LANES, LANES)
            high, low = part_lanes(chunk)

            def body(y, rows, carry):
                value = self.plane[rows, lanes] * self.weight[rows, lanes]
                self.weight[rows, lanes] = value
                self.part[rows, high], self.part[rows, low] = split2(value)
                return carry

            self.each_row(body, 0)

    def later_shares(self, lower):
        self.plane[:, pl.ds(0, HALF)] = dot_nn(self.part[...], lower[...])
        self.plane[:, pl.ds(HALF, HALF)] = dot_nn(self.part[:, pl.ds(512, 512)], lower[pl.ds(0, 512), :])

    def sums(self):
        for chunk in range(CHUNKS):
            lanes = pl.ds(chunk * LANES, LANES)
            screen_y = self.feature(1, chunk) - self.top_y

            def body(y, rows, carry):
                sum_0, sum_1, sum_2 = carry
                delta_y = twice(screen_y - y)
                grad = self.weight[rows, lanes] - self.plane[rows, lanes] * self.ratio[rows, lanes]
                slope = grad * delta_y
                return sum_0 + grad, sum_1 + slope, sum_2 + slope * delta_y

            zero = jnp.zeros((TILE_SIDE, LANES), F32)
            sum_0, sum_1, sum_2 = self.each_row(body, (zero, zero, zero))
            delta_x = twice(self.feature(0, chunk)) - self.pixel_x
            over = lambda rows: jnp.sum(rows, axis=0, keepdims=True)
            first_x = over(delta_x * sum_0)
            first_y = over(sum_1)
            out = pl.ds(self.tile * ENTRIES + chunk * LANES, LANES)
            grads, row_of = self.grads, lambda f: self.row_of(f, chunk)
            grads[pl.ds(0, 1), out] = -row_of(2) * first_x - row_of(3) * first_y
            grads[pl.ds(1, 1), out] = -row_of(4) * first_y - row_of(3) * first_x
            grads[pl.ds(2, 1), out] = -0.5 * over(delta_x * delta_x * sum_0)
            grads[pl.ds(3, 1), out] = -over(delta_x * sum_1)
            grads[pl.ds(4, 1), out] = -0.5 * over(sum_2)
            grads[pl.ds(5, 1), out] = over(sum_0)


def twice(rows):
    return jnp.concatenate([rows, rows], axis=0)


def tile_body(
    tile_ids, tile_len, targets, pictures, slot_grads, feats, planes, parts, upper, lower, grads, masks, left, right
):
    first, second = [
        Tile(
            tile, tile_ids[0, tile], tile_len[0, tile], feats, grads,
            *[planes.at[4 * tile + i] for i in range(4)], parts.at[tile],
        )
        for tile in range(TILES_DEV)
    ]
    first.opacities()
    second.opacities()
    for tile in (first, second):
        tile.log_transmittance(upper)
        tile.weights()
    for tile in (first, second):
        tile.picture(targets, pictures)
        tile.shares()
    for tile in (first, second):
        tile.later_shares(lower)
        tile.sums()
    for n in range(TILES_DEV * CHUNKS):
        spread(grads[:, pl.ds(n * LANES, LANES)], 16, masks, n * 256, left, n * LANES)
    total = dot_nt(left[...], right[...])
    for zc in range(16):
        slot_grads[zc] = total[16 * zc : 16 * zc + FEATS] + total[256 + 16 * zc : 256 + 16 * zc + FEATS]


Y_ARRIVAL = (0, 1, 7, 2, 6, 3, 5, 4)
ZC_ARRIVAL = (0, 1, 15, 2, 14, 3, 13, 4, 12, 5, 11, 6, 10, 7, 9, 8)
LAST = 7 * 256


def render_kernel(
    camera, tile_ids, tile_len, params_hbm, slots_hbm, lists_hbm, targets_hbm,
    pictures, gradient,
    params, packed, dense, lists, targets, slots, cams,
    table, outgoing, landed, staged, received, slot_grads, landed_back, staged_back, returned, every,
    feats, planes, parts, upper, lower, grads, masks, left, right,
    view_masks, view_left, view_right, view_grads, saved, shape_rows, totals, colour,
    load_sem, send_y, recv_y, send_zc, recv_zc, send_zc2, recv_zc2, send_y2, recv_y2,
    send_slots, recv_slots, send_cams, recv_cams, send_view, recv_view,
):
    cell, view = lax.axis_index("cell"), lax.axis_index("view")
    my_y, my_zc = cell // ZC_DEVS, lax.rem(cell, ZC_DEVS)
    barrier, greetings = greet(my_y, my_zc, view)

    pieces = [(first, min(8, ROWS - first)) for first in range(0, ROWS, 8)]
    loads = [
        pltpu.make_async_copy(params_hbm.at[pl.ds(*piece)], params.at[pl.ds(*piece)], load_sem.at[i])
        for i, piece in enumerate(pieces)
    ]
    side_loads = [
        pltpu.make_async_copy(source, target, load_sem.at[8 + i])
        for i, (source, target) in enumerate(
            ((slots_hbm, slots.at[0]), (lists_hbm, lists), (targets_hbm, targets))
        )
    ]
    for load in loads + side_loads:
        load.start()
    table[...] = jnp.zeros_like(table)
    feats[...] = jnp.zeros_like(feats)
    grads[...] = jnp.zeros_like(grads)
    shift_row = lax.broadcasted_iota(jnp.int32, (8, LANES), 0)
    cams[0] = jnp.where(shift_row == 0, camera[0, 0], jnp.where(shift_row == 1, camera[0, 1], camera[0, 2]))

    def unpack(group, size):
        for chunk in range(16):
            packed[pl.ds(group * 16 + chunk * 8, size), :] = params[pl.ds(group, size), pl.ds(chunk * LANES, LANES)]
        for row in range(group, group + size):
            for half in range(2):
                dense[2 * row + half] = packed[pl.ds((row // 8) * 128 + half * 8 + row % 8, 8, stride=16), :]

    def loader(half):
        return lambda row: dense[2 * row + half]

    for load, piece in zip(loads, pieces):
        load.wait()
        unpack(*piece)

    for half in range(2):
        load = loader(half)
        matrix, scales, unit_q, inv_norm = shape_matrix([load(3 + i) for i in range(3)], [load(6 + i) for i in range(4)])
        for i, value in enumerate(matrix + scales + unit_q + [inv_norm]):
            shape_rows[half * SHAPE_ROWS + i] = value
        features = keep_view(load, [camera[0, i] for i in range(3)], matrix, saved, half * KEPT)
        for f, feature in enumerate(features):
            table[pl.ds(half * 16 + f, 8, stride=32), :] = feature

    side_loads[0].wait()
    pl.semaphore_wait(barrier, greetings)
    y_sends = {}
    for k in Y_ORDER + (0,):
        peer, device_id = y_peer(my_y, my_zc, k)
        for half in range(2):
            chunk = 2 * peer + half
            top, bottom = gather_chunk(table, slots[0, pl.ds(chunk, 1), :])
            outgoing[chunk, pl.ds(0, 8), :] = top
            outgoing[chunk, pl.ds(8, 1), :] = bottom[0:1]
        if k:
            y_sends[k] = remote(
                outgoing.at[pl.ds(2 * peer, 2)], landed.at[pl.ds(2 * my_y, 2)],
                send_y.at[k - 1], recv_y.at[k - 1], device_id,
            )
    landed[pl.ds(2 * my_y, 2)] = outgoing[pl.ds(2 * my_y, 2)]
    side_sends = []
    for k in VIEW_ORDER:
        peer = view_peer(view, k)
        side_sends.append(remote(slots.at[0], slots.at[k], send_slots.at[k - 1], recv_slots.at[k - 1], peer))
        side_sends.append(remote(cams.at[0], cams.at[k], send_cams.at[k - 1], recv_cams.at[k - 1], peer))

    fill_triangles(upper, lower)
    side_loads[1].wait()
    side_loads[2].wait()
    for tile in range(TILES_DEV):
        for chunk in range(ENTRIES // LANES):
            n = tile * (ENTRIES // LANES) + chunk
            high, low = entry_slot(lists, tile, chunk)
            fill_masks(high, 16, masks, n * 256)
            right[:, pl.ds(n * LANES, LANES)] = hot_rows(low, LANES)

    def view_factors(k):
        for p, step in enumerate(Y_ARRIVAL):
            for half in range(2):
                n = 2 * p + half
                index = slots[k, pl.ds(2 * lax.rem(my_y + Y_DEVS - step, Y_DEVS) + half, 1), :]
                fill_masks(index >> 8, 8, view_masks, (k * 16 + n) * 128)
                view_right[k, :, pl.ds(n * LANES, LANES)] = hot_rows(index & 255, 256)

    for k in Y_ORDER[::-1]:
        y_sends[k].wait()

    def to_zc(j, half, rows):
        staged[8 * half + j] = rows

    regroup(lambda i, half: landed[2 * i + half], to_zc)
    zc_sends = {}
    for k in ZC_ORDER:
        peer, device_id = zc_peer(my_y, my_zc, k)
        zc_sends[k] = remote(
            staged.at[peer], received.at[my_zc], send_zc.at[k - 1], recv_zc.at[k - 1], device_id
        )
    received[my_zc] = staged[my_zc]

    view_factors(0)
    for copy in side_sends:
        copy.wait()

    def view_forward(k):
        for half in range(2):
            shift = [jnp.broadcast_to(cams[k, pl.ds(i, 1), :], (8, LANES)) for i in range(3)]
            matrix = [shape_rows[half * SHAPE_ROWS + i] for i in range(9)]
            keep_view(loader(half), shift, matrix, saved, (2 * k + half) * KEPT)
        view_factors(k)

    places = [entry_slot(lists, n // 4, n % 4) for n in range(8)]
    places = [(jnp.broadcast_to(high, (8, LANES)), jnp.broadcast_to(low, (8, LANES))) for high, low in places]
    tops = [jnp.zeros((8, LANES), F32)] * 8
    bottoms = [jnp.zeros((8, LANES), F32)] * 8
    for k in ZC_ARRIVAL:
        if k:
            zc_sends[k].wait()
        source = lax.rem(my_zc + ZC_DEVS - k, ZC_DEVS)
        top = received[source, pl.ds(0, 8), :]
        bottom = jnp.broadcast_to(received[source, pl.ds(8, 1), :], (8, LANES))
        for n, (high, low) in enumerate(places):
            here = high == source
            tops[n] = jnp.where(here, lane_gather(top, low), tops[n])
            bottoms[n] = jnp.where(here, lane_gather(bottom, low), bottoms[n])
    for n in range(8):
        feats[pl.ds(0, 8), pl.ds(n * LANES, LANES)] = tops[n]
        feats[pl.ds(8, 8), pl.ds(n * LANES, LANES)] = bottoms[n]

    tile_body(
        tile_ids, tile_len, targets, pictures, slot_grads,
        feats, planes, parts, upper, lower, grads, masks, left, right,
    )

    for k in ZC_ORDER:
        peer, device_id = zc_peer(my_y, my_zc, k)
        zc_sends[k] = remote(
            slot_grads.at[peer], landed_back.at[my_zc], send_zc2.at[k - 1], recv_zc2.at[k - 1], device_id
        )
    landed_back[my_zc] = slot_grads[my_zc]
    view_forward(1)
    view_forward(2)
    for k in ZC_ORDER[::-1]:
        zc_sends[k].wait()

    def to_y(j, half, rows):
        staged_back[2 * j + half] = rows

    regroup(lambda i, half: landed_back[8 * half + i], to_y)
    for k in Y_ORDER:
        peer, device_id = y_peer(my_y, my_zc, k)
        y_sends[k] = remote(
            staged_back.at[pl.ds(2 * peer, 2)], returned.at[pl.ds(2 * my_y, 2)],
            send_y2.at[k - 1], recv_y2.at[k - 1], device_id,
        )
    returned[pl.ds(2 * my_y, 2)] = staged_back[pl.ds(2 * my_y, 2)]

    def add_left(k, p, block):
        for half in range(2):
            n = 2 * p + half
            values = jnp.concatenate(
                [block(half, 0, 8), jnp.broadcast_to(block(half, 8, 1), (8, LANES))], axis=0
            )
            spread(values, 8, view_masks, (k * 16 + n) * 128, view_left.at[k], n * LANES)

    def scatter(k, columns, first):
        product = dot_nt(view_left[k, :, columns], view_right[k, :, columns])
        for half in range(2):
            lanes = slice(half * LANES, (half + 1) * LANES)
            rows = pl.ds((2 * k + half) * 128, 128)
            value = product[0:128, lanes] + product[128:256, lanes]
            view_grads[rows, :] = value if first else view_grads[rows, :] + value

    def pull(k):
        for half in range(2):
            matrix = [shape_rows[half * SHAPE_ROWS + i] for i in range(9)]
            slot = lambda f: view_grads[pl.ds((2 * k + half) * 128 + f, 8, stride=16), :]
            pull_view(
                loader(half), slot, matrix, saved, (2 * k + half) * KEPT, totals, half * 13, k == 0,
                colour, (2 * k + half) * 3,
            )

    view_sends = {}
    for p, step in enumerate(Y_ARRIVAL):
        if step:
            y_sends[step].wait()
        y = lax.rem(my_y + Y_DEVS - step, Y_DEVS)
        for k in VIEW_ORDER:
            view_sends[k, p] = remote(
                returned.at[pl.ds(2 * y, 2)], every.at[k, pl.ds(2 * p, 2)],
                send_view.at[k - 1, p], recv_view.at[k - 1, p], view_peer(view, k),
            )
        add_left(0, p, lambda half, row, size, y=y: returned[2 * y + half, pl.ds(row, size), :])
        if p == 0:
            view_forward(3)
    scatter(0, pl.ds(0, G_DEV), True)
    pull(0)
    for p in range(8):
        for k in (1, 3, 2):
            view_sends[k, p].wait()
            if p < 7:
                add_left(k, p, lambda half, row, size: every[k, 2 * p + half, pl.ds(row, size), :])
        if p == 6:
            for k in (1, 3, 2):
                scatter(k, pl.ds(0, LAST), True)
    for k in (1, 3, 2):
        add_left(k, 7, lambda half, row, size: every[k, 14 + half, pl.ds(row, size), :])
        scatter(k, pl.ds(LAST, 256), False)
        pull(k)

    def put(row, half, value):
        packed[pl.ds((row // 8) * 128 + half * 8 + row % 8, 8, stride=16), :] = value

    def pack(first, last):
        for group in range(first, last, 8):
            size = min(8, last - group)
            for chunk in range(16):
                gradient[pl.ds(group, size), pl.ds(chunk * LANES, LANES)] = packed[
                    pl.ds(group * 16 + chunk * 8, size), :
                ]

    for half in range(2):
        kept = lambda k, i: saved[(2 * k + half) * KEPT + i]
        for channel in range(3):
            parts = [colour[(2 * k + half) * 3 + channel] for k in range(VIEW_DEVS)]
            put(11 + 16 * channel, half, sh_first * (parts[0] + parts[1] + parts[2] + parts[3]))
            for j in range(15):
                terms = [kept(k, 22 + j) * parts[k] for k in range(VIEW_DEVS)]
                put(12 + 16 * channel + j, half, terms[0] + terms[1] + terms[2] + terms[3])
    pack(16, ROWS)
    for half in range(2):
        total = [totals[half * 13 + i] for i in range(13)]
        shape = [shape_rows[half * SHAPE_ROWS + i] for i in range(SHAPE_ROWS)]
        matrix, scales, unit_q, inv_norm = shape[0:9], shape[9:12], shape[12:16], shape[16]
        for i in range(3):
            put(i, half, total[i])
            put(3 + i, half, sum(total[3 + 3 * r + i] * matrix[3 * r + i] for r in range(1, 3)) + total[3 + i] * matrix[i])
        _, pull_back = jax.vjp(rotation_of, *unit_q)
        g_unit = pull_back([total[3 + 3 * i + j] * scales[j] for i in range(3) for j in range(3)])
        along = unit_q[0] * g_unit[0] + unit_q[1] * g_unit[1] + unit_q[2] * g_unit[2] + unit_q[3] * g_unit[3]
        for i in range(4):
            put(6 + i, half, inv_norm * (g_unit[i] - unit_q[i] * along))
        put(10, half, total[12] * (1.0 / (1.0 + jnp.exp(dense[20 + half]))))
    pack(0, 16)


def render_call(camera, tile_ids, tile_len, params, slots, lists, targets):
    smem = pl.BlockSpec(memory_space=pltpu.SMEM)
    anywhere = pl.BlockSpec(memory_space=pl.ANY)
    blocks = pltpu.VMEM((16, FEATS, LANES), F32)
    tile = (8, LANES)
    y_sems = [pltpu.SemaphoreType.DMA((Y_DEVS - 1,))] * 2
    zc_sems = [pltpu.SemaphoreType.DMA((ZC_DEVS - 1,))] * 2
    view_sems = [pltpu.SemaphoreType.DMA((VIEW_DEVS - 1,))] * 2
    return pl.pallas_call(
        render_kernel,
        out_shape=(
            pltpu.VMEM(targets.shape, F32),
            pltpu.VMEM(params.shape, F32),
        ),
        in_specs=[smem, smem, smem, anywhere, anywhere, anywhere, anywhere],
        out_specs=(pl.BlockSpec(memory_space=pltpu.VMEM), pl.BlockSpec(memory_space=pltpu.VMEM)),
        scratch_shapes=[
            pltpu.VMEM((ROWS, G_DEV), F32),
            pltpu.VMEM((64 * 16, LANES), F32),
            pltpu.VMEM((2 * ROWS,) + tile, F32),
            pltpu.VMEM(lists.shape, jnp.int32),
            pltpu.VMEM(targets.shape, F32),
            pltpu.VMEM((VIEW_DEVS, 16, LANES), jnp.int32),
            pltpu.VMEM((VIEW_DEVS,) + tile, F32),
            pltpu.VMEM((256, LANES), F32),
        ]
        + [blocks] * 8
        + [
            pltpu.VMEM((VIEW_DEVS, 16, FEATS, LANES), F32),
            pltpu.VMEM((16, TILES_DEV * ENTRIES), F32),
            pltpu.VMEM((4 * TILES_DEV, PIXELS, ENTRIES), F32),
            pltpu.VMEM((TILES_DEV, PIXELS, 2 * ENTRIES), BF16),
            pltpu.VMEM((1024, 256), BF16),
            pltpu.VMEM((1024, 256), BF16),
            pltpu.VMEM((16, TILES_DEV * ENTRIES), F32),
            pltpu.VMEM((8 * 256, LANES), BF16),
            pltpu.VMEM((512, TILES_DEV * ENTRIES), BF16),
            pltpu.VMEM((LANES, TILES_DEV * ENTRIES), BF16),
            pltpu.VMEM((VIEW_DEVS * 16 * 128, LANES), BF16),
            pltpu.VMEM((VIEW_DEVS, 256, G_DEV), BF16),
            pltpu.VMEM((VIEW_DEVS, 256, G_DEV), BF16),
            pltpu.VMEM((VIEW_DEVS * 256, LANES), F32),
            pltpu.VMEM((VIEW_DEVS * 2 * KEPT,) + tile, F32),
            pltpu.VMEM((2 * SHAPE_ROWS,) + tile, F32),
            pltpu.VMEM((2 * 13,) + tile, F32),
            pltpu.VMEM((VIEW_DEVS * 2 * 3,) + tile, F32),
            pltpu.SemaphoreType.DMA((11,)),
        ]
        + y_sems + zc_sems + zc_sems + y_sems + view_sems + view_sems
        + [pltpu.SemaphoreType.DMA((VIEW_DEVS - 1, 8))] * 2,
        compiler_params=pltpu.CompilerParams(
            collective_id=0, has_side_effects=True, vmem_limit_bytes=40 * 2**20
        ),
        name="render",
    )(
        *[
            pltpu.with_memory_space_constraint(operand, pltpu.HBM)
            for operand in (camera, tile_ids, tile_len, params, slots, lists, targets)
        ]
    )


def store_kernel(pictures, gradient, pictures_hbm, gradient_hbm, sems):
    copies = [pltpu.make_async_copy(pictures, pictures_hbm, sems.at[0])]
    for i, (first, size) in enumerate(((0, 16), (16, 16), (32, 16), (48, ROWS - 48))):
        rows = pl.ds(first, size)
        copies.append(pltpu.make_async_copy(gradient.at[rows], gradient_hbm.at[rows], sems.at[1 + i]))
    for copy in copies:
        copy.start()
    for copy in copies:
        copy.wait()


def store_call(pictures, gradient):
    vmem = pl.BlockSpec(memory_space=pltpu.VMEM)
    anywhere = pl.BlockSpec(memory_space=pl.ANY)
    return pl.pallas_call(
        store_kernel,
        out_shape=(jax.ShapeDtypeStruct(pictures.shape, F32), jax.ShapeDtypeStruct(gradient.shape, F32)),
        in_specs=[vmem, vmem],
        out_specs=(anywhere, anywhere),
        scratch_shapes=[pltpu.SemaphoreType.DMA((5,))],
        compiler_params=pltpu.CompilerParams(vmem_limit_bytes=8 * 2**20),
        name="store",
    )(pictures, gradient)


def local(params, cameras, targets, tile_ids, send_slots, tile_lists, tile_len):
    pictures, gradient = render_call(
        cameras, tile_ids, tile_len, params, send_slots.reshape(16, LANES), tile_lists,
        jnp.transpose(targets, (0, 2, 1, 3)),
    )
    pictures, gradient = store_call(pictures, gradient)
    return jnp.transpose(pictures, (0, 2, 1, 3)), gradient


def solution(mesh):
    return jax.shard_map(
        local,
        mesh=mesh,
        in_specs=(
            P(None, "cell"),
            P("view", None),
            P("view", "cell", None, None),
            P("view", "cell"),
            P("view", "cell", None),
            P("view", "cell", None),
            P("view", "cell"),
        ),
        out_specs=(P("view", "cell", None, None), P(None, "cell")),
        check_vma=False,
    )
```

```python
import jax
import jax.numpy as jnp
from jax import lax
from jax.experimental import pallas as pl
from jax.experimental.pallas import tpu as pltpu
from jax.sharding import PartitionSpec as P

TILE_SIDE = 16
TILE_COLS = 32
LANES = 128
Y_DEVS = 8
ZC_DEVS = 16
VIEW_DEVS = 4
FEATS = 9
Y_ORDER = (4, 3, 5, 2, 6, 1, 7)
ZC_ORDER = (8, 9, 7, 6, 10, 5, 11, 4, 12, 3, 13, 2, 14, 1, 15)
VIEW_ORDER = (2, 1, 3)
FAR_Y = 4
ENTRIES = 512
CHUNKS = ENTRIES // LANES
HALF = ENTRIES // 2
TILES_DEV = 2
PIXELS = 256
ROWS = 59
G_DEV = 2048
LOG2_E = 1.4426950408889634
F32 = jnp.float32
BF16 = jnp.bfloat16

focal_length = 800.0
dilation = 0.3
sh_first = 0.28209479177387814
sh_second = 0.4886025119029199
sh_third = (
    1.0925484305920792,
    -1.0925484305920792,
    0.31539156525252005,
    -1.0925484305920792,
    0.5462742152960396,
)
sh_fourth = (
    -0.5900435899266435,
    2.890611442640554,
    -0.4570457994644658,
    0.3731763325901154,
    -0.4570457994644658,
    1.445305721320277,
    -0.5900435899266435,
)


def split2(value):
    high = value.astype(BF16)
    return high, (value - high.astype(F32)).astype(BF16)


def dot_nt(lhs, rhs):
    return lax.dot_general(lhs, rhs, (((1,), (1,)), ((), ())), preferred_element_type=F32)


def dot_nn(lhs, rhs):
    return lax.dot_general(lhs, rhs, (((1,), (0,)), ((), ())), preferred_element_type=F32)


def rotation_of(q_w, q_x, q_y, q_z):
    return [
        1.0 - 2.0 * (q_y * q_y + q_z * q_z),
        2.0 * (q_x * q_y - q_w * q_z),
        2.0 * (q_x * q_z + q_w * q_y),
        2.0 * (q_x * q_y + q_w * q_z),
        1.0 - 2.0 * (q_x * q_x + q_z * q_z),
        2.0 * (q_y * q_z - q_w * q_x),
        2.0 * (q_x * q_z - q_w * q_y),
        2.0 * (q_y * q_z + q_w * q_x),
        1.0 - 2.0 * (q_x * q_x + q_y * q_y),
    ]


def unit_quaternion(quaternion):
    total = sum(part * part for part in quaternion[1:]) + quaternion[0] * quaternion[0]
    inverse = lax.rsqrt(total)
    return [part * inverse for part in quaternion], inverse


def shape_matrix(log_scales, quaternion):
    scales = [jnp.exp(part) for part in log_scales]
    unit, inverse = unit_quaternion(quaternion)
    rotation = rotation_of(*unit)
    matrix = [rotation[3 * i + j] * scales[j] for i in range(3) for j in range(3)]
    return matrix, scales, unit, inverse


def harmonics(x, y, z):
    xx, yy, zz = x * x, y * y, z * z
    rim = 4.0 * zz - xx - yy
    gap = xx - yy
    return [
        -sh_second * y,
        sh_second * z,
        -sh_second * x,
        sh_third[0] * (x * y),
        sh_third[1] * (y * z),
        sh_third[2] * (2.0 * zz - xx - yy),
        sh_third[3] * (x * z),
        sh_third[4] * gap,
        sh_fourth[0] * (y * (3.0 * xx - yy)),
        sh_fourth[1] * (x * y * z),
        sh_fourth[2] * (y * rim),
        sh_fourth[3] * (z * (2.0 * zz - 3.0 * xx - 3.0 * yy)),
        sh_fourth[4] * (x * rim),
        sh_fourth[5] * (z * gap),
        sh_fourth[6] * (x * (xx - 3.0 * yy)),
    ]


def geometry(pos, matrix):
    x, y, z = pos
    inv_z = 1.0 / z
    jac = focal_length * inv_z
    screen_x = x * jac
    screen_y = y * jac
    jac_x = -screen_x * inv_z
    jac_y = -screen_y * inv_z
    row_u = [jac * matrix[j] + jac_x * matrix[6 + j] for j in range(3)]
    row_v = [jac * matrix[3 + j] + jac_y * matrix[6 + j] for j in range(3)]
    cov_a = row_u[0] * row_u[0] + row_u[1] * row_u[1] + row_u[2] * row_u[2] + dilation
    cov_c = row_v[0] * row_v[0] + row_v[1] * row_v[1] + row_v[2] * row_v[2] + dilation
    cov_b = row_u[0] * row_v[0] + row_u[1] * row_v[1] + row_u[2] * row_v[2]
    inv_det = 1.0 / (cov_a * cov_c - cov_b * cov_b)
    return inv_z, jac, screen_x, screen_y, jac_x, jac_y, row_u, row_v, cov_a, cov_b, cov_c, inv_det


def direction(pos):
    x, y, z = pos
    inverse = lax.rsqrt(x * x + y * y + z * z)
    return [x * inverse, y * inverse, z * inverse], inverse


def raw_colour(load, channel, basis):
    total = load(11 + 16 * channel) * sh_first
    for j in range(15):
        total = total + load(12 + 16 * channel + j) * basis[j]
    return total + 0.5


KEPT = 40
SHAPE_ROWS = 17


def keep_geometry(load, shift, matrix, saved, base):
    pos = [load(i) - shift[i] for i in range(3)]
    inv_z, jac, screen_x, screen_y, jac_x, jac_y, row_u, row_v, cov_a, cov_b, cov_c, inv_det = geometry(pos, matrix)
    unit, inv_len = direction(pos)
    values = [pos[0], pos[1], inv_z, jac, screen_x, screen_y, jac_x, jac_y]
    values += row_u + row_v + [cov_a, cov_b, cov_c, inv_det] + unit + [inv_len] + harmonics(*unit)
    for i, value in enumerate(values):
        saved[base + i] = value
    opacity = 1.0 / (1.0 + jnp.exp(-load(10)))
    return [screen_x, screen_y, cov_c * inv_det, -cov_b * inv_det, cov_a * inv_det, opacity]


def keep_colours(load, saved, base):
    basis = [saved[base + 22 + j] for j in range(15)]
    raw = [raw_colour(load, channel, basis) for channel in range(3)]
    for channel, value in enumerate(raw):
        saved[base + 37 + channel] = jnp.where(value > 0.0, 1.0, jnp.where(value < 0.0, 0.0, 0.5))
    return [jnp.maximum(value, 0.0) for value in raw]


def pull_view(load, slot, matrix, saved, base):
    kept = lambda i: saved[base + i]
    inv_z, jac, screen_x, screen_y, jac_x, jac_y = [kept(2 + i) for i in range(6)]
    row_u, row_v = [kept(8 + i) for i in range(3)], [kept(11 + i) for i in range(3)]
    cov_a, cov_b, cov_c, inv_det = [kept(14 + i) for i in range(4)]
    g_a, g_b, g_c = slot(2), slot(3), slot(4)
    g_det = -(g_a * cov_c - g_b * cov_b + g_c * cov_a) * inv_det * inv_det
    d_a = 2.0 * (g_c * inv_det + g_det * cov_c)
    d_c = 2.0 * (g_a * inv_det + g_det * cov_a)
    d_b = -g_b * inv_det - 2.0 * g_det * cov_b
    g_u = [d_a * row_u[j] + d_b * row_v[j] for j in range(3)]
    g_v = [d_c * row_v[j] + d_b * row_u[j] for j in range(3)]
    g_matrix = [jac * g_u[j] for j in range(3)] + [jac * g_v[j] for j in range(3)]
    g_matrix += [jac_x * g_u[j] + jac_y * g_v[j] for j in range(3)]
    g_jac = g_u[0] * matrix[0] + g_v[0] * matrix[3]
    for j in (1, 2):
        g_jac = g_jac + (g_u[j] * matrix[j] + g_v[j] * matrix[3 + j])
    g_jac_x = g_u[0] * matrix[6] + g_u[1] * matrix[7] + g_u[2] * matrix[8]
    g_jac_y = g_v[0] * matrix[6] + g_v[1] * matrix[7] + g_v[2] * matrix[8]
    g_sx = slot(0) - inv_z * g_jac_x
    g_sy = slot(1) - inv_z * g_jac_y
    g_inv = focal_length * (g_jac + kept(0) * g_sx + kept(1) * g_sy) - screen_x * g_jac_x - screen_y * g_jac_y
    g_pos = [jac * g_sx, jac * g_sy, -inv_z * inv_z * g_inv]

    g_colours = [slot(6 + channel) * kept(37 + channel) for channel in range(3)]
    g_basis = []
    for j in range(15):
        terms = [load(12 + 16 * channel + j) * g_colours[channel] for channel in range(3)]
        g_basis.append(terms[0] + terms[1] + terms[2])
    unit, inv_len = [kept(18 + i) for i in range(3)], kept(21)
    _, pull = jax.vjp(harmonics, *unit)
    g_unit = pull(g_basis)
    along = unit[0] * g_unit[0] + unit[1] * g_unit[1] + unit[2] * g_unit[2]
    for i in range(3):
        g_pos[i] = g_pos[i] + inv_len * (g_unit[i] - unit[i] * along)
    return g_pos + g_matrix + [slot(5)], g_colours


def lane_gather(source, index):
    return jnp.take_along_axis(source, index, axis=1, mode="promise_in_bounds")


def gather_chunk(table, index):
    shape = (8, LANES)
    low = jnp.broadcast_to(index & 127, shape)
    high = jnp.broadcast_to(index >> 7, shape)
    top = bottom = jnp.zeros(shape, F32)
    for chunk in range(16):
        here = high == chunk
        top = jnp.where(here, lane_gather(table[pl.ds(16 * chunk, 8), :], low), top)
        bottom = jnp.where(here, lane_gather(table[pl.ds(16 * chunk + 8, 8), :], low), bottom)
    return top, bottom


def block_transpose(rows):
    group = lax.broadcasted_iota(jnp.int32, rows[0].shape, 1) // 16
    for step in (1, 2, 4):
        odd = (group & step) != 0
        fresh = list(rows)
        for i in range(8):
            if i & step:
                continue
            first, second = rows[i], rows[i + step]
            fresh[i] = jnp.where(odd, pltpu.roll(second, 16 * step, 1), first)
            fresh[i + step] = jnp.where(odd, second, pltpu.roll(first, LANES - 16 * step, 1))
        rows = fresh
    return rows


def remote(src_ref, dst_ref, send_sem, recv_sem, device_id):
    copy = pltpu.make_async_remote_copy(
        src_ref=src_ref,
        dst_ref=dst_ref,
        send_sem=send_sem,
        recv_sem=recv_sem,
        device_id=device_id,
        device_id_type=pl.DeviceIdType.MESH,
    )
    copy.start()
    return copy


def y_peer(my_y, my_zc, k):
    peer = lax.rem(my_y + k, Y_DEVS)
    return peer, {"cell": peer * ZC_DEVS + my_zc}


def zc_peer(my_y, my_zc, k):
    peer = lax.rem(my_zc + k, ZC_DEVS)
    return peer, {"cell": my_y * ZC_DEVS + peer}


def view_peer(view, k):
    return {"view": lax.rem(view + k, VIEW_DEVS)}


def far_view_peer(my_y, my_zc, view, k):
    return {**y_peer(my_y, my_zc, FAR_Y)[1], **view_peer(view, k)}


def greet(my_y, my_zc, view):
    barrier = pltpu.get_barrier_semaphore()
    peers = [y_peer(my_y, my_zc, k)[1] for k in Y_ORDER]
    peers += [zc_peer(my_y, my_zc, k)[1] for k in ZC_ORDER]
    peers += [view_peer(view, k) for k in VIEW_ORDER]
    peers += [far_view_peer(my_y, my_zc, view, k) for k in VIEW_ORDER]
    for peer in peers:
        pl.semaphore_signal(barrier, inc=1, device_id=peer, device_id_type=pl.DeviceIdType.MESH)
    return barrier, len(peers)


def regroup(load, store):
    for half in range(2):
        for j, rows in enumerate(block_transpose([load(i, half) for i in range(8)])):
            store(j, half, rows)


def part_lanes(chunk):
    base = (chunk // 2) * 512 + (chunk % 2) * LANES
    return pl.ds(base, LANES), pl.ds(base + 256, LANES)


def fill_triangles(upper, lower):
    row = lax.broadcasted_iota(jnp.int32, (256, 256), 0)
    col = lax.broadcasted_iota(jnp.int32, (256, 256), 1)
    above = jnp.where(row < col, 1.0, 0.0).astype(BF16)
    below = jnp.where(row > col, 1.0, 0.0).astype(BF16)
    ones = jnp.ones((256, 256), BF16)
    for i in range(4):
        upper[pl.ds(256 * i, 256), :] = ones if i < 2 else above
        lower[pl.ds(256 * i, 256), :] = below if i < 2 else ones


def entry_slot(lists, tile, chunk):
    index = lists[0, pl.ds(tile, 1), pl.ds(chunk * LANES, LANES)]
    return (index >> 4) & 15, ((index >> 8) << 4) | (index & 15)


def hot_rows(index, count):
    shape = (count, LANES)
    return jnp.where(
        jnp.broadcast_to(index, shape) == lax.broadcasted_iota(jnp.int32, shape, 0), 1.0, 0.0
    ).astype(BF16)


def fill_masks(high, count, masks, base):
    high = jnp.broadcast_to(high, (16, LANES))
    for value in range(count):
        masks[pl.ds(base + 16 * value, 16), :] = jnp.where(high == value, 1.0, 0.0).astype(BF16)


def spread(values, count, masks, base, left, column):
    for i, piece in enumerate(split2(values)):
        for value in range(count):
            left[pl.ds((i * count + value) * 16, 16), pl.ds(column, LANES)] = (
                masks[pl.ds(base + 16 * value, 16), :] * piece
            )


class Tile:
    def __init__(self, tile, number, length, feats, grads, alpha, ratio, plane, weight, part):
        self.tile, self.length, self.feats, self.grads = tile, length, feats, grads
        self.alpha, self.ratio, self.plane, self.weight, self.part = alpha, ratio, plane, weight, part
        self.whole = pl.ds(tile * ENTRIES, ENTRIES)
        left_x = twice((TILE_SIDE * (number & (TILE_COLS - 1))).astype(F32) + 0.5)
        self.top_y = (TILE_SIDE * (number >> 5)).astype(F32) + 0.5
        self.pixel_x = lax.broadcasted_iota(jnp.int32, (TILE_SIDE, LANES), 0).astype(F32) + left_x

    def row_of(self, f, chunk):
        return self.feats[pl.ds(f, 1), pl.ds(self.tile * ENTRIES + chunk * LANES, LANES)]

    def feature(self, f, chunk):
        return jnp.broadcast_to(self.row_of(f, chunk), (8, LANES))

    def each_row(self, body, carry):
        def one_row(y, carry):
            rows = pl.ds(pl.multiple_of(y * TILE_SIDE, TILE_SIDE), TILE_SIDE)
            return body(y.astype(F32), rows, carry)

        return lax.fori_loop(0, TILE_SIDE, one_row, carry, unroll=TILE_SIDE)

    def opacities(self):
        for chunk in range(CHUNKS):
            lanes = pl.ds(chunk * LANES, LANES)
            high, low = part_lanes(chunk)
            lane = lax.broadcasted_iota(jnp.int32, (8, LANES), 1) + chunk * LANES
            log_opacity = jnp.where(lane < self.length, jnp.log2(self.feature(5, chunk)), -1e30)
            delta_x = twice(self.feature(0, chunk)) - self.pixel_x
            part_x = twice((-0.5 * LOG2_E) * self.feature(2, chunk)) * delta_x * delta_x + twice(log_opacity)
            cross = twice(-LOG2_E * self.feature(3, chunk)) * delta_x
            screen_y = self.feature(1, chunk) - self.top_y
            conic_c = (-0.5 * LOG2_E) * self.feature(4, chunk)

            def body(y, rows, carry):
                delta_y = screen_y - y
                part_y = conic_c * delta_y * delta_y
                value = jnp.exp2(part_x + cross * twice(delta_y) + twice(part_y))
                keep = jnp.log2(1.0 - value)
                self.alpha[rows, lanes] = value
                self.ratio[rows, lanes] = value * jnp.exp2(-keep)
                self.part[rows, high], self.part[rows, low] = split2(keep)
                return carry

            self.each_row(body, 0)

    def log_transmittance(self, upper):
        self.plane[:, pl.ds(0, HALF)] = dot_nn(self.part[:, pl.ds(0, 512)], upper[pl.ds(512, 512), :])
        self.plane[:, pl.ds(HALF, HALF)] = dot_nn(self.part[...], upper[...])

    def weights(self):
        for chunk in range(CHUNKS):
            lanes = pl.ds(chunk * LANES, LANES)
            high, low = part_lanes(chunk)

            def body(y, rows, carry):
                value = jnp.exp2(self.plane[rows, lanes]) * self.alpha[rows, lanes]
                self.weight[rows, lanes] = value
                self.part[rows, high], self.part[rows, low] = split2(value)
                return carry

            self.each_row(body, 0)

    def picture(self, targets, pictures):
        colours = jnp.concatenate([self.feats[pl.ds(6, 3), self.whole], jnp.zeros((5, ENTRIES), F32)], axis=0)
        colour_hi = colours.astype(BF16).astype(F32)
        colour_lo = (colours - colour_hi).astype(BF16).astype(F32)
        both = jnp.concatenate([colour_hi, colour_lo], axis=0)
        both = jnp.concatenate([both[:, :HALF], both[:, :HALF], both[:, HALF:], both[:, HALF:]], axis=1)
        product = dot_nt(both.astype(BF16), self.part[...])
        picture = product[0:8] + product[8:16]
        pictures[0, :, self.tile, :] = picture[0:3]
        residual = picture - jnp.concatenate([targets[0, :, self.tile, :], jnp.zeros((5, PIXELS), F32)], axis=0)
        residual_hi = residual.astype(BF16).astype(F32)
        residual_lo = (residual - residual_hi).astype(BF16).astype(F32)
        pair = jnp.concatenate([residual_hi, residual_lo], axis=0).astype(BF16)
        product = dot_nn(pair, self.part[...])
        product = product[0:8] + product[8:16]
        self.grads[pl.ds(6, 3), self.whole] = jnp.concatenate(
            [product[0:3, 0:256] + product[0:3, 256:512], product[0:3, 512:768] + product[0:3, 768:1024]], axis=1
        )
        stack = jnp.concatenate([residual_hi, residual_lo, residual_hi, jnp.zeros((104, PIXELS), F32)], axis=0)
        rows24 = jnp.concatenate([colour_hi, colour_hi, colour_lo, jnp.zeros((104, ENTRIES), F32)], axis=0)
        self.plane[...] = dot_nn(jnp.transpose(stack).astype(BF16), rows24.astype(BF16))

    def shares(self):
        for chunk in range(CHUNKS):
            lanes = pl.ds(chunk * LANES, LANES)
            high, low = part_lanes(chunk)

            def body(y, rows, carry):
                value = self.plane[rows, lanes] * self.weight[rows, lanes]
                self.weight[rows, lanes] = value
                self.part[rows, high], self.part[rows, low] = split2(value)
                return carry

            self.each_row(body, 0)

    def later_shares(self, lower):
        self.plane[:, pl.ds(0, HALF)] = dot_nn(self.part[...], lower[...])
        self.plane[:, pl.ds(HALF, HALF)] = dot_nn(self.part[:, pl.ds(512, 512)], lower[pl.ds(0, 512), :])

    def sums(self):
        for chunk in range(CHUNKS):
            lanes = pl.ds(chunk * LANES, LANES)
            screen_y = self.feature(1, chunk) - self.top_y

            def body(y, rows, carry):
                sum_0, sum_1, sum_2 = carry
                delta_y = twice(screen_y - y)
                grad = self.weight[rows, lanes] - self.plane[rows, lanes] * self.ratio[rows, lanes]
                slope = grad * delta_y
                return sum_0 + grad, sum_1 + slope, sum_2 + slope * delta_y

            zero = jnp.zeros((TILE_SIDE, LANES), F32)
            sum_0, sum_1, sum_2 = self.each_row(body, (zero, zero, zero))
            delta_x = twice(self.feature(0, chunk)) - self.pixel_x
            over = lambda rows: jnp.sum(rows, axis=0, keepdims=True)
            first_x = over(delta_x * sum_0)
            first_y = over(sum_1)
            out = pl.ds(self.tile * ENTRIES + chunk * LANES, LANES)
            grads, row_of = self.grads, lambda f: self.row_of(f, chunk)
            grads[pl.ds(0, 1), out] = -row_of(2) * first_x - row_of(3) * first_y
            grads[pl.ds(1, 1), out] = -row_of(4) * first_y - row_of(3) * first_x
            grads[pl.ds(2, 1), out] = -0.5 * over(delta_x * delta_x * sum_0)
            grads[pl.ds(3, 1), out] = -over(delta_x * sum_1)
            grads[pl.ds(4, 1), out] = -0.5 * over(sum_2)
            grads[pl.ds(5, 1), out] = over(sum_0)


def wide(row, i):
    return jnp.broadcast_to(row[:, pl.ds(i, 1)], (8, LANES))


def twice(rows):
    return jnp.concatenate([rows, rows], axis=0)


def tile_body(
    tile_ids, tile_len, targets, pictures, slot_grads, feats, planes, parts, upper, lower, grads, masks, left, right
):
    first, second = [
        Tile(
            tile, wide(tile_ids, tile), wide(tile_len, tile), feats, grads,
            *[planes.at[4 * tile + i] for i in range(4)], parts.at[tile],
        )
        for tile in range(TILES_DEV)
    ]
    first.opacities()
    second.opacities()
    for tile in (first, second):
        tile.log_transmittance(upper)
        tile.weights()
    for tile in (first, second):
        tile.picture(targets, pictures)
        tile.shares()
    for tile in (first, second):
        tile.later_shares(lower)
        tile.sums()
    for n in range(TILES_DEV * CHUNKS):
        spread(grads[:, pl.ds(n * LANES, LANES)], 16, masks, n * 256, left, n * LANES)
    total = dot_nt(left[...], right[...])
    for zc in range(16):
        slot_grads[zc] = total[16 * zc : 16 * zc + FEATS] + total[256 + 16 * zc : 256 + 16 * zc + FEATS]


Y_ARRIVAL = (0, 1, 7, 2, 6, 3, 5, 4)
ZC_ARRIVAL = (0, 1, 15, 2, 14, 3, 13, 4, 12, 5, 11, 6, 10, 7, 9, 8)
LAST = 7 * 256


def render_kernel(
    camera_hbm, ids_hbm, len_hbm, params_hbm, slots_hbm, lists_hbm, targets_hbm,
    pictures, view_grads, dense, saved, shape_rows, totals, colour,
    camera, tile_ids, tile_len, params, packed, lists, targets, slots, cams,
    table, outgoing, landed, staged, received, slot_grads, landed_back, staged_back, returned, every,
    feats, planes, parts, upper, lower, grads, masks, left, right, view_masks, view_left, view_right,
    load_sem, send_y, recv_y, send_zc, recv_zc, send_zc2, recv_zc2, send_y2, recv_y2,
    send_slots, recv_slots, send_cams, recv_cams, send_view, recv_view,
):
    cell, view = lax.axis_index("cell"), lax.axis_index("view")
    my_y, my_zc = cell // ZC_DEVS, lax.rem(cell, ZC_DEVS)
    barrier, greetings = greet(my_y, my_zc, view)

    pieces = [(first, min(8, ROWS - first)) for first in range(0, ROWS, 8)]
    loads = [
        pltpu.make_async_copy(params_hbm.at[pl.ds(*piece)], params.at[pl.ds(*piece)], load_sem.at[i])
        for i, piece in enumerate(pieces)
    ]
    side_loads = [
        pltpu.make_async_copy(source, target, load_sem.at[8 + i])
        for i, (source, target) in enumerate(
            (
                (camera_hbm, camera),
                (slots_hbm, slots.at[0]),
                (lists_hbm, lists),
                (targets_hbm, targets),
                (ids_hbm, tile_ids),
                (len_hbm, tile_len),
            )
        )
    ]
    for load in loads[:2] + side_loads[:2] + loads[2:] + side_loads[2:]:
        load.start()
    table[...] = jnp.zeros_like(table)
    feats[...] = jnp.zeros_like(feats)
    grads[...] = jnp.zeros_like(grads)

    def unpack(group, size):
        for chunk in range(16):
            packed[pl.ds(group * 16 + chunk * 8, size), :] = params[pl.ds(group, size), pl.ds(chunk * LANES, LANES)]
        for row in range(group, group + size):
            for half in range(2):
                dense[2 * row + half] = packed[pl.ds((row // 8) * 128 + half * 8 + row % 8, 8, stride=16), :]

    def loader(half):
        return lambda row: dense[2 * row + half]

    def load_pieces(first, last):
        for load, piece in list(zip(loads, pieces))[first:last]:
            load.wait()
            unpack(*piece)

    def put_features(first, features, half):
        for f, feature in enumerate(features):
            table[pl.ds(half * 16 + first + f, 8, stride=32), :] = feature

    side_loads[0].wait()
    shift = [wide(camera, i) for i in range(3)]
    shift_row = lax.broadcasted_iota(jnp.int32, (8, LANES), 0)
    cams[0] = jnp.where(shift_row == 0, shift[0], jnp.where(shift_row == 1, shift[1], shift[2]))
    load_pieces(0, 2)
    for half in range(2):
        load = loader(half)
        matrix, scales, unit_q, inv_norm = shape_matrix([load(3 + i) for i in range(3)], [load(6 + i) for i in range(4)])
        for i, value in enumerate(matrix + scales + unit_q + [inv_norm]):
            shape_rows[half * SHAPE_ROWS + i] = value
        put_features(0, keep_geometry(load, shift, matrix, saved, half * KEPT), half)
    load_pieces(2, 8)
    for half in range(2):
        put_features(6, keep_colours(loader(half), saved, half * KEPT), half)

    side_loads[1].wait()
    pl.semaphore_wait(barrier, greetings)
    y_sends = {}
    for k in Y_ORDER + (0,):
        peer, device_id = y_peer(my_y, my_zc, k)
        for half in range(2):
            chunk = 2 * peer + half
            top, bottom = gather_chunk(table, slots[0, pl.ds(chunk, 1), :])
            outgoing[chunk, pl.ds(0, 8), :] = top
            outgoing[chunk, pl.ds(8, 1), :] = bottom[0:1]
        if k:
            y_sends[k] = remote(
                outgoing.at[pl.ds(2 * peer, 2)], landed.at[pl.ds(2 * my_y, 2)],
                send_y.at[k - 1], recv_y.at[k - 1], device_id,
            )
    landed[pl.ds(2 * my_y, 2)] = outgoing[pl.ds(2 * my_y, 2)]
    side_sends = []
    for k in VIEW_ORDER:
        peer = view_peer(view, k)
        side_sends.append(remote(slots.at[0], slots.at[k], send_slots.at[k - 1], recv_slots.at[k - 1], peer))
        side_sends.append(remote(cams.at[0], cams.at[k], send_cams.at[k - 1], recv_cams.at[k - 1], peer))

    fill_triangles(upper, lower)
    for load in side_loads[2:]:
        load.wait()
    for tile in range(TILES_DEV):
        for chunk in range(ENTRIES // LANES):
            n = tile * (ENTRIES // LANES) + chunk
            high, low = entry_slot(lists, tile, chunk)
            fill_masks(high, 16, masks, n * 256)
            right[:, pl.ds(n * LANES, LANES)] = hot_rows(low, LANES)

    def view_factors(k):
        for p, step in enumerate(Y_ARRIVAL):
            for half in range(2):
                n = 2 * p + half
                index = slots[k, pl.ds(2 * lax.rem(my_y + Y_DEVS - step, Y_DEVS) + half, 1), :]
                fill_masks(index >> 8, 8, view_masks, (k * 16 + n) * 128)
                view_right[k, :, pl.ds(n * LANES, LANES)] = hot_rows(index & 255, 256)

    for k in Y_ORDER[::-1]:
        y_sends[k].wait()

    def to_zc(j, half, rows):
        staged[8 * half + j] = rows

    regroup(lambda i, half: landed[2 * i + half], to_zc)
    zc_sends = {}
    for k in ZC_ORDER:
        peer, device_id = zc_peer(my_y, my_zc, k)
        zc_sends[k] = remote(
            staged.at[peer], received.at[my_zc], send_zc.at[k - 1], recv_zc.at[k - 1], device_id
        )
    received[my_zc] = staged[my_zc]

    view_factors(0)
    for copy in side_sends:
        copy.wait()

    def view_forward(k):
        for half in range(2):
            shift = [jnp.broadcast_to(cams[k, pl.ds(i, 1), :], (8, LANES)) for i in range(3)]
            matrix = [shape_rows[half * SHAPE_ROWS + i] for i in range(9)]
            keep_geometry(loader(half), shift, matrix, saved, (2 * k + half) * KEPT)
            keep_colours(loader(half), saved, (2 * k + half) * KEPT)
        view_factors(k)

    places = [entry_slot(lists, n // 4, n % 4) for n in range(8)]
    places = [(jnp.broadcast_to(high, (8, LANES)), jnp.broadcast_to(low, (8, LANES))) for high, low in places]
    tops = [jnp.zeros((8, LANES), F32)] * 8
    bottoms = [jnp.zeros((8, LANES), F32)] * 8
    for k in ZC_ARRIVAL:
        if k:
            zc_sends[k].wait()
        source = lax.rem(my_zc + ZC_DEVS - k, ZC_DEVS)
        top = received[source, pl.ds(0, 8), :]
        bottom = jnp.broadcast_to(received[source, pl.ds(8, 1), :], (8, LANES))
        for n, (high, low) in enumerate(places):
            here = high == source
            tops[n] = jnp.where(here, lane_gather(top, low), tops[n])
            bottoms[n] = jnp.where(here, lane_gather(bottom, low), bottoms[n])
    for n in range(8):
        feats[pl.ds(0, 8), pl.ds(n * LANES, LANES)] = tops[n]
        feats[pl.ds(8, 8), pl.ds(n * LANES, LANES)] = bottoms[n]

    tile_body(
        tile_ids, tile_len, targets, pictures, slot_grads,
        feats, planes, parts, upper, lower, grads, masks, left, right,
    )

    for k in ZC_ORDER:
        peer, device_id = zc_peer(my_y, my_zc, k)
        zc_sends[k] = remote(
            slot_grads.at[peer], landed_back.at[my_zc], send_zc2.at[k - 1], recv_zc2.at[k - 1], device_id
        )
    landed_back[my_zc] = slot_grads[my_zc]
    view_forward(1)
    view_forward(2)
    for k in ZC_ORDER[::-1]:
        zc_sends[k].wait()

    def to_y(j, half, rows):
        staged_back[2 * j + half] = rows

    regroup(lambda i, half: landed_back[8 * half + i], to_y)
    view_sends = {}
    for k in Y_ORDER:
        peer, device_id = y_peer(my_y, my_zc, k)
        y_sends[k] = remote(
            staged_back.at[pl.ds(2 * peer, 2)], returned.at[pl.ds(2 * my_y, 2)],
            send_y2.at[k - 1], recv_y2.at[k - 1], device_id,
        )
        if k == FAR_Y:
            for other in VIEW_ORDER:
                view_sends[other, 7] = remote(
                    staged_back.at[pl.ds(2 * peer, 2)], every.at[other, pl.ds(14, 2)],
                    send_view.at[other - 1, 7], recv_view.at[other - 1, 7],
                    far_view_peer(my_y, my_zc, view, other),
                )
    returned[pl.ds(2 * my_y, 2)] = staged_back[pl.ds(2 * my_y, 2)]

    def add_left(k, p, block):
        for half in range(2):
            n = 2 * p + half
            values = jnp.concatenate(
                [block(half, 0, 8), jnp.broadcast_to(block(half, 8, 1), (8, LANES))], axis=0
            )
            spread(values, 8, view_masks, (k * 16 + n) * 128, view_left.at[k], n * LANES)

    def scatter(k, columns, first):
        product = dot_nt(view_left[k, :, columns], view_right[k, :, columns])
        for half in range(2):
            lanes = slice(half * LANES, (half + 1) * LANES)
            rows = pl.ds((2 * k + half) * 128, 128)
            value = product[0:128, lanes] + product[128:256, lanes]
            view_grads[rows, :] = value if first else view_grads[rows, :] + value

    for p, step in enumerate(Y_ARRIVAL):
        if step:
            y_sends[step].wait()
        y = lax.rem(my_y + Y_DEVS - step, Y_DEVS)
        for k in VIEW_ORDER if step != FAR_Y else ():
            view_sends[k, p] = remote(
                returned.at[pl.ds(2 * y, 2)], every.at[k, pl.ds(2 * p, 2)],
                send_view.at[k - 1, p], recv_view.at[k - 1, p], view_peer(view, k),
            )
        add_left(0, p, lambda half, row, size, y=y: returned[2 * y + half, pl.ds(row, size), :])
        if p == 0:
            view_forward(3)
    scatter(0, pl.ds(0, G_DEV), True)
    for half in range(2):
        matrix = [shape_rows[half * SHAPE_ROWS + i] for i in range(9)]
        sums, colours = pull_view(loader(half), slot_rows(view_grads, 0, half), matrix, saved, half * KEPT)
        for i, value in enumerate(sums):
            totals[half * SUMS + i] = value
        for i, value in enumerate(colours):
            colour[half * 3 + i] = value
    for p in range(8):
        for k in (1, 3, 2):
            view_sends[k, p].wait()
            add_left(k, p, lambda half, row, size: every[k, 2 * p + half, pl.ds(row, size), :])
        if p == 6:
            for k in (1, 3, 2):
                scatter(k, pl.ds(0, LAST), True)
    for k in (1, 3, 2):
        scatter(k, pl.ds(LAST, 256), False)


SUMS = 13


def slot_rows(view_grads, view, half):
    return lambda f: view_grads[pl.ds((2 * view + half) * 128 + f, 8, stride=16), :]


def finish_kernel(
    pictures, view_grads, dense, saved, shape_rows, totals, colour_mine,
    pictures_hbm, gradient_hbm,
    gradient, packed, colour, sums, sems,
):
    groups = [(first, min(8, ROWS - first)) for first in range(0, ROWS, 8)]
    copies = [
        pltpu.make_async_copy(gradient.at[pl.ds(*group)], gradient_hbm.at[pl.ds(*group)], sems.at[i])
        for i, group in enumerate(groups)
    ]
    copies.append(pltpu.make_async_copy(pictures, pictures_hbm, sems.at[8]))
    copies[8].start()

    def put(row, half, value):
        packed[pl.ds((row // 8) * 128 + half * 8 + row % 8, 8, stride=16), :] = value

    def send(i):
        first, size = groups[i]
        for chunk in range(16):
            gradient[pl.ds(first, size), pl.ds(chunk * LANES, LANES)] = packed[
                pl.ds(first * 16 + chunk * 8, size), :
            ]
        copies[i].start()

    def put_harmonic(row, half):
        channel, j = divmod(row - 11, 16)
        parts = [colour[(2 * k + half) * 3 + channel] for k in range(VIEW_DEVS)]
        if j:
            parts = [saved[(2 * k + half) * KEPT + 21 + j] * parts[k] for k in range(VIEW_DEVS)]
        total = parts[0] + parts[1] + parts[2] + parts[3]
        put(row, half, total if j else sh_first * total)

    for half in range(2):
        load = lambda row: dense[2 * row + half]
        matrix = [shape_rows[half * SHAPE_ROWS + i] for i in range(9)]
        total = [totals[half * SUMS + i] for i in range(SUMS)]
        for i in range(3):
            colour[half * 3 + i] = colour_mine[half * 3 + i]
        for k in range(1, VIEW_DEVS):
            place = 2 * k + half
            values, colours = pull_view(load, slot_rows(view_grads, k, half), matrix, saved, place * KEPT)
            total = [old + value for old, value in zip(total, values)]
            for i, value in enumerate(colours):
                colour[place * 3 + i] = value
        for i, value in enumerate(total):
            sums[half * SUMS + i] = value
    for i in range(2, 8):
        first, size = groups[i]
        for row in range(first, first + size):
            for half in range(2):
                put_harmonic(row, half)
        send(i)
    for half in range(2):
        total = [sums[half * SUMS + i] for i in range(SUMS)]
        shape = [shape_rows[half * SHAPE_ROWS + i] for i in range(SHAPE_ROWS)]
        matrix, scales, unit_q, inv_norm = shape[0:9], shape[9:12], shape[12:16], shape[16]
        for i in range(3):
            put(i, half, total[i])
            put(3 + i, half, total[3 + i] * matrix[i] + total[6 + i] * matrix[3 + i] + total[9 + i] * matrix[6 + i])
        _, pull_back = jax.vjp(rotation_of, *unit_q)
        g_unit = pull_back([total[3 + 3 * i + j] * scales[j] for i in range(3) for j in range(3)])
        along = unit_q[0] * g_unit[0] + unit_q[1] * g_unit[1] + unit_q[2] * g_unit[2] + unit_q[3] * g_unit[3]
        for i in range(4):
            put(6 + i, half, inv_norm * (g_unit[i] - unit_q[i] * along))
        put(10, half, total[12] * (1.0 / (1.0 + jnp.exp(dense[20 + half]))))
        for row in range(11, 16):
            put_harmonic(row, half)
    send(0)
    send(1)
    for copy in copies:
        copy.wait()


def finish_call(operands):
    vmem = pl.BlockSpec(memory_space=pltpu.VMEM)
    anywhere = pl.BlockSpec(memory_space=pl.ANY)
    tile = (8, LANES)
    return pl.pallas_call(
        finish_kernel,
        out_shape=(
            jax.ShapeDtypeStruct(operands[0].shape, F32),
            jax.ShapeDtypeStruct((ROWS, G_DEV), F32),
        ),
        in_specs=[vmem] * len(operands),
        out_specs=(anywhere, anywhere),
        scratch_shapes=[
            pltpu.VMEM((ROWS, G_DEV), F32),
            pltpu.VMEM((64 * 16, LANES), F32),
            pltpu.VMEM((VIEW_DEVS * 2 * 3,) + tile, F32),
            pltpu.VMEM((2 * SUMS,) + tile, F32),
            pltpu.SemaphoreType.DMA((9,)),
        ],
        compiler_params=pltpu.CompilerParams(vmem_limit_bytes=8 * 2**20),
        name="finish",
    )(*operands)


def render_call(camera, tile_ids, tile_len, params, slots, lists, targets):
    anywhere = pl.BlockSpec(memory_space=pl.ANY)
    blocks = pltpu.VMEM((16, FEATS, LANES), F32)
    tile = (8, LANES)
    y_sems = [pltpu.SemaphoreType.DMA((Y_DEVS - 1,))] * 2
    zc_sems = [pltpu.SemaphoreType.DMA((ZC_DEVS - 1,))] * 2
    view_sems = [pltpu.SemaphoreType.DMA((VIEW_DEVS - 1,))] * 2
    return pl.pallas_call(
        render_kernel,
        out_shape=(
            pltpu.VMEM(targets.shape, F32),
            pltpu.VMEM((VIEW_DEVS * 256, LANES), F32),
            pltpu.VMEM((2 * ROWS,) + tile, F32),
            pltpu.VMEM((VIEW_DEVS * 2 * KEPT,) + tile, F32),
            pltpu.VMEM((2 * SHAPE_ROWS,) + tile, F32),
            pltpu.VMEM((2 * SUMS,) + tile, F32),
            pltpu.VMEM((2 * 3,) + tile, F32),
        ),
        in_specs=[anywhere] * 7,
        out_specs=(pl.BlockSpec(memory_space=pltpu.VMEM),) * 7,
        scratch_shapes=[
            pltpu.VMEM(camera.shape, F32),
            pltpu.VMEM(tile_ids.shape, jnp.int32),
            pltpu.VMEM(tile_len.shape, jnp.int32),
            pltpu.VMEM((ROWS, G_DEV), F32),
            pltpu.VMEM((64 * 16, LANES), F32),
            pltpu.VMEM(lists.shape, jnp.int32),
            pltpu.VMEM(targets.shape, F32),
            pltpu.VMEM((VIEW_DEVS, 16, LANES), jnp.int32),
            pltpu.VMEM((VIEW_DEVS,) + tile, F32),
            pltpu.VMEM((256, LANES), F32),
        ]
        + [blocks] * 8
        + [
            pltpu.VMEM((VIEW_DEVS, 16, FEATS, LANES), F32),
            pltpu.VMEM((16, TILES_DEV * ENTRIES), F32),
            pltpu.VMEM((4 * TILES_DEV, PIXELS, ENTRIES), F32),
            pltpu.VMEM((TILES_DEV, PIXELS, 2 * ENTRIES), BF16),
            pltpu.VMEM((1024, 256), BF16),
            pltpu.VMEM((1024, 256), BF16),
            pltpu.VMEM((16, TILES_DEV * ENTRIES), F32),
            pltpu.VMEM((8 * 256, LANES), BF16),
            pltpu.VMEM((512, TILES_DEV * ENTRIES), BF16),
            pltpu.VMEM((LANES, TILES_DEV * ENTRIES), BF16),
            pltpu.VMEM((VIEW_DEVS * 16 * 128, LANES), BF16),
            pltpu.VMEM((VIEW_DEVS, 256, G_DEV), BF16),
            pltpu.VMEM((VIEW_DEVS, 256, G_DEV), BF16),
            pltpu.SemaphoreType.DMA((14,)),
        ]
        + y_sems + zc_sems + zc_sems + y_sems + view_sems + view_sems
        + [pltpu.SemaphoreType.DMA((VIEW_DEVS - 1, 8))] * 2,
        compiler_params=pltpu.CompilerParams(
            collective_id=0, has_side_effects=True, vmem_limit_bytes=40 * 2**20
        ),
        name="render",
    )(
        *[
            pltpu.with_memory_space_constraint(operand, pltpu.HBM)
            for operand in (camera, tile_ids, tile_len, params, slots, lists, targets)
        ]
    )


def local(params, cameras, targets, tile_ids, send_slots, tile_lists, tile_len):
    partial = render_call(
        cameras, tile_ids, tile_len, params, send_slots.reshape(16, LANES), tile_lists,
        jnp.transpose(targets, (0, 2, 1, 3)),
    )
    pictures, gradient = finish_call(partial)
    return jnp.transpose(pictures, (0, 2, 1, 3)), gradient


def solution(mesh):
    return jax.shard_map(
        local,
        mesh=mesh,
        in_specs=(
            P(None, "cell"),
            P("view", None),
            P("view", "cell", None, None),
            P("view", "cell"),
            P("view", "cell", None),
            P("view", "cell", None),
            P("view", "cell"),
        ),
        out_specs=(P("view", "cell", None, None), P(None, "cell")),
        check_vma=False,
    )
```

```python
import jax
import jax.numpy as jnp
from jax import lax
from jax.experimental import pallas as pl
from jax.experimental.pallas import tpu as pltpu
from jax.sharding import PartitionSpec as P

TILE_SIDE = 16
TILE_COLS = 32
LANES = 128
Y_DEVS = 8
ZC_DEVS = 16
VIEW_DEVS = 4
FEATS = 9
Y_ORDER = (4, 3, 5, 2, 6, 1, 7)
ZC_ORDER = (8, 9, 7, 6, 10, 5, 11, 4, 12, 3, 13, 2, 14, 1, 15)
VIEW_ORDER = (2, 1, 3)
ENTRIES = 512
CHUNKS = ENTRIES // LANES
HALF = ENTRIES // 2
TILES_DEV = 2
PIXELS = 256
ROWS = 59
G_DEV = 2048
LOG2_E = 1.4426950408889634
F32 = jnp.float32
BF16 = jnp.bfloat16

focal_length = 800.0
dilation = 0.3
sh_first = 0.28209479177387814
sh_second = 0.4886025119029199
sh_third = (
    1.0925484305920792,
    -1.0925484305920792,
    0.31539156525252005,
    -1.0925484305920792,
    0.5462742152960396,
)
sh_fourth = (
    -0.5900435899266435,
    2.890611442640554,
    -0.4570457994644658,
    0.3731763325901154,
    -0.4570457994644658,
    1.445305721320277,
    -0.5900435899266435,
)


def split2(value):
    high = value.astype(BF16)
    return high, (value - high.astype(F32)).astype(BF16)


def dot_nt(lhs, rhs):
    return lax.dot_general(lhs, rhs, (((1,), (1,)), ((), ())), preferred_element_type=F32)


def dot_nn(lhs, rhs):
    return lax.dot_general(lhs, rhs, (((1,), (0,)), ((), ())), preferred_element_type=F32)


def rotation_of(q_w, q_x, q_y, q_z):
    return [
        1.0 - 2.0 * (q_y * q_y + q_z * q_z),
        2.0 * (q_x * q_y - q_w * q_z),
        2.0 * (q_x * q_z + q_w * q_y),
        2.0 * (q_x * q_y + q_w * q_z),
        1.0 - 2.0 * (q_x * q_x + q_z * q_z),
        2.0 * (q_y * q_z - q_w * q_x),
        2.0 * (q_x * q_z - q_w * q_y),
        2.0 * (q_y * q_z + q_w * q_x),
        1.0 - 2.0 * (q_x * q_x + q_y * q_y),
    ]


def unit_quaternion(quaternion):
    total = sum(part * part for part in quaternion[1:]) + quaternion[0] * quaternion[0]
    inverse = lax.rsqrt(total)
    return [part * inverse for part in quaternion], inverse


def shape_matrix(log_scales, quaternion):
    scales = [jnp.exp(part) for part in log_scales]
    unit, inverse = unit_quaternion(quaternion)
    rotation = rotation_of(*unit)
    matrix = [rotation[3 * i + j] * scales[j] for i in range(3) for j in range(3)]
    return matrix, scales, unit, inverse


def harmonics(x, y, z):
    xx, yy, zz = x * x, y * y, z * z
    rim = 4.0 * zz - xx - yy
    gap = xx - yy
    return [
        -sh_second * y,
        sh_second * z,
        -sh_second * x,
        sh_third[0] * (x * y),
        sh_third[1] * (y * z),
        sh_third[2] * (2.0 * zz - xx - yy),
        sh_third[3] * (x * z),
        sh_third[4] * gap,
        sh_fourth[0] * (y * (3.0 * xx - yy)),
        sh_fourth[1] * (x * y * z),
        sh_fourth[2] * (y * rim),
        sh_fourth[3] * (z * (2.0 * zz - 3.0 * xx - 3.0 * yy)),
        sh_fourth[4] * (x * rim),
        sh_fourth[5] * (z * gap),
        sh_fourth[6] * (x * (xx - 3.0 * yy)),
    ]


def geometry(pos, matrix):
    x, y, z = pos
    inv_z = 1.0 / z
    jac = focal_length * inv_z
    screen_x = x * jac
    screen_y = y * jac
    jac_x = -screen_x * inv_z
    jac_y = -screen_y * inv_z
    row_u = [jac * matrix[j] + jac_x * matrix[6 + j] for j in range(3)]
    row_v = [jac * matrix[3 + j] + jac_y * matrix[6 + j] for j in range(3)]
    cov_a = row_u[0] * row_u[0] + row_u[1] * row_u[1] + row_u[2] * row_u[2] + dilation
    cov_c = row_v[0] * row_v[0] + row_v[1] * row_v[1] + row_v[2] * row_v[2] + dilation
    cov_b = row_u[0] * row_v[0] + row_u[1] * row_v[1] + row_u[2] * row_v[2]
    inv_det = 1.0 / (cov_a * cov_c - cov_b * cov_b)
    return inv_z, jac, screen_x, screen_y, jac_x, jac_y, row_u, row_v, cov_a, cov_b, cov_c, inv_det


def direction(pos):
    x, y, z = pos
    inverse = lax.rsqrt(x * x + y * y + z * z)
    return [x * inverse, y * inverse, z * inverse], inverse


def raw_colour(load, channel, basis):
    total = load(11 + 16 * channel) * sh_first
    for j in range(15):
        total = total + load(12 + 16 * channel + j) * basis[j]
    return total + 0.5


KEPT = 40
SHAPE_ROWS = 17


def keep_geometry(load, shift, matrix, saved, base):
    pos = [load(i) - shift[i] for i in range(3)]
    inv_z, jac, screen_x, screen_y, jac_x, jac_y, row_u, row_v, cov_a, cov_b, cov_c, inv_det = geometry(pos, matrix)
    unit, inv_len = direction(pos)
    values = [pos[0], pos[1], inv_z, jac, screen_x, screen_y, jac_x, jac_y]
    values += row_u + row_v + [cov_a, cov_b, cov_c, inv_det] + unit + [inv_len] + harmonics(*unit)
    for i, value in enumerate(values):
        saved[base + i] = value
    opacity = 1.0 / (1.0 + jnp.exp(-load(10)))
    return [screen_x, screen_y, cov_c * inv_det, -cov_b * inv_det, cov_a * inv_det, opacity]


def keep_colours(load, saved, base):
    basis = [saved[base + 22 + j] for j in range(15)]
    raw = [raw_colour(load, channel, basis) for channel in range(3)]
    for channel, value in enumerate(raw):
        saved[base + 37 + channel] = jnp.where(value > 0.0, 1.0, jnp.where(value < 0.0, 0.0, 0.5))
    return [jnp.maximum(value, 0.0) for value in raw]


def pull_view(load, slot, matrix, saved, base):
    kept = lambda i: saved[base + i]
    inv_z, jac, screen_x, screen_y, jac_x, jac_y = [kept(2 + i) for i in range(6)]
    row_u, row_v = [kept(8 + i) for i in range(3)], [kept(11 + i) for i in range(3)]
    cov_a, cov_b, cov_c, inv_det = [kept(14 + i) for i in range(4)]
    g_a, g_b, g_c = slot(2), slot(3), slot(4)
    g_det = -(g_a * cov_c - g_b * cov_b + g_c * cov_a) * inv_det * inv_det
    d_a = 2.0 * (g_c * inv_det + g_det * cov_c)
    d_c = 2.0 * (g_a * inv_det + g_det * cov_a)
    d_b = -g_b * inv_det - 2.0 * g_det * cov_b
    g_u = [d_a * row_u[j] + d_b * row_v[j] for j in range(3)]
    g_v = [d_c * row_v[j] + d_b * row_u[j] for j in range(3)]
    g_matrix = [jac * g_u[j] for j in range(3)] + [jac * g_v[j] for j in range(3)]
    g_matrix += [jac_x * g_u[j] + jac_y * g_v[j] for j in range(3)]
    g_jac = g_u[0] * matrix[0] + g_v[0] * matrix[3]
    for j in (1, 2):
        g_jac = g_jac + (g_u[j] * matrix[j] + g_v[j] * matrix[3 + j])
    g_jac_x = g_u[0] * matrix[6] + g_u[1] * matrix[7] + g_u[2] * matrix[8]
    g_jac_y = g_v[0] * matrix[6] + g_v[1] * matrix[7] + g_v[2] * matrix[8]
    g_sx = slot(0) - inv_z * g_jac_x
    g_sy = slot(1) - inv_z * g_jac_y
    g_inv = focal_length * (g_jac + kept(0) * g_sx + kept(1) * g_sy) - screen_x * g_jac_x - screen_y * g_jac_y
    g_pos = [jac * g_sx, jac * g_sy, -inv_z * inv_z * g_inv]

    g_colours = [slot(6 + channel) * kept(37 + channel) for channel in range(3)]
    g_basis = []
    for j in range(15):
        terms = [load(12 + 16 * channel + j) * g_colours[channel] for channel in range(3)]
        g_basis.append(terms[0] + terms[1] + terms[2])
    unit, inv_len = [kept(18 + i) for i in range(3)], kept(21)
    _, pull = jax.vjp(harmonics, *unit)
    g_unit = pull(g_basis)
    along = unit[0] * g_unit[0] + unit[1] * g_unit[1] + unit[2] * g_unit[2]
    for i in range(3):
        g_pos[i] = g_pos[i] + inv_len * (g_unit[i] - unit[i] * along)
    return g_pos + g_matrix + [slot(5)], g_colours


def lane_gather(source, index):
    return jnp.take_along_axis(source, index, axis=1, mode="promise_in_bounds")


def gather_chunk(table, index):
    shape = (8, LANES)
    low = jnp.broadcast_to(index & 127, shape)
    high = jnp.broadcast_to(index >> 7, shape)
    top = bottom = jnp.zeros(shape, F32)
    for chunk in range(16):
        here = high == chunk
        top = jnp.where(here, lane_gather(table[pl.ds(16 * chunk, 8), :], low), top)
        bottom = jnp.where(here, lane_gather(table[pl.ds(16 * chunk + 8, 8), :], low), bottom)
    return top, bottom


def block_transpose(rows):
    group = lax.broadcasted_iota(jnp.int32, rows[0].shape, 1) // 16
    for step in (1, 2, 4):
        odd = (group & step) != 0
        fresh = list(rows)
        for i in range(8):
            if i & step:
                continue
            first, second = rows[i], rows[i + step]
            fresh[i] = jnp.where(odd, pltpu.roll(second, 16 * step, 1), first)
            fresh[i + step] = jnp.where(odd, second, pltpu.roll(first, LANES - 16 * step, 1))
        rows = fresh
    return rows


def remote(src_ref, dst_ref, send_sem, recv_sem, device_id):
    copy = pltpu.make_async_remote_copy(
        src_ref=src_ref,
        dst_ref=dst_ref,
        send_sem=send_sem,
        recv_sem=recv_sem,
        device_id=device_id,
        device_id_type=pl.DeviceIdType.MESH,
    )
    copy.start()
    return copy


def y_peer(my_y, my_zc, k):
    peer = lax.rem(my_y + k, Y_DEVS)
    return peer, {"cell": peer * ZC_DEVS + my_zc}


def zc_peer(my_y, my_zc, k):
    peer = lax.rem(my_zc + k, ZC_DEVS)
    return peer, {"cell": my_y * ZC_DEVS + peer}


def view_peer(view, k):
    return {"view": lax.rem(view + k, VIEW_DEVS)}


def greet(my_y, my_zc, view):
    barrier = pltpu.get_barrier_semaphore()
    peers = [y_peer(my_y, my_zc, k)[1] for k in Y_ORDER]
    peers += [zc_peer(my_y, my_zc, k)[1] for k in ZC_ORDER]
    peers += [view_peer(view, k) for k in VIEW_ORDER]
    for peer in peers:
        pl.semaphore_signal(barrier, inc=1, device_id=peer, device_id_type=pl.DeviceIdType.MESH)
    return barrier, len(peers)


def regroup(load, store):
    for half in range(2):
        for j, rows in enumerate(block_transpose([load(i, half) for i in range(8)])):
            store(j, half, rows)


def part_lanes(chunk):
    base = (chunk // 2) * 512 + (chunk % 2) * LANES
    return pl.ds(base, LANES), pl.ds(base + 256, LANES)


def fill_triangles(upper, lower):
    row = lax.broadcasted_iota(jnp.int32, (256, 256), 0)
    col = lax.broadcasted_iota(jnp.int32, (256, 256), 1)
    above = jnp.where(row < col, 1.0, 0.0).astype(BF16)
    below = jnp.where(row > col, 1.0, 0.0).astype(BF16)
    ones = jnp.ones((256, 256), BF16)
    for i in range(4):
        upper[pl.ds(256 * i, 256), :] = ones if i < 2 else above
        lower[pl.ds(256 * i, 256), :] = below if i < 2 else ones


def entry_slot(lists, my_y, tile, chunk):
    index = lists[0, pl.ds(tile, 1), pl.ds(chunk * LANES, LANES)]
    steps = (my_y - (index >> 8)) & (Y_DEVS - 1)
    return (index >> 4) & 15, (steps << 4) | (index & 15)


def hot_rows(index, count):
    shape = (count, LANES)
    return jnp.where(
        jnp.broadcast_to(index, shape) == lax.broadcasted_iota(jnp.int32, shape, 0), 1.0, 0.0
    ).astype(BF16)


def fill_masks(high, count, masks, base):
    high = jnp.broadcast_to(high, (16, LANES))
    for value in range(count):
        masks[pl.ds(base + 16 * value, 16), :] = jnp.where(high == value, 1.0, 0.0).astype(BF16)


def spread(values, count, masks, base, left, column):
    for i, piece in enumerate(split2(values)):
        for value in range(count):
            left[pl.ds((i * count + value) * 16, 16), pl.ds(column, LANES)] = (
                masks[pl.ds(base + 16 * value, 16), :] * piece
            )


class Tile:
    def __init__(self, tile, number, length, feats, grads, alpha, ratio, plane, weight, part):
        self.tile, self.length, self.feats, self.grads = tile, length, feats, grads
        self.alpha, self.ratio, self.plane, self.weight, self.part = alpha, ratio, plane, weight, part
        self.whole = pl.ds(tile * ENTRIES, ENTRIES)
        left_x = twice((TILE_SIDE * (number & (TILE_COLS - 1))).astype(F32) + 0.5)
        self.top_y = (TILE_SIDE * (number >> 5)).astype(F32) + 0.5
        self.pixel_x = lax.broadcasted_iota(jnp.int32, (TILE_SIDE, LANES), 0).astype(F32) + left_x

    def row_of(self, f, chunk):
        return self.feats[pl.ds(f, 1), pl.ds(self.tile * ENTRIES + chunk * LANES, LANES)]

    def feature(self, f, chunk):
        return jnp.broadcast_to(self.row_of(f, chunk), (8, LANES))

    def each_row(self, body, carry):
        def one_row(y, carry):
            rows = pl.ds(pl.multiple_of(y * TILE_SIDE, TILE_SIDE), TILE_SIDE)
            return body(y.astype(F32), rows, carry)

        return lax.fori_loop(0, TILE_SIDE, one_row, carry, unroll=TILE_SIDE)

    def opacities(self):
        for chunk in range(CHUNKS):
            lanes = pl.ds(chunk * LANES, LANES)
            high, low = part_lanes(chunk)
            lane = lax.broadcasted_iota(jnp.int32, (8, LANES), 1) + chunk * LANES
            log_opacity = jnp.where(lane < self.length, jnp.log2(self.feature(5, chunk)), -1e30)
            delta_x = twice(self.feature(0, chunk)) - self.pixel_x
            part_x = twice((-0.5 * LOG2_E) * self.feature(2, chunk)) * delta_x * delta_x + twice(log_opacity)
            cross = twice(-LOG2_E * self.feature(3, chunk)) * delta_x
            screen_y = self.feature(1, chunk) - self.top_y
            conic_c = (-0.5 * LOG2_E) * self.feature(4, chunk)

            def body(y, rows, carry):
                delta_y = screen_y - y
                part_y = conic_c * delta_y * delta_y
                value = jnp.exp2(part_x + cross * twice(delta_y) + twice(part_y))
                keep = jnp.log2(1.0 - value)
                self.alpha[rows, lanes] = value
                self.ratio[rows, lanes] = value * jnp.exp2(-keep)
                self.part[rows, high], self.part[rows, low] = split2(keep)
                return carry

            self.each_row(body, 0)

    def log_transmittance(self, upper):
        self.plane[:, pl.ds(0, HALF)] = dot_nn(self.part[:, pl.ds(0, 512)], upper[pl.ds(512, 512), :])
        self.plane[:, pl.ds(HALF, HALF)] = dot_nn(self.part[...], upper[...])

    def weights(self):
        for chunk in range(CHUNKS):
            lanes = pl.ds(chunk * LANES, LANES)
            high, low = part_lanes(chunk)

            def body(y, rows, carry):
                value = jnp.exp2(self.plane[rows, lanes]) * self.alpha[rows, lanes]
                self.weight[rows, lanes] = value
                self.part[rows, high], self.part[rows, low] = split2(value)
                return carry

            self.each_row(body, 0)

    def picture(self, targets, pictures):
        colours = jnp.concatenate([self.feats[pl.ds(6, 3), self.whole], jnp.zeros((5, ENTRIES), F32)], axis=0)
        colour_hi = colours.astype(BF16).astype(F32)
        colour_lo = (colours - colour_hi).astype(BF16).astype(F32)
        both = jnp.concatenate([colour_hi, colour_lo], axis=0)
        both = jnp.concatenate([both[:, :HALF], both[:, :HALF], both[:, HALF:], both[:, HALF:]], axis=1)
        product = dot_nt(both.astype(BF16), self.part[...])
        picture = product[0:8] + product[8:16]
        pictures[0, :, self.tile, :] = picture[0:3]
        residual = picture - jnp.concatenate([targets[0, :, self.tile, :], jnp.zeros((5, PIXELS), F32)], axis=0)
        residual_hi = residual.astype(BF16).astype(F32)
        residual_lo = (residual - residual_hi).astype(BF16).astype(F32)
        pair = jnp.concatenate([residual_hi, residual_lo], axis=0).astype(BF16)
        product = dot_nn(pair, self.part[...])
        product = product[0:8] + product[8:16]
        self.grads[pl.ds(6, 3), self.whole] = jnp.concatenate(
            [product[0:3, 0:256] + product[0:3, 256:512], product[0:3, 512:768] + product[0:3, 768:1024]], axis=1
        )
        stack = jnp.concatenate([residual_hi, residual_lo, residual_hi, jnp.zeros((104, PIXELS), F32)], axis=0)
        rows24 = jnp.concatenate([colour_hi, colour_hi, colour_lo, jnp.zeros((104, ENTRIES), F32)], axis=0)
        self.plane[...] = dot_nn(jnp.transpose(stack).astype(BF16), rows24.astype(BF16))

    def shares(self):
        for chunk in range(CHUNKS):
            lanes = pl.ds(chunk * LANES, LANES)
            high, low = part_lanes(chunk)

            def body(y, rows, carry):
                value = self.plane[rows, lanes] * self.weight[rows, lanes]
                self.weight[rows, lanes] = value
                self.part[rows, high], self.part[rows, low] = split2(value)
                return carry

            self.each_row(body, 0)

    def later_shares(self, lower):
        self.plane[:, pl.ds(0, HALF)] = dot_nn(self.part[...], lower[...])
        self.plane[:, pl.ds(HALF, HALF)] = dot_nn(self.part[:, pl.ds(512, 512)], lower[pl.ds(0, 512), :])

    def sums(self):
        for chunk in range(CHUNKS):
            lanes = pl.ds(chunk * LANES, LANES)
            screen_y = self.feature(1, chunk) - self.top_y

            def body(y, rows, carry):
                sum_0, sum_1, sum_2 = carry
                delta_y = twice(screen_y - y)
                grad = self.weight[rows, lanes] - self.plane[rows, lanes] * self.ratio[rows, lanes]
                slope = grad * delta_y
                return sum_0 + grad, sum_1 + slope, sum_2 + slope * delta_y

            zero = jnp.zeros((TILE_SIDE, LANES), F32)
            sum_0, sum_1, sum_2 = self.each_row(body, (zero, zero, zero))
            delta_x = twice(self.feature(0, chunk)) - self.pixel_x
            over = lambda rows: jnp.sum(rows, axis=0, keepdims=True)
            first_x = over(delta_x * sum_0)
            first_y = over(sum_1)
            out = pl.ds(self.tile * ENTRIES + chunk * LANES, LANES)
            grads, row_of = self.grads, lambda f: self.row_of(f, chunk)
            grads[pl.ds(0, 1), out] = -row_of(2) * first_x - row_of(3) * first_y
            grads[pl.ds(1, 1), out] = -row_of(4) * first_y - row_of(3) * first_x
            grads[pl.ds(2, 1), out] = -0.5 * over(delta_x * delta_x * sum_0)
            grads[pl.ds(3, 1), out] = -over(delta_x * sum_1)
            grads[pl.ds(4, 1), out] = -0.5 * over(sum_2)
            grads[pl.ds(5, 1), out] = over(sum_0)


def wide(row, i):
    return jnp.broadcast_to(row[:, pl.ds(i, 1)], (8, LANES))


def twice(rows):
    return jnp.concatenate([rows, rows], axis=0)


def tile_body(
    tile_ids, tile_len, targets, pictures, slot_grads, feats, planes, parts, upper, lower, grads, masks, left, right
):
    first, second = [
        Tile(
            tile, wide(tile_ids, tile), wide(tile_len, tile), feats, grads,
            *[planes.at[4 * tile + i] for i in range(4)], parts.at[tile],
        )
        for tile in range(TILES_DEV)
    ]
    first.opacities()
    second.opacities()
    for tile in (first, second):
        tile.log_transmittance(upper)
        tile.weights()
    for tile in (first, second):
        tile.picture(targets, pictures)
        tile.shares()
    for tile in (first, second):
        tile.later_shares(lower)
        tile.sums()
    for n in range(TILES_DEV * CHUNKS):
        spread(grads[:, pl.ds(n * LANES, LANES)], 16, masks, n * 256, left, n * LANES)
    total = dot_nt(left[...], right[...])
    for zc in range(16):
        slot_grads[zc] = total[16 * zc : 16 * zc + FEATS] + total[256 + 16 * zc : 256 + 16 * zc + FEATS]


Y_ARRIVAL = (0, 1, 7, 2, 6, 3, 5, 4)
ZC_ARRIVAL = (0, 1, 15, 2, 14, 3, 13, 4, 12, 5, 11, 6, 10, 7, 9, 8)
LAST = 7 * 256


def render_kernel(
    camera_hbm, ids_hbm, len_hbm, params_hbm, slots_hbm, lists_hbm, targets_hbm,
    pictures, view_grads, dense, saved, shape_rows, totals, colour,
    camera, tile_ids, tile_len, params, packed, lists, targets, slots, cams,
    table, outgoing, landed, staged, received, slot_grads, landed_back, staged_back, returned, every,
    feats, planes, parts, upper, lower, grads, masks, left, right, view_masks, view_left, view_right,
    load_sem, send_y, recv_y, send_zc, recv_zc, send_zc2, recv_zc2, send_y2, recv_y2,
    send_slots, recv_slots, send_cams, recv_cams, send_view, recv_view,
):
    cell, view = lax.axis_index("cell"), lax.axis_index("view")
    my_y, my_zc = cell // ZC_DEVS, lax.rem(cell, ZC_DEVS)
    barrier, greetings = greet(my_y, my_zc, view)

    pieces = [(first, min(8, ROWS - first)) for first in range(0, ROWS, 8)]
    loads = [
        pltpu.make_async_copy(params_hbm.at[pl.ds(*piece)], params.at[pl.ds(*piece)], load_sem.at[i])
        for i, piece in enumerate(pieces)
    ]
    side_loads = [
        pltpu.make_async_copy(source, target, load_sem.at[8 + i])
        for i, (source, target) in enumerate(
            (
                (camera_hbm, camera),
                (slots_hbm, slots.at[0]),
                (lists_hbm, lists),
                (targets_hbm, targets),
                (ids_hbm, tile_ids),
                (len_hbm, tile_len),
            )
        )
    ]
    for load in loads[:2] + side_loads[:2] + loads[2:] + side_loads[2:]:
        load.start()
    table[...] = jnp.zeros_like(table)
    feats[...] = jnp.zeros_like(feats)
    grads[...] = jnp.zeros_like(grads)

    def unpack(group, size):
        for chunk in range(16):
            packed[pl.ds(group * 16 + chunk * 8, size), :] = params[pl.ds(group, size), pl.ds(chunk * LANES, LANES)]
        for row in range(group, group + size):
            for half in range(2):
                dense[2 * row + half] = packed[pl.ds((row // 8) * 128 + half * 8 + row % 8, 8, stride=16), :]

    def loader(half):
        return lambda row: dense[2 * row + half]

    def load_pieces(first, last):
        for load, piece in list(zip(loads, pieces))[first:last]:
            load.wait()
            unpack(*piece)

    def put_features(first, features, half):
        for f, feature in enumerate(features):
            table[pl.ds(half * 16 + first + f, 8, stride=32), :] = feature

    side_loads[0].wait()
    shift = [wide(camera, i) for i in range(3)]
    shift_row = lax.broadcasted_iota(jnp.int32, (8, LANES), 0)
    cams[0] = jnp.where(shift_row == 0, shift[0], jnp.where(shift_row == 1, shift[1], shift[2]))
    load_pieces(0, 2)
    for half in range(2):
        load = loader(half)
        matrix, scales, unit_q, inv_norm = shape_matrix([load(3 + i) for i in range(3)], [load(6 + i) for i in range(4)])
        for i, value in enumerate(matrix + scales + unit_q + [inv_norm]):
            shape_rows[half * SHAPE_ROWS + i] = value
        put_features(0, keep_geometry(load, shift, matrix, saved, half * KEPT), half)
    load_pieces(2, 8)
    for half in range(2):
        put_features(6, keep_colours(loader(half), saved, half * KEPT), half)

    side_loads[1].wait()
    pl.semaphore_wait(barrier, greetings)
    y_sends = {}
    for k in Y_ORDER + (0,):
        peer, device_id = y_peer(my_y, my_zc, k)
        for half in range(2):
            chunk = 2 * peer + half
            top, bottom = gather_chunk(table, slots[0, pl.ds(chunk, 1), :])
            outgoing[chunk, pl.ds(0, 8), :] = top
            outgoing[chunk, pl.ds(8, 1), :] = bottom[0:1]
        if k:
            y_sends[k] = remote(
                outgoing.at[pl.ds(2 * peer, 2)], landed.at[pl.ds(2 * k, 2)],
                send_y.at[k - 1], recv_y.at[k - 1], device_id,
            )
    landed[pl.ds(0, 2)] = outgoing[pl.ds(2 * my_y, 2)]
    side_sends = []
    for k in VIEW_ORDER:
        peer = view_peer(view, k)
        side_sends.append(remote(slots.at[0], slots.at[k], send_slots.at[k - 1], recv_slots.at[k - 1], peer))
        side_sends.append(remote(cams.at[0], cams.at[k], send_cams.at[k - 1], recv_cams.at[k - 1], peer))

    fill_triangles(upper, lower)
    for load in side_loads[2:]:
        load.wait()
    for tile in range(TILES_DEV):
        for chunk in range(ENTRIES // LANES):
            n = tile * (ENTRIES // LANES) + chunk
            high, low = entry_slot(lists, my_y, tile, chunk)
            fill_masks(high, 16, masks, n * 256)
            right[:, pl.ds(n * LANES, LANES)] = hot_rows(low, LANES)

    def view_factors(k):
        for p, step in enumerate(Y_ARRIVAL):
            for half in range(2):
                n = 2 * p + half
                index = slots[k, pl.ds(2 * lax.rem(my_y + Y_DEVS - step, Y_DEVS) + half, 1), :]
                fill_masks(index >> 8, 8, view_masks, (k * 16 + n) * 128)
                view_right[k, :, pl.ds(n * LANES, LANES)] = hot_rows(index & 255, 256)

    blocks = [jnp.zeros((FEATS, LANES), F32)] * ZC_DEVS
    group = lax.broadcasted_iota(jnp.int32, (FEATS, LANES), 1) // 16
    for k in Y_ARRIVAL:
        if k:
            y_sends[k].wait()
        for zc in range(ZC_DEVS):
            rows = landed[2 * k + zc // 8]
            turn = 16 * ((k - zc) % 8)
            blocks[zc] = jnp.where(group == k, pltpu.roll(rows, turn, 1) if turn else rows, blocks[zc])
    for zc in range(ZC_DEVS):
        staged[zc] = blocks[zc]
    zc_sends = {}
    for k in ZC_ORDER:
        peer, device_id = zc_peer(my_y, my_zc, k)
        zc_sends[k] = remote(
            staged.at[peer], received.at[my_zc], send_zc.at[k - 1], recv_zc.at[k - 1], device_id
        )
    received[my_zc] = staged[my_zc]

    view_factors(0)
    for copy in side_sends:
        copy.wait()

    def view_forward(k):
        for half in range(2):
            shift = [jnp.broadcast_to(cams[k, pl.ds(i, 1), :], (8, LANES)) for i in range(3)]
            matrix = [shape_rows[half * SHAPE_ROWS + i] for i in range(9)]
            keep_geometry(loader(half), shift, matrix, saved, (2 * k + half) * KEPT)
            keep_colours(loader(half), saved, (2 * k + half) * KEPT)
        view_factors(k)

    places = [entry_slot(lists, my_y, n // 4, n % 4) for n in range(8)]
    places = [(jnp.broadcast_to(high, (8, LANES)), jnp.broadcast_to(low, (8, LANES))) for high, low in places]
    tops = [jnp.zeros((8, LANES), F32)] * 8
    bottoms = [jnp.zeros((8, LANES), F32)] * 8
    for k in ZC_ARRIVAL:
        if k:
            zc_sends[k].wait()
        source = lax.rem(my_zc + ZC_DEVS - k, ZC_DEVS)
        top = received[source, pl.ds(0, 8), :]
        bottom = jnp.broadcast_to(received[source, pl.ds(8, 1), :], (8, LANES))
        for n, (high, low) in enumerate(places):
            here = high == source
            tops[n] = jnp.where(here, lane_gather(top, low), tops[n])
            bottoms[n] = jnp.where(here, lane_gather(bottom, low), bottoms[n])
    for n in range(8):
        feats[pl.ds(0, 8), pl.ds(n * LANES, LANES)] = tops[n]
        feats[pl.ds(8, 8), pl.ds(n * LANES, LANES)] = bottoms[n]

    tile_body(
        tile_ids, tile_len, targets, pictures, slot_grads,
        feats, planes, parts, upper, lower, grads, masks, left, right,
    )

    for k in ZC_ORDER:
        peer, device_id = zc_peer(my_y, my_zc, k)
        zc_sends[k] = remote(
            slot_grads.at[peer], landed_back.at[my_zc], send_zc2.at[k - 1], recv_zc2.at[k - 1], device_id
        )
    landed_back[my_zc] = slot_grads[my_zc]
    view_forward(1)
    view_forward(2)
    for k in ZC_ORDER[::-1]:
        zc_sends[k].wait()

    def to_y(j, half, rows):
        staged_back[2 * j + half] = rows

    regroup(lambda i, half: landed_back[8 * half + i], to_y)
    view_sends = {}
    for k in Y_ORDER:
        peer, device_id = y_peer(my_y, my_zc, k)
        y_sends[k] = remote(
            staged_back.at[pl.ds(2 * (Y_DEVS - k), 2)], returned.at[pl.ds(2 * my_y, 2)],
            send_y2.at[k - 1], recv_y2.at[k - 1], device_id,
        )
    returned[pl.ds(2 * my_y, 2)] = staged_back[pl.ds(0, 2)]

    def add_left(k, p, block):
        for half in range(2):
            n = 2 * p + half
            values = jnp.concatenate(
                [block(half, 0, 8), jnp.broadcast_to(block(half, 8, 1), (8, LANES))], axis=0
            )
            spread(values, 8, view_masks, (k * 16 + n) * 128, view_left.at[k], n * LANES)

    def scatter(k, columns, first):
        product = dot_nt(view_left[k, :, columns], view_right[k, :, columns])
        for half in range(2):
            lanes = slice(half * LANES, (half + 1) * LANES)
            rows = pl.ds((2 * k + half) * 128, 128)
            value = product[0:128, lanes] + product[128:256, lanes]
            view_grads[rows, :] = value if first else view_grads[rows, :] + value

    for p, step in enumerate(Y_ARRIVAL):
        if step:
            y_sends[step].wait()
        y = lax.rem(my_y + Y_DEVS - step, Y_DEVS)
        for k in VIEW_ORDER:
            view_sends[k, p] = remote(
                returned.at[pl.ds(2 * y, 2)], every.at[k, pl.ds(2 * p, 2)],
                send_view.at[k - 1, p], recv_view.at[k - 1, p], view_peer(view, k),
            )
        add_left(0, p, lambda half, row, size, y=y: returned[2 * y + half, pl.ds(row, size), :])
        if p == 0:
            view_forward(3)
    scatter(0, pl.ds(0, G_DEV), True)
    for half in range(2):
        matrix = [shape_rows[half * SHAPE_ROWS + i] for i in range(9)]
        sums, colours = pull_view(loader(half), slot_rows(view_grads, 0, half), matrix, saved, half * KEPT)
        for i, value in enumerate(sums):
            totals[half * SUMS + i] = value
        for i, value in enumerate(colours):
            colour[half * 3 + i] = value
    for p in range(8):
        for k in (1, 3, 2):
            view_sends[k, p].wait()
            add_left(k, p, lambda half, row, size: every[k, 2 * p + half, pl.ds(row, size), :])
        if p == 6:
            for k in (1, 3, 2):
                scatter(k, pl.ds(0, LAST), True)
    for k in (1, 3, 2):
        scatter(k, pl.ds(LAST, 256), False)


SUMS = 13


def slot_rows(view_grads, view, half):
    return lambda f: view_grads[pl.ds((2 * view + half) * 128 + f, 8, stride=16), :]


def finish_kernel(
    pictures, view_grads, dense, saved, shape_rows, totals, colour_mine,
    pictures_hbm, gradient_hbm,
    gradient, packed, colour, sums, sems,
):
    groups = [(first, min(8, ROWS - first)) for first in range(0, ROWS, 8)]
    copies = [
        pltpu.make_async_copy(gradient.at[pl.ds(*group)], gradient_hbm.at[pl.ds(*group)], sems.at[i])
        for i, group in enumerate(groups)
    ]
    copies.append(pltpu.make_async_copy(pictures, pictures_hbm, sems.at[8]))
    copies[8].start()

    def put(row, half, value):
        packed[pl.ds((row // 8) * 128 + half * 8 + row % 8, 8, stride=16), :] = value

    def send(i):
        first, size = groups[i]
        for chunk in range(16):
            gradient[pl.ds(first, size), pl.ds(chunk * LANES, LANES)] = packed[
                pl.ds(first * 16 + chunk * 8, size), :
            ]
        copies[i].start()

    def put_harmonic(row, half):
        channel, j = divmod(row - 11, 16)
        parts = [colour[(2 * k + half) * 3 + channel] for k in range(VIEW_DEVS)]
        if j:
            parts = [saved[(2 * k + half) * KEPT + 21 + j] * parts[k] for k in range(VIEW_DEVS)]
        total = parts[0] + parts[1] + parts[2] + parts[3]
        put(row, half, total if j else sh_first * total)

    for half in range(2):
        load = lambda row: dense[2 * row + half]
        matrix = [shape_rows[half * SHAPE_ROWS + i] for i in range(9)]
        total = [totals[half * SUMS + i] for i in range(SUMS)]
        for i in range(3):
            colour[half * 3 + i] = colour_mine[half * 3 + i]
        for k in range(1, VIEW_DEVS):
            place = 2 * k + half
            values, colours = pull_view(load, slot_rows(view_grads, k, half), matrix, saved, place * KEPT)
            total = [old + value for old, value in zip(total, values)]
            for i, value in enumerate(colours):
                colour[place * 3 + i] = value
        for i, value in enumerate(total):
            sums[half * SUMS + i] = value
    for i in range(2, 8):
        first, size = groups[i]
        for row in range(first, first + size):
            for half in range(2):
                put_harmonic(row, half)
        send(i)
    for half in range(2):
        total = [sums[half * SUMS + i] for i in range(SUMS)]
        shape = [shape_rows[half * SHAPE_ROWS + i] for i in range(SHAPE_ROWS)]
        matrix, scales, unit_q, inv_norm = shape[0:9], shape[9:12], shape[12:16], shape[16]
        for i in range(3):
            put(i, half, total[i])
            put(3 + i, half, total[3 + i] * matrix[i] + total[6 + i] * matrix[3 + i] + total[9 + i] * matrix[6 + i])
        _, pull_back = jax.vjp(rotation_of, *unit_q)
        g_unit = pull_back([total[3 + 3 * i + j] * scales[j] for i in range(3) for j in range(3)])
        along = unit_q[0] * g_unit[0] + unit_q[1] * g_unit[1] + unit_q[2] * g_unit[2] + unit_q[3] * g_unit[3]
        for i in range(4):
            put(6 + i, half, inv_norm * (g_unit[i] - unit_q[i] * along))
        put(10, half, total[12] * (1.0 / (1.0 + jnp.exp(dense[20 + half]))))
        for row in range(11, 16):
            put_harmonic(row, half)
    send(0)
    send(1)
    for copy in copies:
        copy.wait()


def finish_call(operands):
    vmem = pl.BlockSpec(memory_space=pltpu.VMEM)
    anywhere = pl.BlockSpec(memory_space=pl.ANY)
    tile = (8, LANES)
    return pl.pallas_call(
        finish_kernel,
        out_shape=(
            jax.ShapeDtypeStruct(operands[0].shape, F32),
            jax.ShapeDtypeStruct((ROWS, G_DEV), F32),
        ),
        in_specs=[vmem] * len(operands),
        out_specs=(anywhere, anywhere),
        scratch_shapes=[
            pltpu.VMEM((ROWS, G_DEV), F32),
            pltpu.VMEM((64 * 16, LANES), F32),
            pltpu.VMEM((VIEW_DEVS * 2 * 3,) + tile, F32),
            pltpu.VMEM((2 * SUMS,) + tile, F32),
            pltpu.SemaphoreType.DMA((9,)),
        ],
        compiler_params=pltpu.CompilerParams(vmem_limit_bytes=8 * 2**20),
        name="finish",
    )(*operands)


def render_call(camera, tile_ids, tile_len, params, slots, lists, targets):
    anywhere = pl.BlockSpec(memory_space=pl.ANY)
    blocks = pltpu.VMEM((16, FEATS, LANES), F32)
    tile = (8, LANES)
    y_sems = [pltpu.SemaphoreType.DMA((Y_DEVS - 1,))] * 2
    zc_sems = [pltpu.SemaphoreType.DMA((ZC_DEVS - 1,))] * 2
    view_sems = [pltpu.SemaphoreType.DMA((VIEW_DEVS - 1,))] * 2
    return pl.pallas_call(
        render_kernel,
        out_shape=(
            pltpu.VMEM(targets.shape, F32),
            pltpu.VMEM((VIEW_DEVS * 256, LANES), F32),
            pltpu.VMEM((2 * ROWS,) + tile, F32),
            pltpu.VMEM((VIEW_DEVS * 2 * KEPT,) + tile, F32),
            pltpu.VMEM((2 * SHAPE_ROWS,) + tile, F32),
            pltpu.VMEM((2 * SUMS,) + tile, F32),
            pltpu.VMEM((2 * 3,) + tile, F32),
        ),
        in_specs=[anywhere] * 7,
        out_specs=(pl.BlockSpec(memory_space=pltpu.VMEM),) * 7,
        scratch_shapes=[
            pltpu.VMEM(camera.shape, F32),
            pltpu.VMEM(tile_ids.shape, jnp.int32),
            pltpu.VMEM(tile_len.shape, jnp.int32),
            pltpu.VMEM((ROWS, G_DEV), F32),
            pltpu.VMEM((64 * 16, LANES), F32),
            pltpu.VMEM(lists.shape, jnp.int32),
            pltpu.VMEM(targets.shape, F32),
            pltpu.VMEM((VIEW_DEVS, 16, LANES), jnp.int32),
            pltpu.VMEM((VIEW_DEVS,) + tile, F32),
            pltpu.VMEM((256, LANES), F32),
        ]
        + [blocks] * 8
        + [
            pltpu.VMEM((VIEW_DEVS, 16, FEATS, LANES), F32),
            pltpu.VMEM((16, TILES_DEV * ENTRIES), F32),
            pltpu.VMEM((4 * TILES_DEV, PIXELS, ENTRIES), F32),
            pltpu.VMEM((TILES_DEV, PIXELS, 2 * ENTRIES), BF16),
            pltpu.VMEM((1024, 256), BF16),
            pltpu.VMEM((1024, 256), BF16),
            pltpu.VMEM((16, TILES_DEV * ENTRIES), F32),
            pltpu.VMEM((8 * 256, LANES), BF16),
            pltpu.VMEM((512, TILES_DEV * ENTRIES), BF16),
            pltpu.VMEM((LANES, TILES_DEV * ENTRIES), BF16),
            pltpu.VMEM((VIEW_DEVS * 16 * 128, LANES), BF16),
            pltpu.VMEM((VIEW_DEVS, 256, G_DEV), BF16),
            pltpu.VMEM((VIEW_DEVS, 256, G_DEV), BF16),
            pltpu.SemaphoreType.DMA((14,)),
        ]
        + y_sems + zc_sems + zc_sems + y_sems + view_sems + view_sems
        + [pltpu.SemaphoreType.DMA((VIEW_DEVS - 1, 8))] * 2,
        compiler_params=pltpu.CompilerParams(
            collective_id=0, has_side_effects=True, vmem_limit_bytes=40 * 2**20
        ),
        name="render",
    )(
        *[
            pltpu.with_memory_space_constraint(operand, pltpu.HBM)
            for operand in (camera, tile_ids, tile_len, params, slots, lists, targets)
        ]
    )


def local(params, cameras, targets, tile_ids, send_slots, tile_lists, tile_len):
    partial = render_call(
        cameras, tile_ids, tile_len, params, send_slots.reshape(16, LANES), tile_lists,
        jnp.transpose(targets, (0, 2, 1, 3)),
    )
    pictures, gradient = finish_call(partial)
    return jnp.transpose(pictures, (0, 2, 1, 3)), gradient


def solution(mesh):
    return jax.shard_map(
        local,
        mesh=mesh,
        in_specs=(
            P(None, "cell"),
            P("view", None),
            P("view", "cell", None, None),
            P("view", "cell"),
            P("view", "cell", None),
            P("view", "cell", None),
            P("view", "cell"),
        ),
        out_specs=(P("view", "cell", None, None), P(None, "cell")),
        check_vma=False,
    )
```

```python
import jax
import jax.numpy as jnp
from jax import lax
from jax.experimental import pallas as pl
from jax.experimental.pallas import tpu as pltpu
from jax.sharding import PartitionSpec as P

TILE_SIDE = 16
TILE_COLS = 32
LANES = 128
Y_DEVS = 8
ZC_DEVS = 16
VIEW_DEVS = 4
FEATS = 9
Y_ORDER = (4, 3, 5, 2, 6, 1, 7)
ZC_ORDER = (8, 9, 7, 6, 10, 5, 11, 4, 12, 3, 13, 2, 14, 1, 15)
VIEW_ORDER = (2, 1, 3)
ENTRIES = 512
CHUNKS = ENTRIES // LANES
HALF = ENTRIES // 2
TILES_DEV = 2
PIXELS = 256
ROWS = 59
G_DEV = 2048
LOG2_E = 1.4426950408889634
F32 = jnp.float32
BF16 = jnp.bfloat16

focal_length = 800.0
dilation = 0.3
sh_first = 0.28209479177387814
sh_second = 0.4886025119029199
sh_third = (
    1.0925484305920792,
    -1.0925484305920792,
    0.31539156525252005,
    -1.0925484305920792,
    0.5462742152960396,
)
sh_fourth = (
    -0.5900435899266435,
    2.890611442640554,
    -0.4570457994644658,
    0.3731763325901154,
    -0.4570457994644658,
    1.445305721320277,
    -0.5900435899266435,
)


def split2(value):
    high = value.astype(BF16)
    return high, (value - high.astype(F32)).astype(BF16)


def dot_nt(lhs, rhs):
    return lax.dot_general(lhs, rhs, (((1,), (1,)), ((), ())), preferred_element_type=F32)


def dot_nn(lhs, rhs):
    return lax.dot_general(lhs, rhs, (((1,), (0,)), ((), ())), preferred_element_type=F32)


def rotation_of(q_w, q_x, q_y, q_z):
    return [
        1.0 - 2.0 * (q_y * q_y + q_z * q_z),
        2.0 * (q_x * q_y - q_w * q_z),
        2.0 * (q_x * q_z + q_w * q_y),
        2.0 * (q_x * q_y + q_w * q_z),
        1.0 - 2.0 * (q_x * q_x + q_z * q_z),
        2.0 * (q_y * q_z - q_w * q_x),
        2.0 * (q_x * q_z - q_w * q_y),
        2.0 * (q_y * q_z + q_w * q_x),
        1.0 - 2.0 * (q_x * q_x + q_y * q_y),
    ]


def unit_quaternion(quaternion):
    total = sum(part * part for part in quaternion[1:]) + quaternion[0] * quaternion[0]
    inverse = lax.rsqrt(total)
    return [part * inverse for part in quaternion], inverse


def shape_matrix(log_scales, quaternion):
    scales = [jnp.exp(part) for part in log_scales]
    unit, inverse = unit_quaternion(quaternion)
    rotation = rotation_of(*unit)
    matrix = [rotation[3 * i + j] * scales[j] for i in range(3) for j in range(3)]
    return matrix, scales, unit, inverse


def harmonics(x, y, z):
    xx, yy, zz = x * x, y * y, z * z
    rim = 4.0 * zz - xx - yy
    gap = xx - yy
    return [
        -sh_second * y,
        sh_second * z,
        -sh_second * x,
        sh_third[0] * (x * y),
        sh_third[1] * (y * z),
        sh_third[2] * (2.0 * zz - xx - yy),
        sh_third[3] * (x * z),
        sh_third[4] * gap,
        sh_fourth[0] * (y * (3.0 * xx - yy)),
        sh_fourth[1] * (x * y * z),
        sh_fourth[2] * (y * rim),
        sh_fourth[3] * (z * (2.0 * zz - 3.0 * xx - 3.0 * yy)),
        sh_fourth[4] * (x * rim),
        sh_fourth[5] * (z * gap),
        sh_fourth[6] * (x * (xx - 3.0 * yy)),
    ]


def geometry(pos, matrix):
    x, y, z = pos
    inv_z = 1.0 / z
    jac = focal_length * inv_z
    screen_x = x * jac
    screen_y = y * jac
    jac_x = -screen_x * inv_z
    jac_y = -screen_y * inv_z
    row_u = [jac * matrix[j] + jac_x * matrix[6 + j] for j in range(3)]
    row_v = [jac * matrix[3 + j] + jac_y * matrix[6 + j] for j in range(3)]
    cov_a = row_u[0] * row_u[0] + row_u[1] * row_u[1] + row_u[2] * row_u[2] + dilation
    cov_c = row_v[0] * row_v[0] + row_v[1] * row_v[1] + row_v[2] * row_v[2] + dilation
    cov_b = row_u[0] * row_v[0] + row_u[1] * row_v[1] + row_u[2] * row_v[2]
    inv_det = 1.0 / (cov_a * cov_c - cov_b * cov_b)
    return inv_z, jac, screen_x, screen_y, jac_x, jac_y, row_u, row_v, cov_a, cov_b, cov_c, inv_det


def direction(pos):
    x, y, z = pos
    inverse = lax.rsqrt(x * x + y * y + z * z)
    return [x * inverse, y * inverse, z * inverse], inverse


def raw_colour(load, channel, basis):
    total = load(11 + 16 * channel) * sh_first
    for j in range(15):
        total = total + load(12 + 16 * channel + j) * basis[j]
    return total + 0.5


KEPT = 40
SHAPE_ROWS = 17


def keep_geometry(load, shift, matrix, saved, base):
    pos = [load(i) - shift[i] for i in range(3)]
    inv_z, jac, screen_x, screen_y, jac_x, jac_y, row_u, row_v, cov_a, cov_b, cov_c, inv_det = geometry(pos, matrix)
    unit, inv_len = direction(pos)
    values = [pos[0], pos[1], inv_z, jac, screen_x, screen_y, jac_x, jac_y]
    values += row_u + row_v + [cov_a, cov_b, cov_c, inv_det] + unit + [inv_len] + harmonics(*unit)
    for i, value in enumerate(values):
        saved[base + i] = value
    opacity = 1.0 / (1.0 + jnp.exp(-load(10)))
    return [screen_x, screen_y, cov_c * inv_det, -cov_b * inv_det, cov_a * inv_det, opacity]


def keep_colours(load, saved, base):
    basis = [saved[base + 22 + j] for j in range(15)]
    raw = [raw_colour(load, channel, basis) for channel in range(3)]
    for channel, value in enumerate(raw):
        saved[base + 37 + channel] = jnp.where(value > 0.0, 1.0, jnp.where(value < 0.0, 0.0, 0.5))
    return [jnp.maximum(value, 0.0) for value in raw]


def pull_view(load, slot, matrix, saved, base):
    kept = lambda i: saved[base + i]
    inv_z, jac, screen_x, screen_y, jac_x, jac_y = [kept(2 + i) for i in range(6)]
    row_u, row_v = [kept(8 + i) for i in range(3)], [kept(11 + i) for i in range(3)]
    cov_a, cov_b, cov_c, inv_det = [kept(14 + i) for i in range(4)]
    g_a, g_b, g_c = slot(2), slot(3), slot(4)
    g_det = -(g_a * cov_c - g_b * cov_b + g_c * cov_a) * inv_det * inv_det
    d_a = 2.0 * (g_c * inv_det + g_det * cov_c)
    d_c = 2.0 * (g_a * inv_det + g_det * cov_a)
    d_b = -g_b * inv_det - 2.0 * g_det * cov_b
    g_u = [d_a * row_u[j] + d_b * row_v[j] for j in range(3)]
    g_v = [d_c * row_v[j] + d_b * row_u[j] for j in range(3)]
    g_matrix = [jac * g_u[j] for j in range(3)] + [jac * g_v[j] for j in range(3)]
    g_matrix += [jac_x * g_u[j] + jac_y * g_v[j] for j in range(3)]
    g_jac = g_u[0] * matrix[0] + g_v[0] * matrix[3]
    for j in (1, 2):
        g_jac = g_jac + (g_u[j] * matrix[j] + g_v[j] * matrix[3 + j])
    g_jac_x = g_u[0] * matrix[6] + g_u[1] * matrix[7] + g_u[2] * matrix[8]
    g_jac_y = g_v[0] * matrix[6] + g_v[1] * matrix[7] + g_v[2] * matrix[8]
    g_sx = slot(0) - inv_z * g_jac_x
    g_sy = slot(1) - inv_z * g_jac_y
    g_inv = focal_length * (g_jac + kept(0) * g_sx + kept(1) * g_sy) - screen_x * g_jac_x - screen_y * g_jac_y
    g_pos = [jac * g_sx, jac * g_sy, -inv_z * inv_z * g_inv]

    g_colours = [slot(6 + channel) * kept(37 + channel) for channel in range(3)]
    g_basis = []
    for j in range(15):
        terms = [load(12 + 16 * channel + j) * g_colours[channel] for channel in range(3)]
        g_basis.append(terms[0] + terms[1] + terms[2])
    unit, inv_len = [kept(18 + i) for i in range(3)], kept(21)
    _, pull = jax.vjp(harmonics, *unit)
    g_unit = pull(g_basis)
    along = unit[0] * g_unit[0] + unit[1] * g_unit[1] + unit[2] * g_unit[2]
    for i in range(3):
        g_pos[i] = g_pos[i] + inv_len * (g_unit[i] - unit[i] * along)
    return g_pos + g_matrix + [slot(5)], g_colours


def lane_gather(source, index):
    return jnp.take_along_axis(source, index, axis=1, mode="promise_in_bounds")


def gather_chunk(table, index):
    shape = (8, LANES)
    low = jnp.broadcast_to(index & 127, shape)
    high = jnp.broadcast_to(index >> 7, shape)
    top = bottom = jnp.zeros(shape, F32)
    for chunk in range(16):
        here = high == chunk
        top = jnp.where(here, lane_gather(table[pl.ds(16 * chunk, 8), :], low), top)
        bottom = jnp.where(here, lane_gather(table[pl.ds(16 * chunk + 8, 8), :], low), bottom)
    return top, bottom


def remote(src_ref, dst_ref, send_sem, recv_sem, device_id):
    copy = pltpu.make_async_remote_copy(
        src_ref=src_ref,
        dst_ref=dst_ref,
        send_sem=send_sem,
        recv_sem=recv_sem,
        device_id=device_id,
        device_id_type=pl.DeviceIdType.MESH,
    )
    copy.start()
    return copy


def y_peer(my_y, my_zc, k):
    peer = lax.rem(my_y + k, Y_DEVS)
    return peer, {"cell": peer * ZC_DEVS + my_zc}


def zc_peer(my_y, my_zc, k):
    peer = lax.rem(my_zc + k, ZC_DEVS)
    return peer, {"cell": my_y * ZC_DEVS + peer}


def view_peer(view, k):
    return {"view": lax.rem(view + k, VIEW_DEVS)}


def greet(my_y, my_zc, view):
    barrier = pltpu.get_barrier_semaphore()
    peers = [y_peer(my_y, my_zc, k)[1] for k in Y_ORDER]
    peers += [zc_peer(my_y, my_zc, k)[1] for k in ZC_ORDER]
    peers += [view_peer(view, k) for k in VIEW_ORDER]
    for peer in peers:
        pl.semaphore_signal(barrier, inc=1, device_id=peer, device_id_type=pl.DeviceIdType.MESH)
    return barrier, len(peers)


def part_lanes(chunk):
    base = (chunk // 2) * 512 + (chunk % 2) * LANES
    return pl.ds(base, LANES), pl.ds(base + 256, LANES)


def fill_triangles(upper, lower):
    row = lax.broadcasted_iota(jnp.int32, (256, 256), 0)
    col = lax.broadcasted_iota(jnp.int32, (256, 256), 1)
    above = jnp.where(row < col, 1.0, 0.0).astype(BF16)
    below = jnp.where(row > col, 1.0, 0.0).astype(BF16)
    ones = jnp.ones((256, 256), BF16)
    for i in range(4):
        upper[pl.ds(256 * i, 256), :] = ones if i < 2 else above
        lower[pl.ds(256 * i, 256), :] = below if i < 2 else ones


def entry_slot(lists, my_y, tile, chunk):
    index = lists[0, pl.ds(tile, 1), pl.ds(chunk * LANES, LANES)]
    steps = (my_y - (index >> 8)) & (Y_DEVS - 1)
    return (index >> 4) & 15, (steps << 4) | (index & 15)


def hot_rows(index, count):
    shape = (count, LANES)
    return jnp.where(
        jnp.broadcast_to(index, shape) == lax.broadcasted_iota(jnp.int32, shape, 0), 1.0, 0.0
    ).astype(BF16)


def fill_masks(high, count, masks, base):
    high = jnp.broadcast_to(high, (16, LANES))
    for value in range(count):
        masks[pl.ds(base + 16 * value, 16), :] = jnp.where(high == value, 1.0, 0.0).astype(BF16)


def spread(values, count, masks, base, left, column):
    for i, piece in enumerate(split2(values)):
        for value in range(count):
            left[pl.ds((i * count + value) * 16, 16), pl.ds(column, LANES)] = (
                masks[pl.ds(base + 16 * value, 16), :] * piece
            )


class Tile:
    def __init__(self, tile, number, length, feats, grads, alpha, ratio, plane, weight, part):
        self.tile, self.length, self.feats, self.grads = tile, length, feats, grads
        self.alpha, self.ratio, self.plane, self.weight, self.part = alpha, ratio, plane, weight, part
        self.whole = pl.ds(tile * ENTRIES, ENTRIES)
        left_x = twice((TILE_SIDE * (number & (TILE_COLS - 1))).astype(F32) + 0.5)
        self.top_y = (TILE_SIDE * (number >> 5)).astype(F32) + 0.5
        self.pixel_x = lax.broadcasted_iota(jnp.int32, (TILE_SIDE, LANES), 0).astype(F32) + left_x

    def row_of(self, f, chunk):
        return self.feats[pl.ds(f, 1), pl.ds(self.tile * ENTRIES + chunk * LANES, LANES)]

    def feature(self, f, chunk):
        return jnp.broadcast_to(self.row_of(f, chunk), (8, LANES))

    def each_row(self, body, carry):
        def one_row(y, carry):
            rows = pl.ds(pl.multiple_of(y * TILE_SIDE, TILE_SIDE), TILE_SIDE)
            return body(y.astype(F32), rows, carry)

        return lax.fori_loop(0, TILE_SIDE, one_row, carry, unroll=TILE_SIDE)

    def opacities(self):
        for chunk in range(CHUNKS):
            lanes = pl.ds(chunk * LANES, LANES)
            high, low = part_lanes(chunk)
            lane = lax.broadcasted_iota(jnp.int32, (8, LANES), 1) + chunk * LANES
            log_opacity = jnp.where(lane < self.length, jnp.log2(self.feature(5, chunk)), -1e30)
            delta_x = twice(self.feature(0, chunk)) - self.pixel_x
            part_x = twice((-0.5 * LOG2_E) * self.feature(2, chunk)) * delta_x * delta_x + twice(log_opacity)
            cross = twice(-LOG2_E * self.feature(3, chunk)) * delta_x
            screen_y = self.feature(1, chunk) - self.top_y
            conic_c = (-0.5 * LOG2_E) * self.feature(4, chunk)

            def body(y, rows, carry):
                delta_y = screen_y - y
                part_y = conic_c * delta_y * delta_y
                value = jnp.exp2(part_x + cross * twice(delta_y) + twice(part_y))
                keep = jnp.log2(1.0 - value)
                self.alpha[rows, lanes] = value
                self.ratio[rows, lanes] = value * jnp.exp2(-keep)
                self.part[rows, high], self.part[rows, low] = split2(keep)
                return carry

            self.each_row(body, 0)

    def log_transmittance(self, upper):
        self.plane[:, pl.ds(0, HALF)] = dot_nn(self.part[:, pl.ds(0, 512)], upper[pl.ds(512, 512), :])
        self.plane[:, pl.ds(HALF, HALF)] = dot_nn(self.part[...], upper[...])

    def weights(self):
        for chunk in range(CHUNKS):
            lanes = pl.ds(chunk * LANES, LANES)
            high, low = part_lanes(chunk)

            def body(y, rows, carry):
                value = jnp.exp2(self.plane[rows, lanes]) * self.alpha[rows, lanes]
                self.weight[rows, lanes] = value
                self.part[rows, high], self.part[rows, low] = split2(value)
                return carry

            self.each_row(body, 0)

    def picture(self, targets, pictures):
        colours = jnp.concatenate([self.feats[pl.ds(6, 3), self.whole], jnp.zeros((5, ENTRIES), F32)], axis=0)
        colour_hi = colours.astype(BF16).astype(F32)
        colour_lo = (colours - colour_hi).astype(BF16).astype(F32)
        both = jnp.concatenate([colour_hi, colour_lo], axis=0)
        both = jnp.concatenate([both[:, :HALF], both[:, :HALF], both[:, HALF:], both[:, HALF:]], axis=1)
        product = dot_nt(both.astype(BF16), self.part[...])
        picture = product[0:8] + product[8:16]
        pictures[0, :, self.tile, :] = picture[0:3]
        residual = picture - jnp.concatenate([targets[0, :, self.tile, :], jnp.zeros((5, PIXELS), F32)], axis=0)
        residual_hi = residual.astype(BF16).astype(F32)
        residual_lo = (residual - residual_hi).astype(BF16).astype(F32)
        pair = jnp.concatenate([residual_hi, residual_lo], axis=0).astype(BF16)
        product = dot_nn(pair, self.part[...])
        product = product[0:8] + product[8:16]
        self.grads[pl.ds(6, 3), self.whole] = jnp.concatenate(
            [product[0:3, 0:256] + product[0:3, 256:512], product[0:3, 512:768] + product[0:3, 768:1024]], axis=1
        )
        stack = jnp.concatenate([residual_hi, residual_lo, residual_hi, jnp.zeros((104, PIXELS), F32)], axis=0)
        rows24 = jnp.concatenate([colour_hi, colour_hi, colour_lo, jnp.zeros((104, ENTRIES), F32)], axis=0)
        self.plane[...] = dot_nn(jnp.transpose(stack).astype(BF16), rows24.astype(BF16))

    def shares(self):
        for chunk in range(CHUNKS):
            lanes = pl.ds(chunk * LANES, LANES)
            high, low = part_lanes(chunk)

            def body(y, rows, carry):
                value = self.plane[rows, lanes] * self.weight[rows, lanes]
                self.weight[rows, lanes] = value
                self.part[rows, high], self.part[rows, low] = split2(value)
                return carry

            self.each_row(body, 0)

    def later_shares(self, lower):
        self.plane[:, pl.ds(0, HALF)] = dot_nn(self.part[...], lower[...])
        self.plane[:, pl.ds(HALF, HALF)] = dot_nn(self.part[:, pl.ds(512, 512)], lower[pl.ds(0, 512), :])

    def sums(self):
        for chunk in range(CHUNKS):
            lanes = pl.ds(chunk * LANES, LANES)
            screen_y = self.feature(1, chunk) - self.top_y

            def body(y, rows, carry):
                sum_0, sum_1, sum_2 = carry
                delta_y = twice(screen_y - y)
                grad = self.weight[rows, lanes] - self.plane[rows, lanes] * self.ratio[rows, lanes]
                slope = grad * delta_y
                return sum_0 + grad, sum_1 + slope, sum_2 + slope * delta_y

            zero = jnp.zeros((TILE_SIDE, LANES), F32)
            sum_0, sum_1, sum_2 = self.each_row(body, (zero, zero, zero))
            delta_x = twice(self.feature(0, chunk)) - self.pixel_x
            over = lambda rows: jnp.sum(rows, axis=0, keepdims=True)
            first_x = over(delta_x * sum_0)
            first_y = over(sum_1)
            out = pl.ds(self.tile * ENTRIES + chunk * LANES, LANES)
            grads, row_of = self.grads, lambda f: self.row_of(f, chunk)
            grads[pl.ds(0, 1), out] = -row_of(2) * first_x - row_of(3) * first_y
            grads[pl.ds(1, 1), out] = -row_of(4) * first_y - row_of(3) * first_x
            grads[pl.ds(2, 1), out] = -0.5 * over(delta_x * delta_x * sum_0)
            grads[pl.ds(3, 1), out] = -over(delta_x * sum_1)
            grads[pl.ds(4, 1), out] = -0.5 * over(sum_2)
            grads[pl.ds(5, 1), out] = over(sum_0)


def wide(row, i):
    return jnp.broadcast_to(row[:, pl.ds(i, 1)], (8, LANES))


def twice(rows):
    return jnp.concatenate([rows, rows], axis=0)


def tile_body(
    tile_ids, tile_len, targets, pictures, slot_grads, feats, planes, parts, upper, lower, grads, masks, left, right
):
    first, second = [
        Tile(
            tile, wide(tile_ids, tile), wide(tile_len, tile), feats, grads,
            *[planes.at[4 * tile + i] for i in range(4)], parts.at[tile],
        )
        for tile in range(TILES_DEV)
    ]
    first.opacities()
    second.opacities()
    for tile in (first, second):
        tile.log_transmittance(upper)
        tile.weights()
    for tile in (first, second):
        tile.picture(targets, pictures)
        tile.shares()
    for tile in (first, second):
        tile.later_shares(lower)
        tile.sums()
    for n in range(TILES_DEV * CHUNKS):
        spread(grads[:, pl.ds(n * LANES, LANES)], 16, masks, n * 256, left, n * LANES)
    total = dot_nt(left[...], right[...])
    for zc in range(16):
        slot_grads[zc] = total[16 * zc : 16 * zc + FEATS] + total[256 + 16 * zc : 256 + 16 * zc + FEATS]


Y_ARRIVAL = (0, 1, 7, 2, 6, 3, 5, 4)
ZC_ARRIVAL = (0, 1, 15, 2, 14, 3, 13, 4, 12, 5, 11, 6, 10, 7, 9, 8)
LAST = 7 * 256


def render_kernel(
    camera_hbm, ids_hbm, len_hbm, params_hbm, slots_hbm, lists_hbm, targets_hbm,
    pictures, view_grads, dense, saved, shape_rows, totals, colour,
    camera, tile_ids, tile_len, params, packed, lists, targets, slots, turned, cams,
    table, outgoing, landed, staged, received, slot_grads, landed_back, staged_back, returned, every,
    feats, planes, parts, upper, lower, grads, masks, left, right, view_masks, view_left, view_right,
    load_sem, send_y, recv_y, send_zc, recv_zc, send_zc2, recv_zc2, send_y2, recv_y2,
    send_slots, recv_slots, send_cams, recv_cams, send_view, recv_view,
):
    cell, view = lax.axis_index("cell"), lax.axis_index("view")
    my_y, my_zc = cell // ZC_DEVS, lax.rem(cell, ZC_DEVS)
    barrier, greetings = greet(my_y, my_zc, view)

    pieces = [(first, min(8, ROWS - first)) for first in range(0, ROWS, 8)]
    loads = [
        pltpu.make_async_copy(params_hbm.at[pl.ds(*piece)], params.at[pl.ds(*piece)], load_sem.at[i])
        for i, piece in enumerate(pieces)
    ]
    side_loads = [
        pltpu.make_async_copy(source, target, load_sem.at[8 + i])
        for i, (source, target) in enumerate(
            (
                (camera_hbm, camera),
                (slots_hbm, slots.at[0]),
                (lists_hbm, lists),
                (targets_hbm, targets),
                (ids_hbm, tile_ids),
                (len_hbm, tile_len),
            )
        )
    ]
    for load in loads[:2] + side_loads[:2] + loads[2:] + side_loads[2:]:
        load.start()
    table[...] = jnp.zeros_like(table)
    feats[...] = jnp.zeros_like(feats)
    grads[...] = jnp.zeros_like(grads)

    def unpack(group, size):
        for chunk in range(16):
            packed[pl.ds(group * 16 + chunk * 8, size), :] = params[pl.ds(group, size), pl.ds(chunk * LANES, LANES)]
        for row in range(group, group + size):
            for half in range(2):
                dense[2 * row + half] = packed[pl.ds((row // 8) * 128 + half * 8 + row % 8, 8, stride=16), :]

    def loader(half):
        return lambda row: dense[2 * row + half]

    def load_pieces(first, last):
        for load, piece in list(zip(loads, pieces))[first:last]:
            load.wait()
            unpack(*piece)

    def put_features(first, features, half):
        for f, feature in enumerate(features):
            table[pl.ds(half * 16 + first + f, 8, stride=32), :] = feature

    side_loads[0].wait()
    shift = [wide(camera, i) for i in range(3)]
    shift_row = lax.broadcasted_iota(jnp.int32, (8, LANES), 0)
    cams[0] = jnp.where(shift_row == 0, shift[0], jnp.where(shift_row == 1, shift[1], shift[2]))
    load_pieces(0, 2)
    for half in range(2):
        load = loader(half)
        matrix, scales, unit_q, inv_norm = shape_matrix([load(3 + i) for i in range(3)], [load(6 + i) for i in range(4)])
        for i, value in enumerate(matrix + scales + unit_q + [inv_norm]):
            shape_rows[half * SHAPE_ROWS + i] = value
        put_features(0, keep_geometry(load, shift, matrix, saved, half * KEPT), half)
    load_pieces(2, 8)
    for half in range(2):
        put_features(6, keep_colours(loader(half), saved, half * KEPT), half)

    side_loads[1].wait()
    pl.semaphore_wait(barrier, greetings)
    y_sends = {}
    for k in Y_ORDER + (0,):
        peer, device_id = y_peer(my_y, my_zc, k)
        for half in range(2):
            chunk = 2 * peer + half
            top, bottom = gather_chunk(table, slots[0, pl.ds(chunk, 1), :])
            outgoing[chunk, pl.ds(0, 8), :] = top
            outgoing[chunk, pl.ds(8, 1), :] = bottom[0:1]
        if k:
            y_sends[k] = remote(
                outgoing.at[pl.ds(2 * peer, 2)], landed.at[pl.ds(2 * k, 2)],
                send_y.at[k - 1], recv_y.at[k - 1], device_id,
            )
    landed[pl.ds(0, 2)] = outgoing[pl.ds(2 * my_y, 2)]
    side_sends = []
    for k in VIEW_ORDER:
        peer = view_peer(view, k)
        side_sends.append(remote(slots.at[0], slots.at[k], send_slots.at[k - 1], recv_slots.at[k - 1], peer))
        side_sends.append(remote(cams.at[0], cams.at[k], send_cams.at[k - 1], recv_cams.at[k - 1], peer))

    fill_triangles(upper, lower)
    for load in side_loads[2:]:
        load.wait()
    for tile in range(TILES_DEV):
        for chunk in range(ENTRIES // LANES):
            n = tile * (ENTRIES // LANES) + chunk
            high, low = entry_slot(lists, my_y, tile, chunk)
            fill_masks(high, 16, masks, n * 256)
            right[:, pl.ds(n * LANES, LANES)] = hot_rows(low, LANES)

    def view_factors(k):
        even, odd = [slots[k, pl.ds(i, 8, stride=2), :] for i in range(2)]
        lane = lax.broadcasted_iota(jnp.int32, (8, LANES), 1)
        for half in range(2):
            owner = (my_zc - (8 * half + (lane >> 4))) & (ZC_DEVS - 1)
            column = ((owner & 7) << 4) | (lane & 15)
            turned[2 * k + half] = jnp.where(owner < 8, lane_gather(even, column), lane_gather(odd, column))
        for p, step in enumerate(Y_ARRIVAL):
            for half in range(2):
                n = 2 * p + half
                index = turned[2 * k + half, pl.ds(lax.rem(my_y + Y_DEVS - step, Y_DEVS), 1), :]
                fill_masks(index >> 8, 8, view_masks, (k * 16 + n) * 128)
                view_right[k, :, pl.ds(n * LANES, LANES)] = hot_rows(index & 255, 256)

    blocks = [jnp.zeros((FEATS, LANES), F32)] * ZC_DEVS
    group = lax.broadcasted_iota(jnp.int32, (FEATS, LANES), 1) // 16
    for k in Y_ARRIVAL:
        if k:
            y_sends[k].wait()
        for zc in range(ZC_DEVS):
            rows = landed[2 * k + zc // 8]
            turn = 16 * ((k - zc) % 8)
            blocks[zc] = jnp.where(group == k, pltpu.roll(rows, turn, 1) if turn else rows, blocks[zc])
    for zc in range(ZC_DEVS):
        staged[zc] = blocks[zc]
    zc_sends = {}
    for k in ZC_ORDER:
        peer, device_id = zc_peer(my_y, my_zc, k)
        zc_sends[k] = remote(
            staged.at[peer], received.at[my_zc], send_zc.at[k - 1], recv_zc.at[k - 1], device_id
        )
    received[my_zc] = staged[my_zc]

    view_factors(0)
    for copy in side_sends:
        copy.wait()

    def view_forward(k):
        for half in range(2):
            shift = [jnp.broadcast_to(cams[k, pl.ds(i, 1), :], (8, LANES)) for i in range(3)]
            matrix = [shape_rows[half * SHAPE_ROWS + i] for i in range(9)]
            keep_geometry(loader(half), shift, matrix, saved, (2 * k + half) * KEPT)
            keep_colours(loader(half), saved, (2 * k + half) * KEPT)
        view_factors(k)

    places = [entry_slot(lists, my_y, n // 4, n % 4) for n in range(8)]
    places = [(jnp.broadcast_to(high, (8, LANES)), jnp.broadcast_to(low, (8, LANES))) for high, low in places]
    tops = [jnp.zeros((8, LANES), F32)] * 8
    bottoms = [jnp.zeros((8, LANES), F32)] * 8
    for k in ZC_ARRIVAL:
        if k:
            zc_sends[k].wait()
        source = lax.rem(my_zc + ZC_DEVS - k, ZC_DEVS)
        top = received[source, pl.ds(0, 8), :]
        bottom = jnp.broadcast_to(received[source, pl.ds(8, 1), :], (8, LANES))
        for n, (high, low) in enumerate(places):
            here = high == source
            tops[n] = jnp.where(here, lane_gather(top, low), tops[n])
            bottoms[n] = jnp.where(here, lane_gather(bottom, low), bottoms[n])
    for n in range(8):
        feats[pl.ds(0, 8), pl.ds(n * LANES, LANES)] = tops[n]
        feats[pl.ds(8, 8), pl.ds(n * LANES, LANES)] = bottoms[n]

    tile_body(
        tile_ids, tile_len, targets, pictures, slot_grads,
        feats, planes, parts, upper, lower, grads, masks, left, right,
    )

    for k in ZC_ORDER:
        peer, device_id = zc_peer(my_y, my_zc, k)
        zc_sends[k] = remote(
            slot_grads.at[peer], landed_back.at[k], send_zc2.at[k - 1], recv_zc2.at[k - 1], device_id
        )
    landed_back[0] = slot_grads[my_zc]
    view_forward(1)
    view_forward(2)
    blocks = [[jnp.zeros((FEATS, LANES), F32)] * 2 for _ in range(Y_DEVS)]
    for k in ZC_ARRIVAL:
        if k:
            zc_sends[k].wait()
        rows = landed_back[k]
        half, place = divmod(k, 8)
        for j in range(Y_DEVS):
            turn = 16 * ((place - j) % 8)
            blocks[j][half] = jnp.where(group == place, pltpu.roll(rows, turn, 1) if turn else rows, blocks[j][half])
    for j in range(Y_DEVS):
        for half in range(2):
            staged_back[2 * j + half] = blocks[j][half]
    view_sends = {}
    for k in Y_ORDER:
        peer, device_id = y_peer(my_y, my_zc, k)
        y_sends[k] = remote(
            staged_back.at[pl.ds(2 * (Y_DEVS - k), 2)], returned.at[pl.ds(2 * my_y, 2)],
            send_y2.at[k - 1], recv_y2.at[k - 1], device_id,
        )
    returned[pl.ds(2 * my_y, 2)] = staged_back[pl.ds(0, 2)]

    def add_left(k, p, block):
        for half in range(2):
            n = 2 * p + half
            values = jnp.concatenate(
                [block(half, 0, 8), jnp.broadcast_to(block(half, 8, 1), (8, LANES))], axis=0
            )
            spread(values, 8, view_masks, (k * 16 + n) * 128, view_left.at[k], n * LANES)

    def scatter(k, columns, first):
        product = dot_nt(view_left[k, :, columns], view_right[k, :, columns])
        for half in range(2):
            lanes = slice(half * LANES, (half + 1) * LANES)
            rows = pl.ds((2 * k + half) * 128, 128)
            value = product[0:128, lanes] + product[128:256, lanes]
            view_grads[rows, :] = value if first else view_grads[rows, :] + value

    for p, step in enumerate(Y_ARRIVAL):
        if step:
            y_sends[step].wait()
        y = lax.rem(my_y + Y_DEVS - step, Y_DEVS)
        for k in VIEW_ORDER:
            view_sends[k, p] = remote(
                returned.at[pl.ds(2 * y, 2)], every.at[k, pl.ds(2 * p, 2)],
                send_view.at[k - 1, p], recv_view.at[k - 1, p], view_peer(view, k),
            )
        add_left(0, p, lambda half, row, size, y=y: returned[2 * y + half, pl.ds(row, size), :])
        if p == 0:
            view_forward(3)
    scatter(0, pl.ds(0, G_DEV), True)
    for half in range(2):
        matrix = [shape_rows[half * SHAPE_ROWS + i] for i in range(9)]
        sums, colours = pull_view(loader(half), slot_rows(view_grads, 0, half), matrix, saved, half * KEPT)
        for i, value in enumerate(sums):
            totals[half * SUMS + i] = value
        for i, value in enumerate(colours):
            colour[half * 3 + i] = value
    for p in range(8):
        for k in (1, 3, 2):
            view_sends[k, p].wait()
            add_left(k, p, lambda half, row, size: every[k, 2 * p + half, pl.ds(row, size), :])
        if p == 6:
            for k in (1, 3, 2):
                scatter(k, pl.ds(0, LAST), True)
    for k in (1, 3, 2):
        scatter(k, pl.ds(LAST, 256), False)


SUMS = 13


def slot_rows(view_grads, view, half):
    return lambda f: view_grads[pl.ds((2 * view + half) * 128 + f, 8, stride=16), :]


def finish_kernel(
    pictures, view_grads, dense, saved, shape_rows, totals, colour_mine,
    pictures_hbm, gradient_hbm,
    gradient, packed, colour, sums, sems,
):
    groups = [(first, min(8, ROWS - first)) for first in range(0, ROWS, 8)]
    copies = [
        pltpu.make_async_copy(gradient.at[pl.ds(*group)], gradient_hbm.at[pl.ds(*group)], sems.at[i])
        for i, group in enumerate(groups)
    ]
    copies.append(pltpu.make_async_copy(pictures, pictures_hbm, sems.at[8]))
    copies[8].start()

    def put(row, half, value):
        packed[pl.ds((row // 8) * 128 + half * 8 + row % 8, 8, stride=16), :] = value

    def send(i):
        first, size = groups[i]
        for chunk in range(16):
            gradient[pl.ds(first, size), pl.ds(chunk * LANES, LANES)] = packed[
                pl.ds(first * 16 + chunk * 8, size), :
            ]
        copies[i].start()

    def put_harmonic(row, half):
        channel, j = divmod(row - 11, 16)
        parts = [colour[(2 * k + half) * 3 + channel] for k in range(VIEW_DEVS)]
        if j:
            parts = [saved[(2 * k + half) * KEPT + 21 + j] * parts[k] for k in range(VIEW_DEVS)]
        total = parts[0] + parts[1] + parts[2] + parts[3]
        put(row, half, total if j else sh_first * total)

    for half in range(2):
        load = lambda row: dense[2 * row + half]
        matrix = [shape_rows[half * SHAPE_ROWS + i] for i in range(9)]
        total = [totals[half * SUMS + i] for i in range(SUMS)]
        for i in range(3):
            colour[half * 3 + i] = colour_mine[half * 3 + i]
        for k in range(1, VIEW_DEVS):
            place = 2 * k + half
            values, colours = pull_view(load, slot_rows(view_grads, k, half), matrix, saved, place * KEPT)
            total = [old + value for old, value in zip(total, values)]
            for i, value in enumerate(colours):
                colour[place * 3 + i] = value
        for i, value in enumerate(total):
            sums[half * SUMS + i] = value
    for i in range(2, 8):
        first, size = groups[i]
        for row in range(first, first + size):
            for half in range(2):
                put_harmonic(row, half)
        send(i)
    for half in range(2):
        total = [sums[half * SUMS + i] for i in range(SUMS)]
        shape = [shape_rows[half * SHAPE_ROWS + i] for i in range(SHAPE_ROWS)]
        matrix, scales, unit_q, inv_norm = shape[0:9], shape[9:12], shape[12:16], shape[16]
        for i in range(3):
            put(i, half, total[i])
            put(3 + i, half, total[3 + i] * matrix[i] + total[6 + i] * matrix[3 + i] + total[9 + i] * matrix[6 + i])
        _, pull_back = jax.vjp(rotation_of, *unit_q)
        g_unit = pull_back([total[3 + 3 * i + j] * scales[j] for i in range(3) for j in range(3)])
        along = unit_q[0] * g_unit[0] + unit_q[1] * g_unit[1] + unit_q[2] * g_unit[2] + unit_q[3] * g_unit[3]
        for i in range(4):
            put(6 + i, half, inv_norm * (g_unit[i] - unit_q[i] * along))
        put(10, half, total[12] * (1.0 / (1.0 + jnp.exp(dense[20 + half]))))
        for row in range(11, 16):
            put_harmonic(row, half)
    send(0)
    send(1)
    for copy in copies:
        copy.wait()


def finish_call(operands):
    vmem = pl.BlockSpec(memory_space=pltpu.VMEM)
    anywhere = pl.BlockSpec(memory_space=pl.ANY)
    tile = (8, LANES)
    return pl.pallas_call(
        finish_kernel,
        out_shape=(
            jax.ShapeDtypeStruct(operands[0].shape, F32),
            jax.ShapeDtypeStruct((ROWS, G_DEV), F32),
        ),
        in_specs=[vmem] * len(operands),
        out_specs=(anywhere, anywhere),
        scratch_shapes=[
            pltpu.VMEM((ROWS, G_DEV), F32),
            pltpu.VMEM((64 * 16, LANES), F32),
            pltpu.VMEM((VIEW_DEVS * 2 * 3,) + tile, F32),
            pltpu.VMEM((2 * SUMS,) + tile, F32),
            pltpu.SemaphoreType.DMA((9,)),
        ],
        compiler_params=pltpu.CompilerParams(vmem_limit_bytes=8 * 2**20),
        name="finish",
    )(*operands)


def render_call(camera, tile_ids, tile_len, params, slots, lists, targets):
    anywhere = pl.BlockSpec(memory_space=pl.ANY)
    blocks = pltpu.VMEM((16, FEATS, LANES), F32)
    tile = (8, LANES)
    y_sems = [pltpu.SemaphoreType.DMA((Y_DEVS - 1,))] * 2
    zc_sems = [pltpu.SemaphoreType.DMA((ZC_DEVS - 1,))] * 2
    view_sems = [pltpu.SemaphoreType.DMA((VIEW_DEVS - 1,))] * 2
    return pl.pallas_call(
        render_kernel,
        out_shape=(
            pltpu.VMEM(targets.shape, F32),
            pltpu.VMEM((VIEW_DEVS * 256, LANES), F32),
            pltpu.VMEM((2 * ROWS,) + tile, F32),
            pltpu.VMEM((VIEW_DEVS * 2 * KEPT,) + tile, F32),
            pltpu.VMEM((2 * SHAPE_ROWS,) + tile, F32),
            pltpu.VMEM((2 * SUMS,) + tile, F32),
            pltpu.VMEM((2 * 3,) + tile, F32),
        ),
        in_specs=[anywhere] * 7,
        out_specs=(pl.BlockSpec(memory_space=pltpu.VMEM),) * 7,
        scratch_shapes=[
            pltpu.VMEM(camera.shape, F32),
            pltpu.VMEM(tile_ids.shape, jnp.int32),
            pltpu.VMEM(tile_len.shape, jnp.int32),
            pltpu.VMEM((ROWS, G_DEV), F32),
            pltpu.VMEM((64 * 16, LANES), F32),
            pltpu.VMEM(lists.shape, jnp.int32),
            pltpu.VMEM(targets.shape, F32),
            pltpu.VMEM((VIEW_DEVS, 16, LANES), jnp.int32),
            pltpu.VMEM((2 * VIEW_DEVS, 8, LANES), jnp.int32),
            pltpu.VMEM((VIEW_DEVS,) + tile, F32),
            pltpu.VMEM((256, LANES), F32),
        ]
        + [blocks] * 8
        + [
            pltpu.VMEM((VIEW_DEVS, 16, FEATS, LANES), F32),
            pltpu.VMEM((16, TILES_DEV * ENTRIES), F32),
            pltpu.VMEM((4 * TILES_DEV, PIXELS, ENTRIES), F32),
            pltpu.VMEM((TILES_DEV, PIXELS, 2 * ENTRIES), BF16),
            pltpu.VMEM((1024, 256), BF16),
            pltpu.VMEM((1024, 256), BF16),
            pltpu.VMEM((16, TILES_DEV * ENTRIES), F32),
            pltpu.VMEM((8 * 256, LANES), BF16),
            pltpu.VMEM((512, TILES_DEV * ENTRIES), BF16),
            pltpu.VMEM((LANES, TILES_DEV * ENTRIES), BF16),
            pltpu.VMEM((VIEW_DEVS * 16 * 128, LANES), BF16),
            pltpu.VMEM((VIEW_DEVS, 256, G_DEV), BF16),
            pltpu.VMEM((VIEW_DEVS, 256, G_DEV), BF16),
            pltpu.SemaphoreType.DMA((14,)),
        ]
        + y_sems + zc_sems + zc_sems + y_sems + view_sems + view_sems
        + [pltpu.SemaphoreType.DMA((VIEW_DEVS - 1, 8))] * 2,
        compiler_params=pltpu.CompilerParams(
            collective_id=0, has_side_effects=True, vmem_limit_bytes=40 * 2**20
        ),
        name="render",
    )(
        *[
            pltpu.with_memory_space_constraint(operand, pltpu.HBM)
            for operand in (camera, tile_ids, tile_len, params, slots, lists, targets)
        ]
    )


def local(params, cameras, targets, tile_ids, send_slots, tile_lists, tile_len):
    partial = render_call(
        cameras, tile_ids, tile_len, params, send_slots.reshape(16, LANES), tile_lists,
        jnp.transpose(targets, (0, 2, 1, 3)),
    )
    pictures, gradient = finish_call(partial)
    return jnp.transpose(pictures, (0, 2, 1, 3)), gradient


def solution(mesh):
    return jax.shard_map(
        local,
        mesh=mesh,
        in_specs=(
            P(None, "cell"),
            P("view", None),
            P("view", "cell", None, None),
            P("view", "cell"),
            P("view", "cell", None),
            P("view", "cell", None),
            P("view", "cell"),
        ),
        out_specs=(P("view", "cell", None, None), P(None, "cell")),
        check_vma=False,
    )
```

```python
import jax
import jax.numpy as jnp
from jax import lax
from jax.experimental import pallas as pl
from jax.experimental.pallas import tpu as pltpu
from jax.sharding import PartitionSpec as P

TILE_SIDE = 16
TILE_COLS = 32
LANES = 128
Y_DEVS = 8
ZC_DEVS = 16
VIEW_DEVS = 4
FEATS = 9
Y_ORDER = (4, 3, 5, 2, 6, 1, 7)
ZC_ORDER = (8, 9, 7, 6, 10, 5, 11, 4, 12, 3, 13, 2, 14, 1, 15)
VIEW_ORDER = (2, 1, 3)
ENTRIES = 512
CHUNKS = ENTRIES // LANES
HALF = ENTRIES // 2
TILES_DEV = 2
PIXELS = 256
ROWS = 59
G_DEV = 2048
LOG2_E = 1.4426950408889634
F32 = jnp.float32
BF16 = jnp.bfloat16

focal_length = 800.0
dilation = 0.3
sh_first = 0.28209479177387814
sh_second = 0.4886025119029199
sh_third = (
    1.0925484305920792,
    -1.0925484305920792,
    0.31539156525252005,
    -1.0925484305920792,
    0.5462742152960396,
)
sh_fourth = (
    -0.5900435899266435,
    2.890611442640554,
    -0.4570457994644658,
    0.3731763325901154,
    -0.4570457994644658,
    1.445305721320277,
    -0.5900435899266435,
)


def split2(value):
    high = value.astype(BF16)
    return high, (value - high.astype(F32)).astype(BF16)


def dot_nt(lhs, rhs):
    return lax.dot_general(lhs, rhs, (((1,), (1,)), ((), ())), preferred_element_type=F32)


def dot_nn(lhs, rhs):
    return lax.dot_general(lhs, rhs, (((1,), (0,)), ((), ())), preferred_element_type=F32)


def rotation_of(q_w, q_x, q_y, q_z):
    return [
        1.0 - 2.0 * (q_y * q_y + q_z * q_z),
        2.0 * (q_x * q_y - q_w * q_z),
        2.0 * (q_x * q_z + q_w * q_y),
        2.0 * (q_x * q_y + q_w * q_z),
        1.0 - 2.0 * (q_x * q_x + q_z * q_z),
        2.0 * (q_y * q_z - q_w * q_x),
        2.0 * (q_x * q_z - q_w * q_y),
        2.0 * (q_y * q_z + q_w * q_x),
        1.0 - 2.0 * (q_x * q_x + q_y * q_y),
    ]


def unit_quaternion(quaternion):
    total = sum(part * part for part in quaternion[1:]) + quaternion[0] * quaternion[0]
    inverse = lax.rsqrt(total)
    return [part * inverse for part in quaternion], inverse


def shape_matrix(log_scales, quaternion):
    scales = [jnp.exp(part) for part in log_scales]
    unit, inverse = unit_quaternion(quaternion)
    rotation = rotation_of(*unit)
    matrix = [rotation[3 * i + j] * scales[j] for i in range(3) for j in range(3)]
    return matrix, scales, unit, inverse


def harmonics(x, y, z):
    xx, yy, zz = x * x, y * y, z * z
    rim = 4.0 * zz - xx - yy
    gap = xx - yy
    return [
        -sh_second * y,
        sh_second * z,
        -sh_second * x,
        sh_third[0] * (x * y),
        sh_third[1] * (y * z),
        sh_third[2] * (2.0 * zz - xx - yy),
        sh_third[3] * (x * z),
        sh_third[4] * gap,
        sh_fourth[0] * (y * (3.0 * xx - yy)),
        sh_fourth[1] * (x * y * z),
        sh_fourth[2] * (y * rim),
        sh_fourth[3] * (z * (2.0 * zz - 3.0 * xx - 3.0 * yy)),
        sh_fourth[4] * (x * rim),
        sh_fourth[5] * (z * gap),
        sh_fourth[6] * (x * (xx - 3.0 * yy)),
    ]


def geometry(pos, matrix):
    x, y, z = pos
    inv_z = 1.0 / z
    jac = focal_length * inv_z
    screen_x = x * jac
    screen_y = y * jac
    jac_x = -screen_x * inv_z
    jac_y = -screen_y * inv_z
    row_u = [jac * matrix[j] + jac_x * matrix[6 + j] for j in range(3)]
    row_v = [jac * matrix[3 + j] + jac_y * matrix[6 + j] for j in range(3)]
    cov_a = row_u[0] * row_u[0] + row_u[1] * row_u[1] + row_u[2] * row_u[2] + dilation
    cov_c = row_v[0] * row_v[0] + row_v[1] * row_v[1] + row_v[2] * row_v[2] + dilation
    cov_b = row_u[0] * row_v[0] + row_u[1] * row_v[1] + row_u[2] * row_v[2]
    inv_det = 1.0 / (cov_a * cov_c - cov_b * cov_b)
    return inv_z, jac, screen_x, screen_y, jac_x, jac_y, row_u, row_v, cov_a, cov_b, cov_c, inv_det


def direction(pos):
    x, y, z = pos
    inverse = lax.rsqrt(x * x + y * y + z * z)
    return [x * inverse, y * inverse, z * inverse], inverse


def raw_colour(load, channel, basis):
    total = load(11 + 16 * channel) * sh_first
    for j in range(15):
        total = total + load(12 + 16 * channel + j) * basis[j]
    return total + 0.5


KEPT = 40
SHAPE_ROWS = 17


def keep_geometry(load, shift, matrix, saved, base):
    pos = [load(i) - shift[i] for i in range(3)]
    inv_z, jac, screen_x, screen_y, jac_x, jac_y, row_u, row_v, cov_a, cov_b, cov_c, inv_det = geometry(pos, matrix)
    unit, inv_len = direction(pos)
    values = [pos[0], pos[1], inv_z, jac, screen_x, screen_y, jac_x, jac_y]
    values += row_u + row_v + [cov_a, cov_b, cov_c, inv_det] + unit + [inv_len] + harmonics(*unit)
    for i, value in enumerate(values):
        saved[base + i] = value
    opacity = 1.0 / (1.0 + jnp.exp(-load(10)))
    return [screen_x, screen_y, cov_c * inv_det, -cov_b * inv_det, cov_a * inv_det, opacity]


def keep_colours(load, saved, base):
    basis = [saved[base + 22 + j] for j in range(15)]
    raw = [raw_colour(load, channel, basis) for channel in range(3)]
    for channel, value in enumerate(raw):
        saved[base + 37 + channel] = jnp.where(value > 0.0, 1.0, jnp.where(value < 0.0, 0.0, 0.5))
    return [jnp.maximum(value, 0.0) for value in raw]


def pull_view(load, slot, matrix, saved, base):
    kept = lambda i: saved[base + i]
    inv_z, jac, screen_x, screen_y, jac_x, jac_y = [kept(2 + i) for i in range(6)]
    row_u, row_v = [kept(8 + i) for i in range(3)], [kept(11 + i) for i in range(3)]
    cov_a, cov_b, cov_c, inv_det = [kept(14 + i) for i in range(4)]
    g_a, g_b, g_c = slot(2), slot(3), slot(4)
    g_det = -(g_a * cov_c - g_b * cov_b + g_c * cov_a) * inv_det * inv_det
    d_a = 2.0 * (g_c * inv_det + g_det * cov_c)
    d_c = 2.0 * (g_a * inv_det + g_det * cov_a)
    d_b = -g_b * inv_det - 2.0 * g_det * cov_b
    g_u = [d_a * row_u[j] + d_b * row_v[j] for j in range(3)]
    g_v = [d_c * row_v[j] + d_b * row_u[j] for j in range(3)]
    g_matrix = [jac * g_u[j] for j in range(3)] + [jac * g_v[j] for j in range(3)]
    g_matrix += [jac_x * g_u[j] + jac_y * g_v[j] for j in range(3)]
    g_jac = g_u[0] * matrix[0] + g_v[0] * matrix[3]
    for j in (1, 2):
        g_jac = g_jac + (g_u[j] * matrix[j] + g_v[j] * matrix[3 + j])
    g_jac_x = g_u[0] * matrix[6] + g_u[1] * matrix[7] + g_u[2] * matrix[8]
    g_jac_y = g_v[0] * matrix[6] + g_v[1] * matrix[7] + g_v[2] * matrix[8]
    g_sx = slot(0) - inv_z * g_jac_x
    g_sy = slot(1) - inv_z * g_jac_y
    g_inv = focal_length * (g_jac + kept(0) * g_sx + kept(1) * g_sy) - screen_x * g_jac_x - screen_y * g_jac_y
    g_pos = [jac * g_sx, jac * g_sy, -inv_z * inv_z * g_inv]

    g_colours = [slot(6 + channel) * kept(37 + channel) for channel in range(3)]
    g_basis = []
    for j in range(15):
        terms = [load(12 + 16 * channel + j) * g_colours[channel] for channel in range(3)]
        g_basis.append(terms[0] + terms[1] + terms[2])
    unit, inv_len = [kept(18 + i) for i in range(3)], kept(21)
    _, pull = jax.vjp(harmonics, *unit)
    g_unit = pull(g_basis)
    along = unit[0] * g_unit[0] + unit[1] * g_unit[1] + unit[2] * g_unit[2]
    for i in range(3):
        g_pos[i] = g_pos[i] + inv_len * (g_unit[i] - unit[i] * along)
    return g_pos + g_matrix + [slot(5)], g_colours


def lane_gather(source, index):
    return jnp.take_along_axis(source, index, axis=1, mode="promise_in_bounds")


def gather_chunk(table, index):
    shape = (8, LANES)
    low = jnp.broadcast_to(index & 127, shape)
    high = jnp.broadcast_to(index >> 7, shape)
    top = bottom = jnp.zeros(shape, F32)
    for chunk in range(16):
        here = high == chunk
        top = jnp.where(here, lane_gather(table[pl.ds(16 * chunk, 8), :], low), top)
        bottom = jnp.where(here, lane_gather(table[pl.ds(16 * chunk + 8, 8), :], low), bottom)
    return top, bottom


def block_transpose(rows):
    group = lax.broadcasted_iota(jnp.int32, rows[0].shape, 1) // 16
    for step in (1, 2, 4):
        odd = (group & step) != 0
        fresh = list(rows)
        for i in range(8):
            if i & step:
                continue
            first, second = rows[i], rows[i + step]
            fresh[i] = jnp.where(odd, pltpu.roll(second, 16 * step, 1), first)
            fresh[i + step] = jnp.where(odd, second, pltpu.roll(first, LANES - 16 * step, 1))
        rows = fresh
    return rows


def remote(src_ref, dst_ref, send_sem, recv_sem, device_id):
    copy = pltpu.make_async_remote_copy(
        src_ref=src_ref,
        dst_ref=dst_ref,
        send_sem=send_sem,
        recv_sem=recv_sem,
        device_id=device_id,
        device_id_type=pl.DeviceIdType.MESH,
    )
    copy.start()
    return copy


def y_peer(my_y, my_zc, k):
    peer = lax.rem(my_y + k, Y_DEVS)
    return peer, {"cell": peer * ZC_DEVS + my_zc}


def zc_peer(my_y, my_zc, k):
    peer = lax.rem(my_zc + k, ZC_DEVS)
    return peer, {"cell": my_y * ZC_DEVS + peer}


def view_peer(view, k):
    return {"view": lax.rem(view + k, VIEW_DEVS)}


def greet(my_y, my_zc, view):
    barrier = pltpu.get_barrier_semaphore()
    peers = [y_peer(my_y, my_zc, k)[1] for k in Y_ORDER]
    peers += [zc_peer(my_y, my_zc, k)[1] for k in ZC_ORDER]
    peers += [view_peer(view, k) for k in VIEW_ORDER]
    for peer in peers:
        pl.semaphore_signal(barrier, inc=1, device_id=peer, device_id_type=pl.DeviceIdType.MESH)
    return barrier, len(peers)


def regroup(load, store):
    for half in range(2):
        for j, rows in enumerate(block_transpose([load(i, half) for i in range(8)])):
            store(j, half, rows)


def part_lanes(chunk):
    base = (chunk // 2) * 512 + (chunk % 2) * LANES
    return pl.ds(base, LANES), pl.ds(base + 256, LANES)


def fill_triangles(upper, lower):
    row = lax.broadcasted_iota(jnp.int32, (256, 256), 0)
    col = lax.broadcasted_iota(jnp.int32, (256, 256), 1)
    above = jnp.where(row < col, 1.0, 0.0).astype(BF16)
    below = jnp.where(row > col, 1.0, 0.0).astype(BF16)
    ones = jnp.ones((256, 256), BF16)
    for i in range(4):
        upper[pl.ds(256 * i, 256), :] = ones if i < 2 else above
        lower[pl.ds(256 * i, 256), :] = below if i < 2 else ones


def entry_slot(lists, my_y, tile, chunk):
    index = lists[0, pl.ds(tile, 1), pl.ds(chunk * LANES, LANES)]
    steps = (my_y - (index >> 8)) & (Y_DEVS - 1)
    return (index >> 4) & 15, (steps << 4) | (index & 15)


def hot_rows(index, count):
    shape = (count, LANES)
    return jnp.where(
        jnp.broadcast_to(index, shape) == lax.broadcasted_iota(jnp.int32, shape, 0), 1.0, 0.0
    ).astype(BF16)


def fill_masks(high, count, masks, base):
    high = jnp.broadcast_to(high, (16, LANES))
    for value in range(count):
        masks[pl.ds(base + 16 * value, 16), :] = jnp.where(high == value, 1.0, 0.0).astype(BF16)


def spread(values, count, masks, base, left, column):
    for i, piece in enumerate(split2(values)):
        for value in range(count):
            left[pl.ds((i * count + value) * 16, 16), pl.ds(column, LANES)] = (
                masks[pl.ds(base + 16 * value, 16), :] * piece
            )


class Tile:
    def __init__(self, tile, number, length, feats, grads, alpha, ratio, plane, weight, part):
        self.tile, self.length, self.feats, self.grads = tile, length, feats, grads
        self.alpha, self.ratio, self.plane, self.weight, self.part = alpha, ratio, plane, weight, part
        self.whole = pl.ds(tile * ENTRIES, ENTRIES)
        left_x = twice((TILE_SIDE * (number & (TILE_COLS - 1))).astype(F32) + 0.5)
        self.top_y = (TILE_SIDE * (number >> 5)).astype(F32) + 0.5
        self.pixel_x = lax.broadcasted_iota(jnp.int32, (TILE_SIDE, LANES), 0).astype(F32) + left_x

    def row_of(self, f, chunk):
        return self.feats[pl.ds(f, 1), pl.ds(self.tile * ENTRIES + chunk * LANES, LANES)]

    def feature(self, f, chunk):
        return jnp.broadcast_to(self.row_of(f, chunk), (8, LANES))

    def each_row(self, body, carry):
        def one_row(y, carry):
            rows = pl.ds(pl.multiple_of(y * TILE_SIDE, TILE_SIDE), TILE_SIDE)
            return body(y.astype(F32), rows, carry)

        return lax.fori_loop(0, TILE_SIDE, one_row, carry, unroll=TILE_SIDE)

    def opacities(self):
        for chunk in range(CHUNKS):
            lanes = pl.ds(chunk * LANES, LANES)
            high, low = part_lanes(chunk)
            lane = lax.broadcasted_iota(jnp.int32, (8, LANES), 1) + chunk * LANES
            log_opacity = jnp.where(lane < self.length, jnp.log2(self.feature(5, chunk)), -1e30)
            delta_x = twice(self.feature(0, chunk)) - self.pixel_x
            part_x = twice((-0.5 * LOG2_E) * self.feature(2, chunk)) * delta_x * delta_x + twice(log_opacity)
            cross = twice(-LOG2_E * self.feature(3, chunk)) * delta_x
            screen_y = self.feature(1, chunk) - self.top_y
            conic_c = (-0.5 * LOG2_E) * self.feature(4, chunk)

            def body(y, rows, carry):
                delta_y = screen_y - y
                part_y = conic_c * delta_y * delta_y
                value = jnp.exp2(part_x + cross * twice(delta_y) + twice(part_y))
                keep = jnp.log2(1.0 - value)
                self.alpha[rows, lanes] = value
                self.ratio[rows, lanes] = value * jnp.exp2(-keep)
                self.part[rows, high], self.part[rows, low] = split2(keep)
                return carry

            self.each_row(body, 0)

    def log_transmittance(self, upper):
        self.plane[:, pl.ds(0, HALF)] = dot_nn(self.part[:, pl.ds(0, 512)], upper[pl.ds(512, 512), :])
        self.plane[:, pl.ds(HALF, HALF)] = dot_nn(self.part[...], upper[...])

    def weights(self):
        for chunk in range(CHUNKS):
            lanes = pl.ds(chunk * LANES, LANES)
            high, low = part_lanes(chunk)

            def body(y, rows, carry):
                value = jnp.exp2(self.plane[rows, lanes]) * self.alpha[rows, lanes]
                self.weight[rows, lanes] = value
                self.part[rows, high], self.part[rows, low] = split2(value)
                return carry

            self.each_row(body, 0)

    def picture(self, targets, pictures):
        colours = jnp.concatenate([self.feats[pl.ds(6, 3), self.whole], jnp.zeros((5, ENTRIES), F32)], axis=0)
        colour_hi = colours.astype(BF16).astype(F32)
        colour_lo = (colours - colour_hi).astype(BF16).astype(F32)
        both = jnp.concatenate([colour_hi, colour_lo], axis=0)
        both = jnp.concatenate([both[:, :HALF], both[:, :HALF], both[:, HALF:], both[:, HALF:]], axis=1)
        product = dot_nt(both.astype(BF16), self.part[...])
        picture = product[0:8] + product[8:16]
        pictures[0, :, self.tile, :] = picture[0:3]
        residual = picture - jnp.concatenate([targets[0, :, self.tile, :], jnp.zeros((5, PIXELS), F32)], axis=0)
        residual_hi = residual.astype(BF16).astype(F32)
        residual_lo = (residual - residual_hi).astype(BF16).astype(F32)
        pair = jnp.concatenate([residual_hi, residual_lo], axis=0).astype(BF16)
        product = dot_nn(pair, self.part[...])
        product = product[0:8] + product[8:16]
        self.grads[pl.ds(6, 3), self.whole] = jnp.concatenate(
            [product[0:3, 0:256] + product[0:3, 256:512], product[0:3, 512:768] + product[0:3, 768:1024]], axis=1
        )
        stack = jnp.concatenate([residual_hi, residual_lo, residual_hi, jnp.zeros((104, PIXELS), F32)], axis=0)
        rows24 = jnp.concatenate([colour_hi, colour_hi, colour_lo, jnp.zeros((104, ENTRIES), F32)], axis=0)
        self.plane[...] = dot_nn(jnp.transpose(stack).astype(BF16), rows24.astype(BF16))

    def shares(self):
        for chunk in range(CHUNKS):
            lanes = pl.ds(chunk * LANES, LANES)
            high, low = part_lanes(chunk)

            def body(y, rows, carry):
                value = self.plane[rows, lanes] * self.weight[rows, lanes]
                self.weight[rows, lanes] = value
                self.part[rows, high], self.part[rows, low] = split2(value)
                return carry

            self.each_row(body, 0)

    def later_shares(self, lower):
        self.plane[:, pl.ds(0, HALF)] = dot_nn(self.part[...], lower[...])
        self.plane[:, pl.ds(HALF, HALF)] = dot_nn(self.part[:, pl.ds(512, 512)], lower[pl.ds(0, 512), :])

    def sums(self):
        for chunk in range(CHUNKS):
            lanes = pl.ds(chunk * LANES, LANES)
            screen_y = self.feature(1, chunk) - self.top_y

            def body(y, rows, carry):
                sum_0, sum_1, sum_2 = carry
                delta_y = twice(screen_y - y)
                grad = self.weight[rows, lanes] - self.plane[rows, lanes] * self.ratio[rows, lanes]
                slope = grad * delta_y
                return sum_0 + grad, sum_1 + slope, sum_2 + slope * delta_y

            zero = jnp.zeros((TILE_SIDE, LANES), F32)
            sum_0, sum_1, sum_2 = self.each_row(body, (zero, zero, zero))
            delta_x = twice(self.feature(0, chunk)) - self.pixel_x
            over = lambda rows: jnp.sum(rows, axis=0, keepdims=True)
            first_x = over(delta_x * sum_0)
            first_y = over(sum_1)
            out = pl.ds(self.tile * ENTRIES + chunk * LANES, LANES)
            grads, row_of = self.grads, lambda f: self.row_of(f, chunk)
            grads[pl.ds(0, 1), out] = -row_of(2) * first_x - row_of(3) * first_y
            grads[pl.ds(1, 1), out] = -row_of(4) * first_y - row_of(3) * first_x
            grads[pl.ds(2, 1), out] = -0.5 * over(delta_x * delta_x * sum_0)
            grads[pl.ds(3, 1), out] = -over(delta_x * sum_1)
            grads[pl.ds(4, 1), out] = -0.5 * over(sum_2)
            grads[pl.ds(5, 1), out] = over(sum_0)


def wide(row, i):
    return jnp.broadcast_to(row[:, pl.ds(i, 1)], (8, LANES))


def twice(rows):
    return jnp.concatenate([rows, rows], axis=0)


def tile_body(
    tile_ids, tile_len, targets, pictures, slot_grads, feats, planes, parts, upper, lower, grads, masks, left, right
):
    first, second = [
        Tile(
            tile, wide(tile_ids, tile), wide(tile_len, tile), feats, grads,
            *[planes.at[4 * tile + i] for i in range(4)], parts.at[tile],
        )
        for tile in range(TILES_DEV)
    ]
    first.opacities()
    second.opacities()
    for tile in (first, second):
        tile.log_transmittance(upper)
        tile.weights()
    for tile in (first, second):
        tile.picture(targets, pictures)
        tile.shares()
    for tile in (first, second):
        tile.later_shares(lower)
        tile.sums()
    for n in range(TILES_DEV * CHUNKS):
        spread(grads[:, pl.ds(n * LANES, LANES)], 16, masks, n * 256, left, n * LANES)
    total = dot_nt(left[...], right[...])
    for zc in range(16):
        slot_grads[zc] = total[16 * zc : 16 * zc + FEATS] + total[256 + 16 * zc : 256 + 16 * zc + FEATS]


Y_ARRIVAL = (0, 1, 7, 2, 6, 3, 5, 4)
ZC_ARRIVAL = (0, 1, 15, 2, 14, 3, 13, 4, 12, 5, 11, 6, 10, 7, 9, 8)
LAST = 7 * 256


def render_kernel(
    camera_hbm, ids_hbm, len_hbm, params_hbm, slots_hbm, lists_hbm, targets_hbm,
    pictures, view_grads, dense, saved, shape_rows, totals, colour,
    camera, tile_ids, tile_len, params, packed, lists, targets, slots, cams,
    table, outgoing, landed, staged, received, slot_grads, landed_back, staged_back, returned, every,
    feats, planes, parts, upper, lower, grads, masks, left, right, view_masks, view_left, view_right,
    load_sem, send_y, recv_y, send_zc, recv_zc, send_zc2, recv_zc2, send_y2, recv_y2,
    send_slots, recv_slots, send_cams, recv_cams, send_view, recv_view,
):
    cell, view = lax.axis_index("cell"), lax.axis_index("view")
    my_y, my_zc = cell // ZC_DEVS, lax.rem(cell, ZC_DEVS)
    barrier, greetings = greet(my_y, my_zc, view)

    pieces = [(first, min(8, ROWS - first)) for first in range(0, ROWS, 8)]
    loads = [
        pltpu.make_async_copy(params_hbm.at[pl.ds(*piece)], params.at[pl.ds(*piece)], load_sem.at[i])
        for i, piece in enumerate(pieces)
    ]
    side_loads = [
        pltpu.make_async_copy(source, target, load_sem.at[8 + i])
        for i, (source, target) in enumerate(
            (
                (camera_hbm, camera),
                (slots_hbm, slots.at[0]),
                (lists_hbm, lists),
                (targets_hbm, targets),
                (ids_hbm, tile_ids),
                (len_hbm, tile_len),
            )
        )
    ]
    for load in loads[:2] + side_loads[:2] + loads[2:] + side_loads[2:]:
        load.start()
    table[...] = jnp.zeros_like(table)
    feats[...] = jnp.zeros_like(feats)
    grads[...] = jnp.zeros_like(grads)

    def unpack(group, size):
        for chunk in range(16):
            packed[pl.ds(group * 16 + chunk * 8, size), :] = params[pl.ds(group, size), pl.ds(chunk * LANES, LANES)]
        for row in range(group, group + size):
            for half in range(2):
                dense[2 * row + half] = packed[pl.ds((row // 8) * 128 + half * 8 + row % 8, 8, stride=16), :]

    def loader(half):
        return lambda row: dense[2 * row + half]

    def load_pieces(first, last):
        for load, piece in list(zip(loads, pieces))[first:last]:
            load.wait()
            unpack(*piece)

    def put_features(first, features, half):
        for f, feature in enumerate(features):
            table[pl.ds(half * 16 + first + f, 8, stride=32), :] = feature

    side_loads[0].wait()
    shift = [wide(camera, i) for i in range(3)]
    shift_row = lax.broadcasted_iota(jnp.int32, (8, LANES), 0)
    cams[0] = jnp.where(shift_row == 0, shift[0], jnp.where(shift_row == 1, shift[1], shift[2]))
    load_pieces(0, 2)
    for half in range(2):
        load = loader(half)
        matrix, scales, unit_q, inv_norm = shape_matrix([load(3 + i) for i in range(3)], [load(6 + i) for i in range(4)])
        for i, value in enumerate(matrix + scales + unit_q + [inv_norm]):
            shape_rows[half * SHAPE_ROWS + i] = value
        put_features(0, keep_geometry(load, shift, matrix, saved, half * KEPT), half)
    load_pieces(2, 8)
    for half in range(2):
        put_features(6, keep_colours(loader(half), saved, half * KEPT), half)

    side_loads[1].wait()
    for k in Y_ORDER + (0,):
        peer, _ = y_peer(my_y, my_zc, k)
        for half in range(2):
            chunk = 2 * peer + half
            top, bottom = gather_chunk(table, slots[0, pl.ds(chunk, 1), :])
            outgoing[chunk, pl.ds(0, 8), :] = top
            outgoing[chunk, pl.ds(8, 1), :] = bottom[0:1]
    pl.semaphore_wait(barrier, greetings)
    y_sends = {}
    for k in Y_ORDER:
        peer, device_id = y_peer(my_y, my_zc, k)
        y_sends[k] = remote(
            outgoing.at[pl.ds(2 * peer, 2)], landed.at[pl.ds(2 * k, 2)],
            send_y.at[k - 1], recv_y.at[k - 1], device_id,
        )
    landed[pl.ds(0, 2)] = outgoing[pl.ds(2 * my_y, 2)]
    side_sends = []
    for k in VIEW_ORDER:
        peer = view_peer(view, k)
        side_sends.append(remote(slots.at[0], slots.at[k], send_slots.at[k - 1], recv_slots.at[k - 1], peer))
        side_sends.append(remote(cams.at[0], cams.at[k], send_cams.at[k - 1], recv_cams.at[k - 1], peer))

    fill_triangles(upper, lower)
    for load in side_loads[2:]:
        load.wait()
    for tile in range(TILES_DEV):
        for chunk in range(ENTRIES // LANES):
            n = tile * (ENTRIES // LANES) + chunk
            high, low = entry_slot(lists, my_y, tile, chunk)
            fill_masks(high, 16, masks, n * 256)
            right[:, pl.ds(n * LANES, LANES)] = hot_rows(low, LANES)

    def view_factors(k):
        for p, step in enumerate(Y_ARRIVAL):
            for half in range(2):
                n = 2 * p + half
                index = slots[k, pl.ds(2 * lax.rem(my_y + Y_DEVS - step, Y_DEVS) + half, 1), :]
                fill_masks(index >> 8, 8, view_masks, (k * 16 + n) * 128)
                view_right[k, :, pl.ds(n * LANES, LANES)] = hot_rows(index & 255, 256)

    blocks = [jnp.zeros((FEATS, LANES), F32)] * ZC_DEVS
    group = lax.broadcasted_iota(jnp.int32, (FEATS, LANES), 1) // 16
    for k in Y_ARRIVAL:
        if k:
            y_sends[k].wait()
        for zc in range(ZC_DEVS):
            rows = landed[2 * k + zc // 8]
            turn = 16 * ((k - zc) % 8)
            blocks[zc] = jnp.where(group == k, pltpu.roll(rows, turn, 1) if turn else rows, blocks[zc])
    for zc in range(ZC_DEVS):
        staged[zc] = blocks[zc]
    zc_sends = {}
    for k in ZC_ORDER:
        peer, device_id = zc_peer(my_y, my_zc, k)
        zc_sends[k] = remote(
            staged.at[peer], received.at[my_zc], send_zc.at[k - 1], recv_zc.at[k - 1], device_id
        )
    received[my_zc] = staged[my_zc]

    view_factors(0)
    for copy in side_sends:
        copy.wait()

    def view_forward(k):
        for half in range(2):
            shift = [jnp.broadcast_to(cams[k, pl.ds(i, 1), :], (8, LANES)) for i in range(3)]
            matrix = [shape_rows[half * SHAPE_ROWS + i] for i in range(9)]
            keep_geometry(loader(half), shift, matrix, saved, (2 * k + half) * KEPT)
            keep_colours(loader(half), saved, (2 * k + half) * KEPT)
        view_factors(k)

    places = [entry_slot(lists, my_y, n // 4, n % 4) for n in range(8)]
    places = [(jnp.broadcast_to(high, (8, LANES)), jnp.broadcast_to(low, (8, LANES))) for high, low in places]
    tops = [jnp.zeros((8, LANES), F32)] * 8
    bottoms = [jnp.zeros((8, LANES), F32)] * 8
    for k in ZC_ARRIVAL:
        if k:
            zc_sends[k].wait()
        source = lax.rem(my_zc + ZC_DEVS - k, ZC_DEVS)
        top = received[source, pl.ds(0, 8), :]
        bottom = jnp.broadcast_to(received[source, pl.ds(8, 1), :], (8, LANES))
        for n, (high, low) in enumerate(places):
            here = high == source
            tops[n] = jnp.where(here, lane_gather(top, low), tops[n])
            bottoms[n] = jnp.where(here, lane_gather(bottom, low), bottoms[n])
    for n in range(8):
        feats[pl.ds(0, 8), pl.ds(n * LANES, LANES)] = tops[n]
        feats[pl.ds(8, 8), pl.ds(n * LANES, LANES)] = bottoms[n]

    tile_body(
        tile_ids, tile_len, targets, pictures, slot_grads,
        feats, planes, parts, upper, lower, grads, masks, left, right,
    )

    for k in ZC_ORDER:
        peer, device_id = zc_peer(my_y, my_zc, k)
        zc_sends[k] = remote(
            slot_grads.at[peer], landed_back.at[my_zc], send_zc2.at[k - 1], recv_zc2.at[k - 1], device_id
        )
    landed_back[my_zc] = slot_grads[my_zc]
    view_forward(1)
    view_forward(2)
    for k in ZC_ORDER[::-1]:
        zc_sends[k].wait()

    def to_y(j, half, rows):
        staged_back[2 * j + half] = rows

    regroup(lambda i, half: landed_back[8 * half + i], to_y)
    view_sends = {}
    for k in Y_ORDER:
        peer, device_id = y_peer(my_y, my_zc, k)
        y_sends[k] = remote(
            staged_back.at[pl.ds(2 * (Y_DEVS - k), 2)], returned.at[pl.ds(2 * my_y, 2)],
            send_y2.at[k - 1], recv_y2.at[k - 1], device_id,
        )
    returned[pl.ds(2 * my_y, 2)] = staged_back[pl.ds(0, 2)]

    def add_left(k, p, block):
        for half in range(2):
            n = 2 * p + half
            values = jnp.concatenate(
                [block(half, 0, 8), jnp.broadcast_to(block(half, 8, 1), (8, LANES))], axis=0
            )
            spread(values, 8, view_masks, (k * 16 + n) * 128, view_left.at[k], n * LANES)

    def scatter(k, columns, first):
        product = dot_nt(view_left[k, :, columns], view_right[k, :, columns])
        for half in range(2):
            lanes = slice(half * LANES, (half + 1) * LANES)
            rows = pl.ds((2 * k + half) * 128, 128)
            value = product[0:128, lanes] + product[128:256, lanes]
            view_grads[rows, :] = value if first else view_grads[rows, :] + value

    for p, step in enumerate(Y_ARRIVAL):
        if step:
            y_sends[step].wait()
        y = lax.rem(my_y + Y_DEVS - step, Y_DEVS)
        for k in VIEW_ORDER:
            view_sends[k, p] = remote(
                returned.at[pl.ds(2 * y, 2)], every.at[k, pl.ds(2 * p, 2)],
                send_view.at[k - 1, p], recv_view.at[k - 1, p], view_peer(view, k),
            )
        add_left(0, p, lambda half, row, size, y=y: returned[2 * y + half, pl.ds(row, size), :])
        if p == 0:
            view_forward(3)
    scatter(0, pl.ds(0, G_DEV), True)
    for half in range(2):
        matrix = [shape_rows[half * SHAPE_ROWS + i] for i in range(9)]
        sums, colours = pull_view(loader(half), slot_rows(view_grads, 0, half), matrix, saved, half * KEPT)
        for i, value in enumerate(sums):
            totals[half * SUMS + i] = value
        for i, value in enumerate(colours):
            colour[half * 3 + i] = value
    for p in range(8):
        for k in (1, 3, 2):
            view_sends[k, p].wait()
            add_left(k, p, lambda half, row, size: every[k, 2 * p + half, pl.ds(row, size), :])
        if p == 6:
            for k in (1, 3, 2):
                scatter(k, pl.ds(0, LAST), True)
    for k in (1, 3, 2):
        scatter(k, pl.ds(LAST, 256), False)


SUMS = 13


def slot_rows(view_grads, view, half):
    return lambda f: view_grads[pl.ds((2 * view + half) * 128 + f, 8, stride=16), :]


def finish_kernel(
    pictures, view_grads, dense, saved, shape_rows, totals, colour_mine,
    pictures_hbm, gradient_hbm,
    gradient, packed, colour, sums, sems,
):
    groups = [(first, min(8, ROWS - first)) for first in range(0, ROWS, 8)]
    copies = [
        pltpu.make_async_copy(gradient.at[pl.ds(*group)], gradient_hbm.at[pl.ds(*group)], sems.at[i])
        for i, group in enumerate(groups)
    ]
    copies.append(pltpu.make_async_copy(pictures, pictures_hbm, sems.at[8]))
    copies[8].start()

    def put(row, half, value):
        packed[pl.ds((row // 8) * 128 + half * 8 + row % 8, 8, stride=16), :] = value

    def send(i):
        first, size = groups[i]
        for chunk in range(16):
            gradient[pl.ds(first, size), pl.ds(chunk * LANES, LANES)] = packed[
                pl.ds(first * 16 + chunk * 8, size), :
            ]
        copies[i].start()

    def put_harmonic(row, half):
        channel, j = divmod(row - 11, 16)
        parts = [colour[(2 * k + half) * 3 + channel] for k in range(VIEW_DEVS)]
        if j:
            parts = [saved[(2 * k + half) * KEPT + 21 + j] * parts[k] for k in range(VIEW_DEVS)]
        total = parts[0] + parts[1] + parts[2] + parts[3]
        put(row, half, total if j else sh_first * total)

    for half in range(2):
        load = lambda row: dense[2 * row + half]
        matrix = [shape_rows[half * SHAPE_ROWS + i] for i in range(9)]
        total = [totals[half * SUMS + i] for i in range(SUMS)]
        for i in range(3):
            colour[half * 3 + i] = colour_mine[half * 3 + i]
        for k in range(1, VIEW_DEVS):
            place = 2 * k + half
            values, colours = pull_view(load, slot_rows(view_grads, k, half), matrix, saved, place * KEPT)
            total = [old + value for old, value in zip(total, values)]
            for i, value in enumerate(colours):
                colour[place * 3 + i] = value
        for i, value in enumerate(total):
            sums[half * SUMS + i] = value
    for i in range(2, 8):
        first, size = groups[i]
        for row in range(first, first + size):
            for half in range(2):
                put_harmonic(row, half)
        send(i)
    for half in range(2):
        total = [sums[half * SUMS + i] for i in range(SUMS)]
        shape = [shape_rows[half * SHAPE_ROWS + i] for i in range(SHAPE_ROWS)]
        matrix, scales, unit_q, inv_norm = shape[0:9], shape[9:12], shape[12:16], shape[16]
        for i in range(3):
            put(i, half, total[i])
            put(3 + i, half, total[3 + i] * matrix[i] + total[6 + i] * matrix[3 + i] + total[9 + i] * matrix[6 + i])
        _, pull_back = jax.vjp(rotation_of, *unit_q)
        g_unit = pull_back([total[3 + 3 * i + j] * scales[j] for i in range(3) for j in range(3)])
        along = unit_q[0] * g_unit[0] + unit_q[1] * g_unit[1] + unit_q[2] * g_unit[2] + unit_q[3] * g_unit[3]
        for i in range(4):
            put(6 + i, half, inv_norm * (g_unit[i] - unit_q[i] * along))
        put(10, half, total[12] * (1.0 / (1.0 + jnp.exp(dense[20 + half]))))
        for row in range(11, 16):
            put_harmonic(row, half)
    send(0)
    send(1)
    for copy in copies:
        copy.wait()


def finish_call(operands):
    vmem = pl.BlockSpec(memory_space=pltpu.VMEM)
    anywhere = pl.BlockSpec(memory_space=pl.ANY)
    tile = (8, LANES)
    return pl.pallas_call(
        finish_kernel,
        out_shape=(
            jax.ShapeDtypeStruct(operands[0].shape, F32),
            jax.ShapeDtypeStruct((ROWS, G_DEV), F32),
        ),
        in_specs=[vmem] * len(operands),
        out_specs=(anywhere, anywhere),
        scratch_shapes=[
            pltpu.VMEM((ROWS, G_DEV), F32),
            pltpu.VMEM((64 * 16, LANES), F32),
            pltpu.VMEM((VIEW_DEVS * 2 * 3,) + tile, F32),
            pltpu.VMEM((2 * SUMS,) + tile, F32),
            pltpu.SemaphoreType.DMA((9,)),
        ],
        compiler_params=pltpu.CompilerParams(vmem_limit_bytes=8 * 2**20),
        name="finish",
    )(*operands)


def render_call(camera, tile_ids, tile_len, params, slots, lists, targets):
    anywhere = pl.BlockSpec(memory_space=pl.ANY)
    blocks = pltpu.VMEM((16, FEATS, LANES), F32)
    tile = (8, LANES)
    y_sems = [pltpu.SemaphoreType.DMA((Y_DEVS - 1,))] * 2
    zc_sems = [pltpu.SemaphoreType.DMA((ZC_DEVS - 1,))] * 2
    view_sems = [pltpu.SemaphoreType.DMA((VIEW_DEVS - 1,))] * 2
    return pl.pallas_call(
        render_kernel,
        out_shape=(
            pltpu.VMEM(targets.shape, F32),
            pltpu.VMEM((VIEW_DEVS * 256, LANES), F32),
            pltpu.VMEM((2 * ROWS,) + tile, F32),
            pltpu.VMEM((VIEW_DEVS * 2 * KEPT,) + tile, F32),
            pltpu.VMEM((2 * SHAPE_ROWS,) + tile, F32),
            pltpu.VMEM((2 * SUMS,) + tile, F32),
            pltpu.VMEM((2 * 3,) + tile, F32),
        ),
        in_specs=[anywhere] * 7,
        out_specs=(pl.BlockSpec(memory_space=pltpu.VMEM),) * 7,
        scratch_shapes=[
            pltpu.VMEM(camera.shape, F32),
            pltpu.VMEM(tile_ids.shape, jnp.int32),
            pltpu.VMEM(tile_len.shape, jnp.int32),
            pltpu.VMEM((ROWS, G_DEV), F32),
            pltpu.VMEM((64 * 16, LANES), F32),
            pltpu.VMEM(lists.shape, jnp.int32),
            pltpu.VMEM(targets.shape, F32),
            pltpu.VMEM((VIEW_DEVS, 16, LANES), jnp.int32),
            pltpu.VMEM((VIEW_DEVS,) + tile, F32),
            pltpu.VMEM((256, LANES), F32),
        ]
        + [blocks] * 8
        + [
            pltpu.VMEM((VIEW_DEVS, 16, FEATS, LANES), F32),
            pltpu.VMEM((16, TILES_DEV * ENTRIES), F32),
            pltpu.VMEM((4 * TILES_DEV, PIXELS, ENTRIES), F32),
            pltpu.VMEM((TILES_DEV, PIXELS, 2 * ENTRIES), BF16),
            pltpu.VMEM((1024, 256), BF16),
            pltpu.VMEM((1024, 256), BF16),
            pltpu.VMEM((16, TILES_DEV * ENTRIES), F32),
            pltpu.VMEM((8 * 256, LANES), BF16),
            pltpu.VMEM((512, TILES_DEV * ENTRIES), BF16),
            pltpu.VMEM((LANES, TILES_DEV * ENTRIES), BF16),
            pltpu.VMEM((VIEW_DEVS * 16 * 128, LANES), BF16),
            pltpu.VMEM((VIEW_DEVS, 256, G_DEV), BF16),
            pltpu.VMEM((VIEW_DEVS, 256, G_DEV), BF16),
            pltpu.SemaphoreType.DMA((14,)),
        ]
        + y_sems + zc_sems + zc_sems + y_sems + view_sems + view_sems
        + [pltpu.SemaphoreType.DMA((VIEW_DEVS - 1, 8))] * 2,
        compiler_params=pltpu.CompilerParams(
            collective_id=0, has_side_effects=True, vmem_limit_bytes=40 * 2**20
        ),
        name="render",
    )(
        *[
            pltpu.with_memory_space_constraint(operand, pltpu.HBM)
            for operand in (camera, tile_ids, tile_len, params, slots, lists, targets)
        ]
    )


def local(params, cameras, targets, tile_ids, send_slots, tile_lists, tile_len):
    partial = render_call(
        cameras, tile_ids, tile_len, params, send_slots.reshape(16, LANES), tile_lists,
        jnp.transpose(targets, (0, 2, 1, 3)),
    )
    pictures, gradient = finish_call(partial)
    return jnp.transpose(pictures, (0, 2, 1, 3)), gradient


def solution(mesh):
    return jax.shard_map(
        local,
        mesh=mesh,
        in_specs=(
            P(None, "cell"),
            P("view", None),
            P("view", "cell", None, None),
            P("view", "cell"),
            P("view", "cell", None),
            P("view", "cell", None),
            P("view", "cell"),
        ),
        out_specs=(P("view", "cell", None, None), P(None, "cell")),
        check_vma=False,
    )
```
